128 devices in a mesh: batch: 32 (over z, x, core), tile: 4 (over y).
Axes of the slice: x: 4, y: 4, z: 4, core: 2. Of those that a mesh axis runs over, the one named last changes fastest.
Arguments:
- slot_state_vectors: bfloat16 [128, 256, 768], P(('batch', 'tile')), may hold values from -6 to 6
- sequence_token_counts: int32 [128], P(('batch', 'tile')), may hold values from 8 to 256, as said below
- positive_companion: int32 [128], replicated, may hold values from 0 to 127, as said below
- leading_dimension_counts: int32 [4], replicated, may hold values from 64 to 768, as said below
- affinity_divisor: float32 [1], replicated, may hold values from 0.02 to 0.08
- triple_projection_matrix: bfloat16 [2, 768, 2304], replicated, may hold values from -0.21875 to 0.21875
- probe_payload_shift: bfloat16 [2, 1536], replicated, may hold values from -1.5 to 1.5
- mixer_projection_matrix: bfloat16 [2, 768, 768], replicated, may hold values from -0.875 to 0.875
- mixer_projection_shift: bfloat16 [2, 768], replicated, may hold values from -1.5 to 1.5
- mixer_scale_factor: bfloat16 [2, 768], replicated, may hold values from 0.5 to 1.5
- mixer_shift_term: bfloat16 [2, 768], replicated, may hold values from -1.5 to 1.5
- expand_layer_matrix: bfloat16 [2, 768, 3072], replicated, may hold values from -0.21875 to 0.21875
- expand_layer_shift: bfloat16 [2, 3072], replicated, may hold values from -1.5 to 1.5
- shrink_layer_matrix: bfloat16 [2, 3072, 768], replicated, may hold values from -0.109375 to 0.109375
- shrink_layer_shift: bfloat16 [2, 768], replicated, may hold values from -1.5 to 1.5
- closing_scale_factor: bfloat16 [2, 768], replicated, may hold values from 0.5 to 1.5
- closing_shift_term: bfloat16 [2, 768], replicated, may hold values from -1.5 to 1.5
Outputs:
- loss: float32 [128], P('batch')
- embeddings: float32 [128, 2, 768], P(('batch', 'tile'))
- input_grad: float32 [128, 256, 768], P(('batch', 'tile'))
- query_key_value_gradient: float32 [2, 768, 2304], P(None, ('batch', 'tile'))
- grad_qvbias: float32 [2, 1536], P(None, ('batch', 'tile'))
- grad_outproj: float32 [2, 768, 768], P(None, ('batch', 'tile'))
- grad_outbias: float32 [2, 768], P(None, ('batch', 'tile'))
- grad_attgain: float32 [2, 768], P(None, ('batch', 'tile'))
- grad_attshift: float32 [2, 768], P(None, ('batch', 'tile'))
- feedforward_input_gradient: float32 [2, 768, 3072], P(None, ('batch', 'tile'))
- grad_ffnbias: float32 [2, 3072], P(None, ('batch', 'tile'))
- grad_downproj: float32 [2, 3072, 768], P(None, ('batch', 'tile'))
- grad_downbias: float32 [2, 768], P(None, ('batch', 'tile'))
- grad_fingain: float32 [2, 768], P(None, ('batch', 'tile'))
- grad_finshift: float32 [2, 768], P(None, ('batch', 'tile'))
The draws below stay inside these ranges and needn't reach their ends.
Inputs may be any that keep to these rules, and one draw needn't show every extreme that they name: The first sequence_token_counts[i] slots of sequence i are real, the rest padding; some sequence has 256 and some has 8. positive_companion[positive_companion[i]] == i and positive_companion[i] != i. `leading_dimension_counts`: strictly increasing multiples of 32, none under 64, the last equal to 768.
All inputs are finite; a program needn't handle non-finite values.
Results may differ from the reference program's by a relative error of at most 0.012.
Values sent between devices are 32-bit elements; how exact they have to be, the bound alone decides.
A program may use at most 320 MiB of HBM per device.

```python
import math
import jax
import jax.numpy as jnp
from jax import lax

D = 768
HEADS = 12
FF = 3072
LAYERS = 2
SEQ_LEN = 256
NPREF = 4
NSEQ = 128
N_BATCH = 32


def draw_sequence_token_counts(key, part):
    key = jax.random.fold_in(key, 11)
    first, second, third = jax.random.split(key, 3)
    level = jax.random.randint(first, (NSEQ,), 0, 6)
    top = jnp.minimum(jnp.left_shift(jnp.int32(8), level), SEQ_LEN)
    half = top // 2
    sizes = half + jax.random.randint(second, (NSEQ,), 0, half + 1)
    sizes = jnp.clip(sizes, 8, SEQ_LEN)
    longest = jax.random.randint(third, (), 0, NSEQ)
    sizes = sizes.at[longest].set(SEQ_LEN)
    sizes = sizes.at[(longest + 1) % NSEQ].set(8)
    return sizes.astype(jnp.int32)


def draw_positive_companion(key, part):
    key = jax.random.fold_in(key, 12)
    order = jax.random.permutation(key, NSEQ).astype(jnp.int32)
    evens = order[0::2]
    odds = order[1::2]
    paired = jnp.zeros((NSEQ,), jnp.int32)
    paired = paired.at[evens].set(odds)
    paired = paired.at[odds].set(evens)
    return paired


def draw_leading_dimension_counts(key, part):
    key = jax.random.fold_in(key, 13)
    units = D // 32
    picks = jax.random.permutation(key, units - 2)[:NPREF - 1] + 2
    picks = jnp.sort(picks.astype(jnp.int32))
    whole = jnp.concatenate([picks, jnp.array([units], jnp.int32)])
    return (whole * 32).astype(jnp.int32)


def shard_levels(own_key, dims, shards, low, high):
    loudness, own = 1.0, jax.random.fold_in(own_key, 6)
    for axis_at, parts in shards:
        heights = jnp.exp(jax.random.uniform(jax.random.fold_in(own, axis_at), (parts,), jnp.float32, low / len(shards), high / len(shards)))
        loudness = loudness * jnp.repeat(heights, dims[axis_at] // parts).reshape([-1 if axis == axis_at else 1 for axis in range(len(dims))])
    return loudness


def normal_values(rng, shape, scale, bound, pieces=(), held_as=jnp.bfloat16):
    entries = scale * jax.random.normal(rng, shape, jnp.float32)
    if pieces:
        entries = entries * shard_levels(rng, shape, pieces, -0.22, 0.18)
    return jnp.clip(entries, -bound, bound).astype(held_as)


def setup_inputs(seed: int = 0) -> dict:
    key_of = jax.random.split(jax.random.key(seed), 18)
    slot_state_vectors = normal_values(key_of[0], (NSEQ, SEQ_LEN, D), 1.0, 6.0, ((0, 128),))
    sequence_token_counts = draw_sequence_token_counts(jax.random.fold_in(key_of[17], 71), 0)
    positive_companion = draw_positive_companion(jax.random.fold_in(key_of[17], 71), 0)
    leading_dimension_counts = draw_leading_dimension_counts(jax.random.fold_in(key_of[17], 71), 0)
    affinity_divisor = jnp.clip(jnp.exp(jax.random.uniform(key_of[4], (1,), jnp.float32, math.log(0.02), math.log(0.08))), 0.02, 0.08)
    triple_projection_matrix = normal_values(key_of[5], (LAYERS, D, 3 * D), D ** -0.5, 0.21875)
    probe_payload_shift = normal_values(key_of[6], (LAYERS, 2 * D), 0.3, 1.5)
    mixer_projection_matrix = normal_values(key_of[7], (LAYERS, D, D), (D // 16) ** -0.5, 0.875)
    mixer_projection_shift = normal_values(key_of[8], (LAYERS, D), 0.3, 1.5)
    mixer_scale_factor = jnp.clip(1.0 + 0.1 * jax.random.normal(key_of[9], (LAYERS, D), jnp.float32), 0.5, 1.5).astype(jnp.bfloat16)
    mixer_shift_term = normal_values(key_of[10], (LAYERS, D), 0.3, 1.5)
    expand_layer_matrix = normal_values(key_of[11], (LAYERS, D, FF), D ** -0.5, 0.21875)
    expand_layer_shift = normal_values(key_of[12], (LAYERS, FF), 0.3, 1.5)
    shrink_layer_matrix = normal_values(key_of[13], (LAYERS, FF, D), FF ** -0.5, 0.109375)
    shrink_layer_shift = normal_values(key_of[14], (LAYERS, D), 0.3, 1.5)
    closing_scale_factor = jnp.clip(1.0 + 0.1 * jax.random.normal(key_of[15], (LAYERS, D), jnp.float32), 0.5, 1.5).astype(jnp.bfloat16)
    closing_shift_term = normal_values(key_of[16], (LAYERS, D), 0.3, 1.5)
    return dict(slot_state_vectors=slot_state_vectors, sequence_token_counts=sequence_token_counts, positive_companion=positive_companion, leading_dimension_counts=leading_dimension_counts, affinity_divisor=affinity_divisor, triple_projection_matrix=triple_projection_matrix, probe_payload_shift=probe_payload_shift, mixer_projection_matrix=mixer_projection_matrix, mixer_projection_shift=mixer_projection_shift, mixer_scale_factor=mixer_scale_factor, mixer_shift_term=mixer_shift_term, expand_layer_matrix=expand_layer_matrix, expand_layer_shift=expand_layer_shift, shrink_layer_matrix=shrink_layer_matrix, shrink_layer_shift=shrink_layer_shift, closing_scale_factor=closing_scale_factor, closing_shift_term=closing_shift_term)


@jax.custom_vjp
def low(v):
    return lax.optimization_barrier(v.astype(jnp.bfloat16)).astype(jnp.float32)

@jax.custom_vjp
def low_back(v):
    return v

def low_keep(v):
    return (low(v), None)

def low_pass(kept, grad):
    return (grad,)

def back_keep(v):
    return (v, None)

def back_low(kept, grad):
    return (low(grad),)
low.defvjp(low_keep, low_pass)
low_back.defvjp(back_keep, back_low)
eps_norm = 1e-06
exact_arithmetic_mode = lax.Precision.HIGHEST

def project(left_operand, right_operand):
    return jnp.einsum('gwk,km->gwm', left_operand, right_operand, precision=exact_arithmetic_mode)

def layer_norm(total_loss, gain, shift):
    center = total_loss - lax.optimization_barrier(jnp.mean(total_loss, axis=-1, keepdims=True))
    spread = lax.optimization_barrier(jnp.mean(center * center, axis=-1, keepdims=True))
    return center * lax.rsqrt(spread + eps_norm) * gain + shift

def encoder_layer(hidden, params, keymask):
    triple_projection_matrix, probe_payload_shift, mixer_projection_matrix, mixer_projection_shift, mixer_scale_factor, mixer_shift_term, expand_layer_matrix, expand_layer_shift, shrink_layer_matrix, shrink_layer_shift, closing_scale_factor, closing_shift_term = params
    width = hidden.shape[-1]
    count = hidden.shape[0]
    length = hidden.shape[1]
    heads_size = width // HEADS
    bias = jnp.concatenate([probe_payload_shift[:width], jnp.zeros((width,), hidden.dtype), probe_payload_shift[width:]])
    mixed = low(low_back(project(low(hidden), triple_projection_matrix) + bias))
    query = mixed[..., :width].reshape(count, length, HEADS, heads_size)
    keys = mixed[..., width:2 * width].reshape(count, length, HEADS, heads_size)
    values = mixed[..., 2 * width:].reshape(count, length, HEADS, heads_size)
    scores = jnp.einsum('sqhd,skhd->shqk', query, keys, precision=exact_arithmetic_mode) * heads_size ** (-0.5)
    scores = low_back(scores + keymask[:, None, None, :])
    probs = jax.nn.softmax(scores, axis=-1)
    context = jnp.einsum('shqk,skhd->sqhd', low(probs), values, precision=exact_arithmetic_mode)
    context = low(low_back(context)).reshape(count, length, width)
    attended = low_back(project(context, mixer_projection_matrix) + mixer_projection_shift)
    middle = layer_norm(hidden + attended, mixer_scale_factor, mixer_shift_term)
    inner = low_back(project(low(middle), expand_layer_matrix) + expand_layer_shift)
    active = low(jax.nn.gelu(inner, approximate=False))
    outer = low_back(project(active, shrink_layer_matrix) + shrink_layer_shift)
    return layer_norm(middle + outer, closing_scale_factor, closing_shift_term)

def encode_group(slot_state_vectors, sequence_token_counts, first, second):
    places = lax.broadcasted_iota(jnp.int32, slot_state_vectors.shape[:2], 1)
    valid = (places < sequence_token_counts[:, None]).astype(jnp.float32)
    keymask = (valid - 1.0) * 1000000000.0
    front = encoder_layer(slot_state_vectors, first, keymask)
    behind = encoder_layer(front, second, keymask)
    counts = sequence_token_counts.astype(jnp.float32)[:, None]
    pooled_front = lax.optimization_barrier(jnp.sum(front * valid[:, :, None], axis=1)) / counts
    pooled_behind = lax.optimization_barrier(jnp.sum(behind * valid[:, :, None], axis=1)) / counts
    return jnp.stack([pooled_front, pooled_behind], axis=1)

def nested_pairing_cost(averaged_layer_states, positive_companion, leading_dimension_counts, logit_divisor_scalar):
    columns = lax.broadcasted_iota(jnp.int32, (NPREF, D), 1)
    keep = (columns < leading_dimension_counts[:, None]).astype(jnp.float32)
    masked = averaged_layer_states[:, :, None, :] * keep
    normalized_direction = masked * lax.rsqrt(lax.optimization_barrier(jnp.sum(masked * masked, axis=-1, keepdims=True)) + eps_norm)
    affinity_matrix = jnp.einsum('zwfq,xwfq->wfzx', normalized_direction, normalized_direction, precision=exact_arithmetic_mode) / logit_divisor_scalar
    idents = jnp.arange(NSEQ, dtype=jnp.int32)
    selfs = idents[:, None] == idents[None, :]
    latent_affinity_matrix = jnp.where(selfs, -1e+30, affinity_matrix)
    top = lax.optimization_barrier(jnp.max(latent_affinity_matrix, axis=-1))
    logsumexp_values = top + jnp.log(lax.optimization_barrier(jnp.sum(jnp.exp(latent_affinity_matrix - top[..., None]), axis=-1)))
    target = affinity_matrix[:, :, idents, positive_companion]
    return lax.optimization_barrier(jnp.sum(logsumexp_values - target, axis=(0, 1))) / (2 * NPREF)

def reference(slot_state_vectors, sequence_token_counts, positive_companion, leading_dimension_counts, affinity_divisor, triple_projection_matrix, probe_payload_shift, mixer_projection_matrix, mixer_projection_shift, mixer_scale_factor, mixer_shift_term, expand_layer_matrix, expand_layer_shift, shrink_layer_matrix, shrink_layer_shift, closing_scale_factor, closing_shift_term):
    weights = (triple_projection_matrix, probe_payload_shift, mixer_projection_matrix, mixer_projection_shift, mixer_scale_factor, mixer_shift_term, expand_layer_matrix, expand_layer_shift, shrink_layer_matrix, shrink_layer_shift, closing_scale_factor, closing_shift_term)

    def forward(inputs, *params):
        first = tuple((p[0] for p in params))
        second = tuple((p[1] for p in params))
        grouped = inputs.reshape(N_BATCH, -1, SEQ_LEN, D)
        group_len = sequence_token_counts.reshape(N_BATCH, -1)
        encode = jax.checkpoint(lambda pair: encode_group(pair[0], pair[1], first, second))
        averaged_layer_states = lax.map(encode, (grouped, group_len)).reshape(-1, 2, D)
        return (averaged_layer_states, nested_pairing_cost(averaged_layer_states, positive_companion, leading_dimension_counts, affinity_divisor[0]))
    floats = tuple((w.astype(jnp.float32) for w in weights))
    outputs, pullback = jax.vjp(forward, slot_state_vectors.astype(jnp.float32), *floats)
    averaged_layer_states = outputs[0]
    row_losses = outputs[1]
    grads = pullback((jnp.zeros_like(averaged_layer_states), jnp.ones_like(row_losses)))
    return (row_losses, averaged_layer_states, grads[0], grads[1], grads[2], grads[3], grads[4], grads[5], grads[6], grads[7], grads[8], grads[9], grads[10], grads[11], grads[12])
```

```python
from functools import partial

import jax
import jax.numpy as jnp
import ml_dtypes
import numpy as np
from jax import lax
from jax.experimental import pallas as pl
from jax.experimental.pallas import tpu as pltpu
from jax.sharding import PartitionSpec as P

HEADS = 12


eps_norm = 1e-06
exact_arithmetic_mode = lax.Precision.HIGHEST


f32, bf16 = jnp.float32, jnp.bfloat16
MESH = pl.DeviceIdType.MESH
TRIPLES = 12
SLOTS = 3
ORDERS = (("x", "y", "z"), ("y", "z", "x"), ("z", "x", "y"))


def my_place():
    b = lax.axis_index("batch")
    return {"z": b // 8, "x": lax.rem(b // 2, 4), "c": lax.rem(b, 2), "y": lax.axis_index("tile")}


def device_at(place):
    return {"batch": (place["z"] * 4 + place["x"]) * 2 + place["c"], "tile": place["y"]}


def neighbour(place, axis, step):
    there = dict(place)
    if axis == "c":
        there["c"] = 1 - place["c"]
    else:
        there[axis] = lax.rem(place[axis] + step + 4, 4)
    return device_at(there)


def reduce_kernel(
    act_t_ref, a_ref, perm_ref, bd_ref, bu_ref, bq_ref, bo_ref, out_ref,
    apt, half, send, got0, got1a, got1b, half2, got2a, got2b, half3, got3a, got3b, rows24,
    sems_s, sems_r, sem0_s, sem0_r,
):
    place = my_place()
    core = place["c"]
    barrier = pltpu.get_barrier_semaphore()
    for axis, step in (("c", 1), ("x", 1), ("x", -1), ("y", 1), ("y", -1), ("z", 1), ("z", -1)):
        pl.semaphore_signal(barrier, inc=1, device_id=neighbour(place, axis, step), device_id_type=MESH)
    pl.semaphore_wait(barrier, 7)
    half3[...] = jnp.zeros_like(half3)

    def exchange(o, k, slot, src_up, src_down, got):
        axis = ORDERS[o][k // 2]
        return [
            pltpu.make_async_remote_copy(
                src_ref=src, dst_ref=got.at[o, slot, way],
                send_sem=sems_s.at[o, k, way, slot], recv_sem=sems_r.at[o, k, way, slot],
                device_id=neighbour(place, axis, step), device_id_type=MESH,
            )
            for way, (src, step) in enumerate(((src_up, 1), (src_down, -1)))
        ]

    def spots(o, phase):
        a = place[ORDERS[o][phase]]
        return a, lax.rem(a + 1, 4), lax.rem(a + 2, 4), lax.rem(a + 3, 4)

    def copy0(o, u):
        slot = lax.rem(u, 2)
        return pltpu.make_async_remote_copy(
            src_ref=send.at[o], dst_ref=got0.at[o, slot], send_sem=sem0_s.at[o], recv_sem=sem0_r.at[o, slot],
            device_id=neighbour(place, "c", 1), device_id_type=MESH,
        )

    def step_a(o, phase, u):
        slot = lax.rem(u, SLOTS)
        a, up, far, down = spots(o, phase)
        if phase == 0:
            src, got = (half.at[o, slot, pl.ds(far * 4, 2)], half.at[o, slot, pl.ds(far * 4 + 2, 2)]), got1a
        elif phase == 1:
            src, got = (half2.at[o, slot, far, pl.ds(0, 6)], half2.at[o, slot, far, pl.ds(6, 6)]), got2a
        else:
            src, got = (half3.at[o, slot, far, pl.ds(0, 2)], half3.at[o, slot, far, pl.ds(2, 2)]), got3a
        return exchange(o, 2 * phase, slot, src[0], src[1], got)

    def step_b(o, phase, u):
        slot = lax.rem(u, SLOTS)
        a, up, far, down = spots(o, phase)
        if phase == 0:
            src, got = (half.at[o, slot, pl.ds(up * 4, 4)], half.at[o, slot, pl.ds(down * 4, 4)]), got1b
        elif phase == 1:
            src, got = (half2.at[o, slot, up], half2.at[o, slot, down]), got2b
        else:
            src, got = (half3.at[o, slot, up], half3.at[o, slot, down]), got3b
        return exchange(o, 2 * phase + 1, slot, src[0], src[1], got)

    def add_a(o, phase, u):
        slot = lax.rem(u, SLOTS)
        a, up, far, down = spots(o, phase)
        if phase == 0:
            for i in range(2):
                half[o, slot, up * 4 + i] += got1a[o, slot, 0, i]
                half[o, slot, down * 4 + 2 + i] += got1a[o, slot, 1, i]
        elif phase == 1:
            half2[o, slot, up, 0:6] += got2a[o, slot, 0]
            half2[o, slot, down, 6:12] += got2a[o, slot, 1]
        else:
            half3[o, slot, up, 0:2] += got3a[o, slot, 0]
            half3[o, slot, down, 2:4] += got3a[o, slot, 1]

    def add_b(o, phase, u):
        slot = lax.rem(u, SLOTS)
        a, up, far, down = spots(o, phase)
        if phase == 0:
            for i in range(4):
                half2[o, slot, i] = half[o, slot, a * 4 + i] + got1b[o, slot, 0, i] + got1b[o, slot, 1, i]
        elif phase == 1:
            total = half2[o, slot, a] + got2b[o, slot, 0] + got2b[o, slot, 1]

            @pl.when(lax.rem(u, 6) < 2)
            def _():
                for k in range(4):
                    half3[o, slot, k, 0:3] = total[3 * k : 3 * k + 3]

            @pl.when(lax.rem(u, 6) >= 2)
            def _():
                for ct in range(4):
                    rows24[o, ct] = total[3 * ct : 3 * ct + 3].reshape(24, 128)
                for k in range(4):
                    for ct in range(4):
                        half3[o, slot, k, ct, 0:6, :] = rows24[o, ct, 6 * k : 6 * k + 6, :]
        else:
            out_ref[u, o] = half3[o, slot, a] + got3b[o, slot, 0] + got3b[o, slot, 1]

    def store_rows(o, slot, mine, blocks, tile0, value):
        n, m = value.shape[0] // 24, value.shape[1] // 128
        for j in range(m):
            part = value[:, 128 * j : 128 * (j + 1)].reshape(n, 3, 8, 128)
            where = pl.ds(blocks, n)
            if mine:
                half[o, slot, where, tile0 + 3 * j : tile0 + 3 * j + 3] = part
            else:
                send[o, where, tile0 + 3 * j : tile0 + 3 * j + 3] = part

    def product(o, slot, which, ref, layer, at, width, tile0):
        for mine in (True, False):
            c = core if mine else 1 - core

            def rows(i, _):
                lhs = apt[o, which, pl.ds(pl.multiple_of(c * 384 + i * 96, 32), 96), :]
                for w in range(0, width, 256):
                    value = jnp.dot(lhs, ref[layer, :, at + w : at + w + 256], preferred_element_type=f32)
                    store_rows(o, slot, mine, i * 4, tile0 + 3 * (w // 128), value)
                return 0

            lax.fori_loop(0, 4, rows, 0)

    def produce(u):
        slot = lax.rem(u, SLOTS)
        layer = 1 - u // 6
        kind = lax.rem(u, 6)

        @pl.when(kind == 0)
        def _():
            for which in range(3):
                a = a_ref[layer, which]
                for o in range(3):
                    apt[o, which] = lax.dot_general(
                        perm_ref[o], a, (((1,), (1,)), ((), ())), preferred_element_type=f32
                    ).astype(bf16)

        for k in range(2):
            @pl.when(kind == k)
            def _():
                def block(zx, _):
                    z, x = zx // 4, lax.rem(zx, 4)
                    for mine in (True, False):
                        c = core if mine else 1 - core
                        lhs = act_t_ref[layer, pl.ds(pl.multiple_of(zx * 192 + c * 96, 32), 96), :]
                        value = jnp.dot(
                            lhs, bd_ref[layer, :, 384 * k : 384 * (k + 1)], preferred_element_type=f32
                        )
                        for y in range(4):
                            for j in range(3):
                                p = {"x": x, "y": y, "z": z}
                                d1, d2, d3 = (p[axis] for axis in ORDERS[j])
                                row = (y * 3 + j) * 8
                                for ct in range(3):
                                    tile = value[row : row + 8, 128 * ct : 128 * ct + 128]
                                    if mine:
                                        half[j, slot, d1 * 4 + d2, d3 * 3 + ct] = tile
                                    else:
                                        send[j, d1 * 4 + d2, d3 * 3 + ct] = tile
                    return 0

                lax.fori_loop(0, 16, block, 0)

        for k in range(2):
            @pl.when(kind == 2 + k)
            def _():
                for o in range(3):
                    product(o, slot, 2, bu_ref, layer, (k * 3 + o) * 512, 512, 0)

        @pl.when(kind == 4)
        def _():
            for o in range(3):
                product(o, slot, 0, bq_ref, layer, o * 768, 512, 0)

        @pl.when(kind == 5)
        def _():
            for o in range(3):
                product(o, slot, 0, bq_ref, layer, o * 768 + 512, 256, 0)
                product(o, slot, 1, bo_ref, layer, o * 256, 256, 6)

    def when(u, job):
        @pl.when((u >= 0) & (u < TRIPLES))
        def _():
            job(u)

    def tick(now, _):
        t = now - 3

        def enter(u):
            slot = lax.rem(u, SLOTS)
            for o in range(3):
                copy0(o, u).wait()

                def add(i, _):
                    half[o, slot, i] += got0[o, lax.rem(u, 2), i]
                    return 0

                lax.fori_loop(0, 16, add, 0)
                for copy in step_a(o, 0, u):
                    copy.start()

        when(t + 2, enter)

        def second(phase):
            def job(u):
                for o in range(3):
                    for copy in step_a(o, phase, u):
                        copy.wait()
                    add_a(o, phase, u)
                    for copy in step_b(o, phase, u):
                        copy.start()
            return job

        def third(phase):
            def job(u):
                for o in range(3):
                    for copy in step_b(o, phase, u):
                        copy.wait()
                    add_b(o, phase, u)
                    if phase < 2:
                        for copy in step_a(o, phase + 1, u):
                            copy.start()
            return job

        when(t + 1, second(0))
        when(t, third(0))
        when(t - 1, second(1))
        when(t - 2, third(1))
        when(t - 3, second(2))
        when(t - 4, third(2))

        def make(u):
            produce(u)
            for o in range(3):
                copy0(o, u).start()

        when(t + 3, make)
        return 0

    lax.fori_loop(0, TRIPLES + 7, tick, 0)


def permutations():
    rows = np.arange(768).reshape(4, 4, 2, 4, 6)
    names = {"z": 0, "x": 1, "c": 2, "y": 3}
    out = np.zeros((3, 768, 768), np.float32)
    for o, (d1, d2, d3) in enumerate(ORDERS):
        taken = rows.transpose(2, names[d1], names[d2], names[d3], 4).reshape(-1)
        out[o, np.arange(768), taken] = 1
    return out.astype(ml_dtypes.bfloat16)


def reduce_gradients(active_t, operands, d_outer, d_inner, d_qkv, d_att):
    tile = (8, 128)
    vmem = pl.BlockSpec(memory_space=pltpu.VMEM)
    out = pl.pallas_call(
        reduce_kernel,
        out_shape=jax.ShapeDtypeStruct((TRIPLES, 3, 4) + tile, f32),
        in_specs=[vmem] * 7,
        out_specs=vmem,
        scratch_shapes=[
            pltpu.VMEM((3, 3, 768, 256), bf16),
            pltpu.VMEM((3, SLOTS, 16, 12) + tile, f32),
            pltpu.VMEM((3, 16, 12) + tile, f32),
            pltpu.VMEM((3, 2, 16, 12) + tile, f32),
            pltpu.VMEM((3, SLOTS, 2, 2, 12) + tile, f32),
            pltpu.VMEM((3, SLOTS, 2, 4, 12) + tile, f32),
            pltpu.VMEM((3, SLOTS, 4, 12) + tile, f32),
            pltpu.VMEM((3, SLOTS, 2, 6) + tile, f32),
            pltpu.VMEM((3, SLOTS, 2, 12) + tile, f32),
            pltpu.VMEM((3, SLOTS, 4, 4) + tile, f32),
            pltpu.VMEM((3, SLOTS, 2, 2) + tile, f32),
            pltpu.VMEM((3, SLOTS, 2, 4) + tile, f32),
            pltpu.VMEM((3, 4, 24, 128), f32),
            pltpu.SemaphoreType.DMA((3, 6, 2, SLOTS)),
            pltpu.SemaphoreType.DMA((3, 6, 2, SLOTS)),
            pltpu.SemaphoreType.DMA((3,)),
            pltpu.SemaphoreType.DMA((3, 2)),
        ],
        compiler_params=pltpu.CompilerParams(
            collective_id=1, has_side_effects=True, vmem_limit_bytes=60 * 1024 * 1024
        ),
    )(active_t, operands, jnp.asarray(permutations()), d_outer, d_inner, d_qkv, d_att)
    out = out.reshape(2, 6, 3, 4, 8, 128)[::-1]
    down = out[:, 0:2, :, 0:3].transpose(0, 2, 4, 1, 3, 5).reshape(2, 24, 768)
    up = out[:, 2:4, :, :, 0:6].transpose(0, 4, 1, 2, 3, 5).reshape(2, 6, 3072)
    first = out[:, 4, :, :, 0:6].transpose(0, 3, 1, 2, 4)
    last = out[:, 5, :, :, 0:6].transpose(0, 3, 1, 2, 4)
    qkv = jnp.concatenate([first, last[:, :, :, 0:2]], axis=3).reshape(2, 6, 2304)
    mixer = last[:, :, :, 2:4].reshape(2, 6, 768)
    return qkv, mixer, up, down


def combined_all(part, axis, combine):
    gathered = jax.tree.map(lambda a: lax.all_gather(a, axis), part)

    def take(source):
        return jax.tree.map(lambda a: lax.dynamic_index_in_dim(a, source, 0, False), gathered)

    return lax.fori_loop(
        1, lax.axis_size(axis), lambda source, state: combine(state, take(source)), take(0)
    )


def norm_forward(total_loss, gain, shift):
    center = total_loss - jnp.mean(total_loss, axis=-1, keepdims=True)
    spread = jnp.mean(center * center, axis=-1, keepdims=True)
    scaled = lax.rsqrt(spread + eps_norm)
    normed = center * scaled
    return (normed * gain + shift, normed, scaled)


def norm_backward(grad, normed, scaled, gain):
    grad_gain = jnp.sum(grad * normed, axis=(0, 1))
    grad_shift = jnp.sum(grad, axis=(0, 1))
    dnormed = grad * gain
    inside = (
        dnormed
        - jnp.mean(dnormed, axis=-1, keepdims=True)
        - normed * jnp.mean(dnormed * normed, axis=-1, keepdims=True)
    )
    return (scaled * inside, grad_gain, grad_shift)


def layer_forward(hidden, params, keymask):
    (
        triple_projection_matrix,
        probe_payload_shift,
        mixer_projection_matrix,
        mixer_projection_shift,
        mixer_scale_factor,
        mixer_shift_term,
        expand_layer_matrix,
        expand_layer_shift,
        shrink_layer_matrix,
        shrink_layer_shift,
        closing_scale_factor,
        closing_shift_term,
    ) = params
    count, length, width = hidden.shape
    heads_size = width // HEADS
    bias = probe_payload_shift.astype(jnp.float32)
    full_bias = jnp.concatenate([bias[:width], jnp.zeros((width,), jnp.float32), bias[width:]])
    hidden_reduced = hidden.astype(jnp.bfloat16)
    mixed = (
        jnp.einsum(
            "gwk,km->gwm",
            hidden_reduced,
            triple_projection_matrix,
            preferred_element_type=jnp.float32,
        )
        + full_bias
    )
    mixed_low = mixed.astype(jnp.bfloat16)
    query = mixed_low[..., :width].reshape(count, length, HEADS, heads_size)
    keys = mixed_low[..., width : 2 * width].reshape(count, length, HEADS, heads_size)
    values = mixed_low[..., 2 * width :].reshape(count, length, HEADS, heads_size)
    scores = jnp.einsum(
        "sqhd,skhd->shqk", query, keys, preferred_element_type=jnp.float32
    ) * heads_size ** (-0.5)
    scores = scores + keymask[:, None, None, :]
    expo = jnp.exp(scores - jnp.max(scores, axis=-1, keepdims=True))
    probs = expo / jnp.sum(expo, axis=-1, keepdims=True)
    probs_low = probs.astype(jnp.bfloat16)
    context = jnp.einsum("shqk,skhd->sqhd", probs_low, values, preferred_element_type=jnp.float32)
    context_reduced = context.astype(jnp.bfloat16).reshape(count, length, width)
    attended = jnp.einsum(
        "bry,yt->brt", context_reduced, mixer_projection_matrix, preferred_element_type=jnp.float32
    ) + mixer_projection_shift.astype(jnp.float32)
    middle, normed_one, scaled_one = norm_forward(
        hidden + attended,
        mixer_scale_factor.astype(jnp.float32),
        mixer_shift_term.astype(jnp.float32),
    )
    middle_reduced = middle.astype(jnp.bfloat16)
    inner = jnp.einsum(
        "ncm,mj->ncj", middle_reduced, expand_layer_matrix, preferred_element_type=jnp.float32
    ) + expand_layer_shift.astype(jnp.float32)
    activation_reduced = jax.nn.gelu(inner, approximate=False).astype(jnp.bfloat16)
    outer = jnp.einsum(
        "pcx,xj->pcj", activation_reduced, shrink_layer_matrix, preferred_element_type=jnp.float32
    ) + shrink_layer_shift.astype(jnp.float32)
    result, normed_two, scaled_two = norm_forward(
        middle + outer,
        closing_scale_factor.astype(jnp.float32),
        closing_shift_term.astype(jnp.float32),
    )
    saved = (
        hidden_reduced,
        query,
        keys,
        values,
        probs,
        probs_low,
        context_reduced,
        normed_one,
        scaled_one,
        middle_reduced,
        inner,
        activation_reduced,
        normed_two,
        scaled_two,
    )
    return (result, saved)


def layer_backward(grad_out, saved, params):
    (
        triple_projection_matrix,
        probe_payload_shift,
        mixer_projection_matrix,
        mixer_projection_shift,
        mixer_scale_factor,
        mixer_shift_term,
        expand_layer_matrix,
        expand_layer_shift,
        shrink_layer_matrix,
        shrink_layer_shift,
        closing_scale_factor,
        closing_shift_term,
    ) = params
    (
        hidden_reduced,
        query,
        keys,
        values,
        probs,
        probs_low,
        context_reduced,
        normed_one,
        scaled_one,
        middle_reduced,
        inner,
        activation_reduced,
        normed_two,
        scaled_two,
    ) = saved
    count, length, width = grad_out.shape
    heads_size = query.shape[-1]
    dsum_two, grad_fingain, grad_finshift = norm_backward(
        grad_out, normed_two, scaled_two, closing_scale_factor.astype(jnp.float32)
    )
    outer_gradient = dsum_two.astype(jnp.bfloat16)
    grad_downbias = jnp.sum(outer_gradient.astype(jnp.float32), axis=(0, 1))
    activation_gradient = jnp.einsum(
        "cov,gv->cog", outer_gradient, shrink_layer_matrix, preferred_element_type=jnp.float32
    )
    unused, gelu_pull = jax.vjp(partial(jax.nn.gelu, approximate=False), inner)
    inner_gradient = gelu_pull(activation_gradient)[0].astype(jnp.bfloat16)
    grad_ffnbias = jnp.sum(inner_gradient.astype(jnp.float32), axis=(0, 1))
    dmiddle = dsum_two + jnp.einsum(
        "qec,pc->qep", inner_gradient, expand_layer_matrix, preferred_element_type=jnp.float32
    )
    dsum_one, grad_attgain, grad_attshift = norm_backward(
        dmiddle, normed_one, scaled_one, mixer_scale_factor.astype(jnp.float32)
    )
    attention_gradient = dsum_one.astype(jnp.bfloat16)
    grad_outbias = jnp.sum(attention_gradient.astype(jnp.float32), axis=(0, 1))
    context_gradient = jnp.einsum(
        "cqu,wu->cqw",
        attention_gradient,
        mixer_projection_matrix,
        preferred_element_type=jnp.float32,
    )
    context_gradient = context_gradient.astype(jnp.bfloat16).reshape(
        count, length, HEADS, heads_size
    )
    dprobs = jnp.einsum(
        "sqhd,skhd->shqk", context_gradient, values, preferred_element_type=jnp.float32
    )
    dvalues = jnp.einsum(
        "shqk,sqhd->skhd", probs_low, context_gradient, preferred_element_type=jnp.float32
    )
    dscores = probs * (dprobs - jnp.sum(dprobs * probs, axis=-1, keepdims=True))
    dscores = dscores.astype(jnp.bfloat16)
    factor = heads_size ** (-0.5)
    dquery = (
        jnp.einsum("shqk,skhd->sqhd", dscores, keys, preferred_element_type=jnp.float32) * factor
    )
    dkeys = (
        jnp.einsum("shqk,sqhd->skhd", dscores, query, preferred_element_type=jnp.float32) * factor
    )
    mixed_gradient = jnp.concatenate(
        [
            dquery.reshape(count, length, width),
            dkeys.reshape(count, length, width),
            dvalues.reshape(count, length, width),
        ],
        axis=-1,
    )
    mixed_gradient = mixed_gradient.astype(jnp.bfloat16)
    bias_sums = jnp.sum(mixed_gradient.astype(jnp.float32), axis=(0, 1))
    grad_qvbias = jnp.concatenate([bias_sums[:width], bias_sums[2 * width :]])
    dhidden = dsum_one + jnp.einsum(
        "inu,tu->int", mixed_gradient, triple_projection_matrix, preferred_element_type=jnp.float32
    )
    grads = (
        grad_qvbias,
        grad_outbias,
        grad_attgain,
        grad_attshift,
        grad_ffnbias,
        grad_downbias,
        grad_fingain,
        grad_finshift,
    )
    products = (
        activation_reduced[0].T,
        jnp.stack([hidden_reduced[0], context_reduced[0], middle_reduced[0]]),
        outer_gradient[0],
        inner_gradient[0],
        mixed_gradient[0],
        attention_gradient[0],
    )
    return (dhidden, grads, products)


def pairing_cost_term(
    averaged_layer_states, positive_companion, leading_dimension_counts, affinity_divisor
):
    batches = lax.axis_size("batch")
    tiles = lax.axis_size("tile")
    per_dev = averaged_layer_states.shape[0]
    width = averaged_layer_states.shape[-1]
    nested_level_count = leading_dimension_counts.shape[0]
    rows = lax.all_gather(averaged_layer_states, "tile", axis=0, tiled=True)
    cols = lax.all_gather(averaged_layer_states, "batch", axis=0, tiled=True)
    columns = lax.broadcasted_iota(jnp.int32, (nested_level_count, width), 1)
    keep = (columns < leading_dimension_counts[:, None]).astype(jnp.float32)

    def unit_of(embed):
        masked = embed[:, :, None, :] * keep
        inverse = lax.rsqrt(jnp.sum(masked * masked, axis=-1, keepdims=True) + eps_norm)
        return (masked * inverse, inverse)

    def unit_back(normalized_direction, inverse, dunit):
        inside = dunit - normalized_direction * jnp.sum(
            normalized_direction * dunit, axis=-1, keepdims=True
        )
        return jnp.sum(keep * inside * inverse, axis=2)

    row_unit, row_inv = unit_of(rows)
    col_unit, col_inv = unit_of(cols)
    logit_divisor_scalar = affinity_divisor[0]
    affinity_matrix = (
        jnp.einsum("zwfq,xwfq->wfzx", row_unit, col_unit, precision=exact_arithmetic_mode)
        / logit_divisor_scalar
    )
    batch_idx = lax.axis_index("batch")
    tile_idx = lax.axis_index("tile")
    row_ids = batch_idx * tiles * per_dev + jnp.arange(tiles * per_dev, dtype=jnp.int32)
    col_pos = jnp.arange(batches * per_dev, dtype=jnp.int32)
    col_ids = (col_pos // per_dev * tiles + tile_idx) * per_dev + col_pos % per_dev
    selfs = row_ids[:, None] == col_ids[None, :]
    latent_affinity_matrix = jnp.where(selfs, -1e30, affinity_matrix)
    top = jnp.max(latent_affinity_matrix, axis=-1)
    total_exp = jnp.sum(jnp.exp(latent_affinity_matrix - top[..., None]), axis=-1)
    targets = jnp.take(positive_companion, row_ids)
    matching_indicator = (col_ids[None, :] == targets[:, None]).astype(jnp.float32)
    target_part = jnp.sum(affinity_matrix * matching_indicator, axis=-1)

    def combine(first, second):
        upper = jnp.maximum(first[0], second[0])
        return (
            upper,
            first[1] * jnp.exp(first[0] - upper) + second[1] * jnp.exp(second[0] - upper),
            first[2] + second[2],
        )

    top, total_exp, target_sims = combined_all((top, total_exp, target_part), "tile", combine)
    logsumexp_values = top + jnp.log(total_exp)
    row_losses = jnp.sum(logsumexp_values - target_sims, axis=(0, 1)) / (2 * nested_level_count)
    affinity_grad_matrix = (
        (jnp.exp(latent_affinity_matrix - logsumexp_values[..., None]) - matching_indicator)
        / (2 * nested_level_count)
        / logit_divisor_scalar
    )
    drow_unit = jnp.einsum(
        "lpij,jlpd->ilpd", affinity_grad_matrix, col_unit, precision=exact_arithmetic_mode
    )
    dcol_unit = jnp.einsum(
        "lpij,ilpd->jlpd", affinity_grad_matrix, row_unit, precision=exact_arithmetic_mode
    )
    drows = lax.psum_scatter(
        unit_back(row_unit, row_inv, drow_unit), "tile", scatter_dimension=0, tiled=True
    )
    dcols = lax.psum_scatter(
        unit_back(col_unit, col_inv, dcol_unit), "batch", scatter_dimension=0, tiled=True
    )
    return (row_losses, drows + dcols)


def body(
    slot_state_vectors,
    sequence_token_counts,
    positive_companion,
    leading_dimension_counts,
    affinity_divisor,
    triple_projection_matrix,
    probe_payload_shift,
    mixer_projection_matrix,
    mixer_projection_shift,
    mixer_scale_factor,
    mixer_shift_term,
    expand_layer_matrix,
    expand_layer_shift,
    shrink_layer_matrix,
    shrink_layer_shift,
    closing_scale_factor,
    closing_shift_term,
):
    weights = (
        triple_projection_matrix,
        probe_payload_shift,
        mixer_projection_matrix,
        mixer_projection_shift,
        mixer_scale_factor,
        mixer_shift_term,
        expand_layer_matrix,
        expand_layer_shift,
        shrink_layer_matrix,
        shrink_layer_shift,
        closing_scale_factor,
        closing_shift_term,
    )
    first = tuple((w[0] for w in weights))
    second = tuple((w[1] for w in weights))
    places = lax.broadcasted_iota(jnp.int32, slot_state_vectors.shape[:2], 1)
    valid = (places < sequence_token_counts[:, None]).astype(jnp.float32)
    keymask = (valid - 1.0) * 1000000000.0
    counts = sequence_token_counts.astype(jnp.float32)[:, None]
    inputs = slot_state_vectors.astype(jnp.float32)
    front, saved_front = layer_forward(inputs, first, keymask)
    behind, saved_behind = layer_forward(front, second, keymask)
    averaged_layer_states = jnp.stack(
        [
            jnp.sum(front * valid[:, :, None], axis=1) / counts,
            jnp.sum(behind * valid[:, :, None], axis=1) / counts,
        ],
        axis=1,
    )
    row_losses, embedding_gradient = pairing_cost_term(
        averaged_layer_states, positive_companion, leading_dimension_counts, affinity_divisor
    )
    spread = valid[:, :, None] / counts[:, :, None]
    dfront, grads_behind, products_behind = layer_backward(
        spread * embedding_gradient[:, 1][:, None, :], saved_behind, second
    )
    dfront = dfront + spread * embedding_gradient[:, 0][:, None, :]
    dinputs, grads_front, products_front = layer_backward(dfront, saved_front, first)
    stacked = [jnp.stack([gf, gb]) for gf, gb in zip(grads_front, grads_behind)]
    qvbias, outbias, attgain, attshift, ffnbias, downbias, fingain, finshift = (
        lax.psum_scatter(s, ("batch", "tile"), scatter_dimension=1, tiled=True) for s in stacked
    )
    qkv, mixer, up, down = reduce_gradients(
        *(jnp.stack([pf, pb]) for pf, pb in zip(products_front, products_behind))
    )
    return (
        row_losses,
        averaged_layer_states,
        dinputs,
        qkv,
        qvbias,
        mixer,
        outbias,
        attgain,
        attshift,
        up,
        ffnbias,
        down,
        downbias,
        fingain,
        finshift,
    )


def solution(mesh):
    return jax.shard_map(
        body,
        mesh=mesh,
        in_specs=(
            P(("batch", "tile"), None, None),
            P(("batch", "tile")),
            P(),
            P(),
            P(),
            P(),
            P(),
            P(),
            P(),
            P(),
            P(),
            P(),
            P(),
            P(),
            P(),
            P(),
            P(),
        ),
        out_specs=(
            P("batch"),
            P(("batch", "tile"), None, None),
            P(("batch", "tile"), None, None),
            P(None, ("batch", "tile"), None),
            P(None, ("batch", "tile")),
            P(None, ("batch", "tile"), None),
            P(None, ("batch", "tile")),
            P(None, ("batch", "tile")),
            P(None, ("batch", "tile")),
            P(None, ("batch", "tile"), None),
            P(None, ("batch", "tile")),
            P(None, ("batch", "tile"), None),
            P(None, ("batch", "tile")),
            P(None, ("batch", "tile")),
            P(None, ("batch", "tile")),
        ),
        check_vma=False,
    )
```

```python
from functools import partial

import jax
import jax.numpy as jnp
import ml_dtypes
import numpy as np
from jax import lax
from jax.experimental import pallas as pl
from jax.experimental.pallas import tpu as pltpu
from jax.sharding import PartitionSpec as P

HEADS = 12


eps_norm = 1e-06


f32, bf16 = jnp.float32, jnp.bfloat16
MESH = pl.DeviceIdType.MESH
TRIPLES = 12
SLOTS = 3
ORDERS = (("x", "y", "z"), ("y", "z", "x"), ("z", "x", "y"))


def my_place():
    b = lax.axis_index("batch")
    return {"z": b // 8, "x": lax.rem(b // 2, 4), "c": lax.rem(b, 2), "y": lax.axis_index("tile")}


def device_at(place):
    return {"batch": (place["z"] * 4 + place["x"]) * 2 + place["c"], "tile": place["y"]}


def neighbour(place, axis, step):
    there = dict(place)
    if axis == "c":
        there["c"] = 1 - place["c"]
    else:
        there[axis] = lax.rem(place[axis] + step + 4, 4)
    return device_at(there)


GROUP = tuple((flip, step) for flip in (0, 1) for step in range(4) if flip or step)
VECTORS = tuple((768 * k, 768, 6) for k in range(6)) + ((4608, 1536, 12), (6144, 3072, 24))


def in_group(place, flip, step):
    there = dict(place)
    there["c"] = lax.rem(place["c"] + flip, 2)
    there["y"] = lax.rem(place["y"] + step, 4)
    return device_at(there)


def reduce_kernel(
    act_t_ref, a_ref, perm_ref, bd_ref, bu_ref, bq_ref, bo_ref, vec_ref, spread_ref, out_ref, vec_out_ref,
    apt, half, send, got0, got1a, got1b, half2, got2a, got2b, half3, got3a, got3b, rows24,
    vec_src, vec_z, vec_x, vec_mid, vec_cy,
    sems_s, sems_r, sem0_s, sem0_r, vec_s, vec_r,
):
    place = my_place()
    core = place["c"]
    barrier = pltpu.get_barrier_semaphore()
    for axis in ("x", "z"):
        for step in (1, 2, 3):
            pl.semaphore_signal(barrier, inc=1, device_id=neighbour(place, axis, step), device_id_type=MESH)
    for flip, step in GROUP:
        pl.semaphore_signal(barrier, inc=1, device_id=in_group(place, flip, step), device_id_type=MESH)
    pl.semaphore_wait(barrier, 13)
    half3[...] = jnp.zeros_like(half3)

    def exchange(o, k, slot, src_up, src_down, got):
        axis = ORDERS[o][k // 2]
        return [
            pltpu.make_async_remote_copy(
                src_ref=src, dst_ref=got.at[o, slot, way],
                send_sem=sems_s.at[o, k, way, slot], recv_sem=sems_r.at[o, k, way, slot],
                device_id=neighbour(place, axis, step), device_id_type=MESH,
            )
            for way, (src, step) in enumerate(((src_up, 1), (src_down, -1)))
        ]

    def spots(o, phase):
        a = place[ORDERS[o][phase]]
        return a, lax.rem(a + 1, 4), lax.rem(a + 2, 4), lax.rem(a + 3, 4)

    def copy0(o, u):
        slot = lax.rem(u, 2)
        return pltpu.make_async_remote_copy(
            src_ref=send.at[o], dst_ref=got0.at[o, slot], send_sem=sem0_s.at[o], recv_sem=sem0_r.at[o, slot],
            device_id=neighbour(place, "c", 1), device_id_type=MESH,
        )

    def step_a(o, phase, u):
        slot = lax.rem(u, SLOTS)
        a, up, far, down = spots(o, phase)
        if phase == 0:
            src, got = (half.at[o, slot, pl.ds(far * 4, 2)], half.at[o, slot, pl.ds(far * 4 + 2, 2)]), got1a
        elif phase == 1:
            src, got = (half2.at[o, slot, far, pl.ds(0, 6)], half2.at[o, slot, far, pl.ds(6, 6)]), got2a
        else:
            src, got = (half3.at[o, slot, far, pl.ds(0, 2)], half3.at[o, slot, far, pl.ds(2, 2)]), got3a
        return exchange(o, 2 * phase, slot, src[0], src[1], got)

    def step_b(o, phase, u):
        slot = lax.rem(u, SLOTS)
        a, up, far, down = spots(o, phase)
        if phase == 0:
            src, got = (half.at[o, slot, pl.ds(up * 4, 4)], half.at[o, slot, pl.ds(down * 4, 4)]), got1b
        elif phase == 1:
            src, got = (half2.at[o, slot, up], half2.at[o, slot, down]), got2b
        else:
            src, got = (half3.at[o, slot, up], half3.at[o, slot, down]), got3b
        return exchange(o, 2 * phase + 1, slot, src[0], src[1], got)

    def add_a(o, phase, u):
        slot = lax.rem(u, SLOTS)
        a, up, far, down = spots(o, phase)
        if phase == 0:
            for i in range(2):
                half[o, slot, up * 4 + i] += got1a[o, slot, 0, i]
                half[o, slot, down * 4 + 2 + i] += got1a[o, slot, 1, i]
        elif phase == 1:
            half2[o, slot, up, 0:6] += got2a[o, slot, 0]
            half2[o, slot, down, 6:12] += got2a[o, slot, 1]
        else:
            half3[o, slot, up, 0:2] += got3a[o, slot, 0]
            half3[o, slot, down, 2:4] += got3a[o, slot, 1]

    def add_b(o, phase, u):
        slot = lax.rem(u, SLOTS)
        a, up, far, down = spots(o, phase)
        if phase == 0:
            for i in range(4):
                half2[o, slot, i] = half[o, slot, a * 4 + i] + got1b[o, slot, 0, i] + got1b[o, slot, 1, i]
        elif phase == 1:
            total = half2[o, slot, a] + got2b[o, slot, 0] + got2b[o, slot, 1]

            @pl.when(lax.rem(u, 6) < 2)
            def _():
                for k in range(4):
                    half3[o, slot, k, 0:3] = total[3 * k : 3 * k + 3]

            @pl.when(lax.rem(u, 6) >= 2)
            def _():
                for ct in range(4):
                    rows24[o, ct] = total[3 * ct : 3 * ct + 3].reshape(24, 128)
                for k in range(4):
                    for ct in range(4):
                        half3[o, slot, k, ct, 0:6, :] = rows24[o, ct, 6 * k : 6 * k + 6, :]
        else:
            out_ref[u, o] = half3[o, slot, a] + got3b[o, slot, 0] + got3b[o, slot, 1]

    def store_rows(o, slot, mine, blocks, tile0, value):
        n, m = value.shape[0] // 24, value.shape[1] // 128
        for j in range(m):
            part = value[:, 128 * j : 128 * (j + 1)].reshape(n, 3, 8, 128)
            where = pl.ds(blocks, n)
            if mine:
                half[o, slot, where, tile0 + 3 * j : tile0 + 3 * j + 3] = part
            else:
                send[o, where, tile0 + 3 * j : tile0 + 3 * j + 3] = part

    def product(o, slot, which, ref, layer, at, width, tile0):
        for mine in (True, False):
            c = core if mine else 1 - core

            def rows(i, _):
                lhs = apt[o, which, pl.ds(pl.multiple_of(c * 384 + i * 96, 32), 96), :]
                for w in range(0, width, 256):
                    value = jnp.dot(lhs, ref[layer, :, at + w : at + w + 256], preferred_element_type=f32)
                    store_rows(o, slot, mine, i * 4, tile0 + 3 * (w // 128), value)
                return 0

            lax.fori_loop(0, 4, rows, 0)

    def produce(u):
        slot = lax.rem(u, SLOTS)
        layer = 1 - u // 6
        kind = lax.rem(u, 6)

        @pl.when(kind == 0)
        def _():
            for which in range(3):
                a = a_ref[layer, which]
                for o in range(3):
                    apt[o, which] = lax.dot_general(
                        perm_ref[o], a, (((1,), (1,)), ((), ())), preferred_element_type=f32
                    ).astype(bf16)

        for k in range(2):
            @pl.when(kind == k)
            def _():
                def block(zx, _):
                    z, x = zx // 4, lax.rem(zx, 4)
                    for mine in (True, False):
                        c = core if mine else 1 - core
                        lhs = act_t_ref[layer, pl.ds(pl.multiple_of(zx * 192 + c * 96, 32), 96), :]
                        value = jnp.dot(
                            lhs, bd_ref[layer, :, 384 * k : 384 * (k + 1)], preferred_element_type=f32
                        )
                        for y in range(4):
                            for j in range(3):
                                p = {"x": x, "y": y, "z": z}
                                d1, d2, d3 = (p[axis] for axis in ORDERS[j])
                                row = (y * 3 + j) * 8
                                for ct in range(3):
                                    tile = value[row : row + 8, 128 * ct : 128 * ct + 128]
                                    if mine:
                                        half[j, slot, d1 * 4 + d2, d3 * 3 + ct] = tile
                                    else:
                                        send[j, d1 * 4 + d2, d3 * 3 + ct] = tile
                    return 0

                lax.fori_loop(0, 16, block, 0)

        for k in range(2):
            @pl.when(kind == 2 + k)
            def _():
                for o in range(3):
                    product(o, slot, 2, bu_ref, layer, (k * 3 + o) * 512, 512, 0)

        @pl.when(kind == 4)
        def _():
            for o in range(3):
                product(o, slot, 0, bq_ref, layer, o * 768, 512, 0)

        @pl.when(kind == 5)
        def _():
            for o in range(3):
                product(o, slot, 0, bq_ref, layer, o * 768 + 512, 256, 0)
                product(o, slot, 1, bo_ref, layer, o * 256, 256, 6)

    def spread_vectors():
        for layer in range(2):
            total = jnp.zeros((128, 128), f32)
            for start, width, keep in VECTORS:
                d = lax.broadcasted_iota(jnp.int32, (128, width), 0) * keep
                q = lax.broadcasted_iota(jnp.int32, (128, width), 1)
                own = jnp.where((q >= d) & (q < d + keep), vec_ref[layer : layer + 1, start : start + width], 0.0)
                high = own.astype(bf16)
                low = (own - high.astype(f32)).astype(bf16)
                lanes = spread_ref[start : start + width, :]
                total += jnp.dot(high, lanes, preferred_element_type=f32)
                total += jnp.dot(low, lanes, preferred_element_type=f32)
            total = total.reshape(4, 4, 8, 128)
            for z in range(4):
                for x in range(4):
                    vec_src[z, x, layer] = total[z, x]

    def vector_copy(k, src, dst, device):
        return pltpu.make_async_remote_copy(
            src_ref=src, dst_ref=dst, send_sem=vec_s.at[k], recv_sem=vec_r.at[k], device_id=device, device_id_type=MESH
        )

    def copies_z():
        return [
            vector_copy(i, vec_src.at[lax.rem(place["z"] + i + 1, 4)], vec_z.at[i], neighbour(place, "z", i + 1))
            for i in range(3)
        ]

    def copies_x():
        return [
            vector_copy(3 + i, vec_src.at[place["z"], lax.rem(place["x"] + i + 1, 4)], vec_x.at[i], neighbour(place, "x", i + 1))
            for i in range(3)
        ]

    def copies_group():
        return [
            vector_copy(6 + i, vec_mid, vec_cy.at[i], in_group(place, flip, step))
            for i, (flip, step) in enumerate(GROUP)
        ]

    def vectors_start():
        spread_vectors()
        for copy in copies_z():
            copy.start()

    def vectors_second():
        for copy in copies_z():
            copy.wait()
        for x in range(4):
            vec_src[place["z"], x] += vec_z[0, x] + vec_z[1, x] + vec_z[2, x]
        for copy in copies_x():
            copy.start()

    def vectors_third():
        for copy in copies_x():
            copy.wait()
        vec_mid[...] = vec_src[place["z"], place["x"]] + vec_x[0] + vec_x[1] + vec_x[2]
        for copy in copies_group():
            copy.start()

    def vectors_last():
        for copy in copies_group():
            copy.wait()
        total = vec_mid[...]
        for i in range(7):
            total += vec_cy[i]
        mine = lax.broadcasted_iota(jnp.int32, (2, 8, 128), 1) == core * 4 + place["y"]
        vec_out_ref[...] = jnp.sum(jnp.where(mine, total, 0.0), axis=1)

    def when(u, job):
        @pl.when((u >= 0) & (u < TRIPLES))
        def _():
            job(u)

    def tick(now, _):
        t = now - 3

        def enter(u):
            slot = lax.rem(u, SLOTS)
            for o in range(3):
                copy0(o, u).wait()

                def add(i, _):
                    half[o, slot, i] += got0[o, lax.rem(u, 2), i]
                    return 0

                lax.fori_loop(0, 16, add, 0)
                for copy in step_a(o, 0, u):
                    copy.start()

        when(t + 2, enter)

        def second(phase):
            def job(u):
                for o in range(3):
                    for copy in step_a(o, phase, u):
                        copy.wait()
                    add_a(o, phase, u)
                    for copy in step_b(o, phase, u):
                        copy.start()
            return job

        def third(phase):
            def job(u):
                for o in range(3):
                    for copy in step_b(o, phase, u):
                        copy.wait()
                    add_b(o, phase, u)
                    if phase < 2:
                        for copy in step_a(o, phase + 1, u):
                            copy.start()
            return job

        when(t + 1, second(0))
        when(t, third(0))
        when(t - 1, second(1))
        when(t - 2, third(1))
        when(t - 3, second(2))
        when(t - 4, third(2))

        def make(u):
            produce(u)
            for o in range(3):
                copy0(o, u).start()

        when(t + 3, make)
        for k, job in enumerate((vectors_start, vectors_second, vectors_third, vectors_last)):
            pl.when(now == TRIPLES + k)(job)
        return 0

    lax.fori_loop(0, TRIPLES + 7, tick, 0)


def permutations():
    rows = np.arange(768).reshape(4, 4, 2, 4, 6)
    names = {"z": 0, "x": 1, "c": 2, "y": 3}
    out = np.zeros((3, 768, 768), np.float32)
    for o, (d1, d2, d3) in enumerate(ORDERS):
        taken = rows.transpose(2, names[d1], names[d2], names[d3], 4).reshape(-1)
        out[o, np.arange(768), taken] = 1
    return out.astype(ml_dtypes.bfloat16)


def lane_places():
    out = np.zeros((9216, 128), np.float32)
    lane = 0
    for start, width, keep in VECTORS:
        q = np.arange(width)
        out[start + q, lane + q % keep] = 1
        lane += keep
    return out.astype(ml_dtypes.bfloat16)


def reduce_gradients(vectors, active_t, operands, d_outer, d_inner, d_qkv, d_att):
    tile = (8, 128)
    vmem = pl.BlockSpec(memory_space=pltpu.VMEM)
    out, vec_out = pl.pallas_call(
        reduce_kernel,
        out_shape=(jax.ShapeDtypeStruct((TRIPLES, 3, 4) + tile, f32), jax.ShapeDtypeStruct((2, 128), f32)),
        in_specs=[vmem] * 9,
        out_specs=(vmem, vmem),
        scratch_shapes=[
            pltpu.VMEM((3, 3, 768, 256), bf16),
            pltpu.VMEM((3, SLOTS, 16, 12) + tile, f32),
            pltpu.VMEM((3, 16, 12) + tile, f32),
            pltpu.VMEM((3, 2, 16, 12) + tile, f32),
            pltpu.VMEM((3, SLOTS, 2, 2, 12) + tile, f32),
            pltpu.VMEM((3, SLOTS, 2, 4, 12) + tile, f32),
            pltpu.VMEM((3, SLOTS, 4, 12) + tile, f32),
            pltpu.VMEM((3, SLOTS, 2, 6) + tile, f32),
            pltpu.VMEM((3, SLOTS, 2, 12) + tile, f32),
            pltpu.VMEM((3, SLOTS, 4, 4) + tile, f32),
            pltpu.VMEM((3, SLOTS, 2, 2) + tile, f32),
            pltpu.VMEM((3, SLOTS, 2, 4) + tile, f32),
            pltpu.VMEM((3, 4, 24, 128), f32),
            pltpu.VMEM((4, 4, 2) + tile, f32),
            pltpu.VMEM((3, 4, 2) + tile, f32),
            pltpu.VMEM((3, 2) + tile, f32),
            pltpu.VMEM((2,) + tile, f32),
            pltpu.VMEM((7, 2) + tile, f32),
            pltpu.SemaphoreType.DMA((3, 6, 2, SLOTS)),
            pltpu.SemaphoreType.DMA((3, 6, 2, SLOTS)),
            pltpu.SemaphoreType.DMA((3,)),
            pltpu.SemaphoreType.DMA((3, 2)),
            pltpu.SemaphoreType.DMA((13,)),
            pltpu.SemaphoreType.DMA((13,)),
        ],
        compiler_params=pltpu.CompilerParams(
            collective_id=1, has_side_effects=True, vmem_limit_bytes=60 * 1024 * 1024
        ),
    )(
        active_t, operands, jnp.asarray(permutations()), d_outer, d_inner, d_qkv, d_att,
        vectors, jnp.asarray(lane_places()),
    )
    kept, lane = [], 0
    for _, _, keep in VECTORS:
        kept.append(vec_out[:, lane : lane + keep])
        lane += keep
    out = out.reshape(2, 6, 3, 4, 8, 128)[::-1]
    down = out[:, 0:2, :, 0:3].transpose(0, 2, 4, 1, 3, 5).reshape(2, 24, 768)
    up = out[:, 2:4, :, :, 0:6].transpose(0, 4, 1, 2, 3, 5).reshape(2, 6, 3072)
    first = out[:, 4, :, :, 0:6].transpose(0, 3, 1, 2, 4)
    last = out[:, 5, :, :, 0:6].transpose(0, 3, 1, 2, 4)
    qkv = jnp.concatenate([first, last[:, :, :, 0:2]], axis=3).reshape(2, 6, 2304)
    mixer = last[:, :, :, 2:4].reshape(2, 6, 768)
    return qkv, mixer, up, down, kept


def norm_forward(total_loss, gain, shift):
    center = total_loss - jnp.mean(total_loss, axis=-1, keepdims=True)
    spread = jnp.mean(center * center, axis=-1, keepdims=True)
    scaled = lax.rsqrt(spread + eps_norm)
    normed = center * scaled
    return (normed * gain + shift, normed, scaled)


def norm_backward(grad, normed, scaled, gain):
    grad_gain = jnp.sum(grad * normed, axis=(0, 1))
    grad_shift = jnp.sum(grad, axis=(0, 1))
    dnormed = grad * gain
    inside = (
        dnormed
        - jnp.mean(dnormed, axis=-1, keepdims=True)
        - normed * jnp.mean(dnormed * normed, axis=-1, keepdims=True)
    )
    return (scaled * inside, grad_gain, grad_shift)


def layer_forward(hidden, params, keymask):
    (
        triple_projection_matrix,
        probe_payload_shift,
        mixer_projection_matrix,
        mixer_projection_shift,
        mixer_scale_factor,
        mixer_shift_term,
        expand_layer_matrix,
        expand_layer_shift,
        shrink_layer_matrix,
        shrink_layer_shift,
        closing_scale_factor,
        closing_shift_term,
    ) = params
    count, length, width = hidden.shape
    heads_size = width // HEADS
    bias = probe_payload_shift.astype(jnp.float32)
    full_bias = jnp.concatenate([bias[:width], jnp.zeros((width,), jnp.float32), bias[width:]])
    hidden_reduced = hidden.astype(jnp.bfloat16)
    mixed = (
        jnp.einsum(
            "gwk,km->gwm",
            hidden_reduced,
            triple_projection_matrix,
            preferred_element_type=jnp.float32,
        )
        + full_bias
    )
    mixed_low = mixed.astype(jnp.bfloat16)
    query = mixed_low[..., :width].reshape(count, length, HEADS, heads_size)
    keys = mixed_low[..., width : 2 * width].reshape(count, length, HEADS, heads_size)
    values = mixed_low[..., 2 * width :].reshape(count, length, HEADS, heads_size)
    scores = jnp.einsum(
        "sqhd,skhd->shqk", query, keys, preferred_element_type=jnp.float32
    ) * heads_size ** (-0.5)
    scores = scores + keymask[:, None, None, :]
    expo = jnp.exp(scores - jnp.max(scores, axis=-1, keepdims=True))
    probs = expo / jnp.sum(expo, axis=-1, keepdims=True)
    probs_low = probs.astype(jnp.bfloat16)
    context = jnp.einsum("shqk,skhd->sqhd", probs_low, values, preferred_element_type=jnp.float32)
    context_reduced = context.astype(jnp.bfloat16).reshape(count, length, width)
    attended = jnp.einsum(
        "bry,yt->brt", context_reduced, mixer_projection_matrix, preferred_element_type=jnp.float32
    ) + mixer_projection_shift.astype(jnp.float32)
    middle, normed_one, scaled_one = norm_forward(
        hidden + attended,
        mixer_scale_factor.astype(jnp.float32),
        mixer_shift_term.astype(jnp.float32),
    )
    middle_reduced = middle.astype(jnp.bfloat16)
    inner = jnp.einsum(
        "ncm,mj->ncj", middle_reduced, expand_layer_matrix, preferred_element_type=jnp.float32
    ) + expand_layer_shift.astype(jnp.float32)
    activation_reduced = jax.nn.gelu(inner, approximate=False).astype(jnp.bfloat16)
    outer = jnp.einsum(
        "pcx,xj->pcj", activation_reduced, shrink_layer_matrix, preferred_element_type=jnp.float32
    ) + shrink_layer_shift.astype(jnp.float32)
    result, normed_two, scaled_two = norm_forward(
        middle + outer,
        closing_scale_factor.astype(jnp.float32),
        closing_shift_term.astype(jnp.float32),
    )
    saved = (
        hidden_reduced,
        query,
        keys,
        values,
        probs,
        probs_low,
        context_reduced,
        normed_one,
        scaled_one,
        middle_reduced,
        inner,
        activation_reduced,
        normed_two,
        scaled_two,
    )
    return (result, saved)


def layer_backward(grad_out, saved, params):
    (
        triple_projection_matrix,
        probe_payload_shift,
        mixer_projection_matrix,
        mixer_projection_shift,
        mixer_scale_factor,
        mixer_shift_term,
        expand_layer_matrix,
        expand_layer_shift,
        shrink_layer_matrix,
        shrink_layer_shift,
        closing_scale_factor,
        closing_shift_term,
    ) = params
    (
        hidden_reduced,
        query,
        keys,
        values,
        probs,
        probs_low,
        context_reduced,
        normed_one,
        scaled_one,
        middle_reduced,
        inner,
        activation_reduced,
        normed_two,
        scaled_two,
    ) = saved
    count, length, width = grad_out.shape
    heads_size = query.shape[-1]
    dsum_two, grad_fingain, grad_finshift = norm_backward(
        grad_out, normed_two, scaled_two, closing_scale_factor.astype(jnp.float32)
    )
    outer_gradient = dsum_two.astype(jnp.bfloat16)
    grad_downbias = jnp.sum(outer_gradient.astype(jnp.float32), axis=(0, 1))
    activation_gradient = jnp.einsum(
        "cov,gv->cog", outer_gradient, shrink_layer_matrix, preferred_element_type=jnp.float32
    )
    unused, gelu_pull = jax.vjp(partial(jax.nn.gelu, approximate=False), inner)
    inner_gradient = gelu_pull(activation_gradient)[0].astype(jnp.bfloat16)
    grad_ffnbias = jnp.sum(inner_gradient.astype(jnp.float32), axis=(0, 1))
    dmiddle = dsum_two + jnp.einsum(
        "qec,pc->qep", inner_gradient, expand_layer_matrix, preferred_element_type=jnp.float32
    )
    dsum_one, grad_attgain, grad_attshift = norm_backward(
        dmiddle, normed_one, scaled_one, mixer_scale_factor.astype(jnp.float32)
    )
    attention_gradient = dsum_one.astype(jnp.bfloat16)
    grad_outbias = jnp.sum(attention_gradient.astype(jnp.float32), axis=(0, 1))
    context_gradient = jnp.einsum(
        "cqu,wu->cqw",
        attention_gradient,
        mixer_projection_matrix,
        preferred_element_type=jnp.float32,
    )
    context_gradient = context_gradient.astype(jnp.bfloat16).reshape(
        count, length, HEADS, heads_size
    )
    dprobs = jnp.einsum(
        "sqhd,skhd->shqk", context_gradient, values, preferred_element_type=jnp.float32
    )
    dvalues = jnp.einsum(
        "shqk,sqhd->skhd", probs_low, context_gradient, preferred_element_type=jnp.float32
    )
    dscores = probs * (dprobs - jnp.sum(dprobs * probs, axis=-1, keepdims=True))
    dscores = dscores.astype(jnp.bfloat16)
    factor = heads_size ** (-0.5)
    dquery = (
        jnp.einsum("shqk,skhd->sqhd", dscores, keys, preferred_element_type=jnp.float32) * factor
    )
    dkeys = (
        jnp.einsum("shqk,sqhd->skhd", dscores, query, preferred_element_type=jnp.float32) * factor
    )
    mixed_gradient = jnp.concatenate(
        [
            dquery.reshape(count, length, width),
            dkeys.reshape(count, length, width),
            dvalues.reshape(count, length, width),
        ],
        axis=-1,
    )
    mixed_gradient = mixed_gradient.astype(jnp.bfloat16)
    bias_sums = jnp.sum(mixed_gradient.astype(jnp.float32), axis=(0, 1))
    grad_qvbias = jnp.concatenate([bias_sums[:width], bias_sums[2 * width :]])
    dhidden = dsum_one + jnp.einsum(
        "inu,tu->int", mixed_gradient, triple_projection_matrix, preferred_element_type=jnp.float32
    )
    grads = (
        grad_qvbias,
        grad_outbias,
        grad_attgain,
        grad_attshift,
        grad_ffnbias,
        grad_downbias,
        grad_fingain,
        grad_finshift,
    )
    products = (
        activation_reduced[0].T,
        jnp.stack([hidden_reduced[0], context_reduced[0], middle_reduced[0]]),
        outer_gradient[0],
        inner_gradient[0],
        mixed_gradient[0],
        attention_gradient[0],
    )
    return (dhidden, grads, products)


def pairing_kernel(emb_ref, companion_ref, widths_ref, divisor_ref, demb_ref, loss_ref, every, send_sem, recv_sem, core_s, core_r):
    place = my_place()
    core = place["c"]
    barrier = pltpu.get_barrier_semaphore()
    for axis in ("x", "y", "z"):
        for step in (1, 2, 3):
            pl.semaphore_signal(barrier, inc=1, device_id=neighbour(place, axis, step), device_id_type=MESH)
    pl.semaphore_signal(barrier, inc=1, device_id=neighbour(place, "c", 1), device_id_type=MESH)
    pl.semaphore_wait(barrier, 10)

    def slab(o, phase):
        done = ORDERS[o][:phase]
        at = tuple(pl.ds(0, 4) if axis in done else place[axis] for axis in ("z", "x", "c", "y"))
        return every.at[(o,) + at]

    def copies(o, phase):
        return [
            pltpu.make_async_remote_copy(
                src_ref=slab(o, phase), dst_ref=slab(o, phase),
                send_sem=send_sem.at[o, phase, step - 1], recv_sem=recv_sem.at[o, phase, step - 1],
                device_id=neighbour(place, ORDERS[o][phase], step), device_id_type=MESH,
            )
            for step in (1, 2, 3)
        ]

    for o in range(3):
        every[o, place["z"], place["x"], core, place["y"]] = emb_ref[o]
        for copy in copies(o, 0):
            copy.start()
    for phase in range(3):
        for o in range(3):
            for copy in copies(o, phase):
                copy.wait()
            if phase < 2:
                for copy in copies(o, phase + 1):
                    copy.start()
    mine = every.at[:, :, :, core]
    swap = pltpu.make_async_remote_copy(
        src_ref=mine, dst_ref=mine, send_sem=core_s, recv_sem=core_r,
        device_id=neighbour(place, "c", 1), device_id_type=MESH,
    )
    swap.start()
    swap.wait()

    me = ((place["z"] * 4 + place["x"]) * 2 + core) * 4 + place["y"]
    row = lax.broadcasted_iota(jnp.int32, (128, 128), 0)
    col = lax.broadcasted_iota(jnp.int32, (128, 128), 1)
    rows = lax.broadcasted_iota(jnp.int32, (128, 1), 0)
    lane = lax.broadcasted_iota(jnp.int32, (1, 768), 1)
    companion = companion_ref[...]
    divisor = divisor_ref[0]
    partner = (col == companion).astype(f32)
    is_me = rows == me
    loss = jnp.zeros((128, 1), f32)
    keeps = [(lane < widths_ref[p]).astype(f32) for p in range(4)]
    for e in range(2):
        embed = jnp.concatenate(
            [every[o].reshape(128, 4, 128)[:, e * 2 + r, :] for o in range(3) for r in range(2)], axis=1
        )
        high = embed.astype(bf16)
        low = (embed - high.astype(f32)).astype(bf16)
        own = jnp.sum(jnp.where(is_me, embed, 0.0), axis=0, keepdims=True)
        total = jnp.zeros((1, 768), f32)
        for p in range(4):
            keep = keeps[p]
            keep_low = keep.astype(bf16)
            high_p, low_p = high * keep_low, low * keep_low
            nt = (((1,), (1,)), ((), ()))
            gram = (
                lax.dot_general(high_p, high, nt, preferred_element_type=f32)
                + lax.dot_general(high_p, low, nt, preferred_element_type=f32)
                + lax.dot_general(low_p, high, nt, preferred_element_type=f32)
            )
            diagonal = jnp.where(row == col, gram, 0.0)
            inverse = lax.rsqrt(jnp.sum(diagonal, axis=1, keepdims=True) + eps_norm)
            inverse_row = lax.rsqrt(jnp.sum(diagonal, axis=0, keepdims=True) + eps_norm)
            sims = gram * inverse * inverse_row / divisor
            sims = jnp.where(row == col, -1e30, sims)
            top = jnp.max(sims, axis=1, keepdims=True)
            lse = top + jnp.log(jnp.sum(jnp.exp(sims - top), axis=1, keepdims=True))
            loss = loss + (lse - jnp.sum(sims * partner, axis=1, keepdims=True))
            to_me = jnp.sum(jnp.where(col == me, sims, 0.0), axis=1, keepdims=True)
            lse_me = jnp.sum(jnp.where(is_me, lse, 0.0), axis=0, keepdims=True)
            chosen = (companion == me).astype(f32)
            weight = jnp.exp(to_me - lse_me) + jnp.exp(to_me - lse) - 2.0 * chosen
            dunit = jnp.sum(embed * (weight * inverse), axis=0, keepdims=True) * keep
            inverse_me = jnp.sum(jnp.where(is_me, inverse, 0.0), axis=0, keepdims=True)
            unit_me = own * keep * inverse_me
            inside = dunit - unit_me * jnp.sum(unit_me * dunit, axis=1, keepdims=True)
            total = total + inside * inverse_me
        demb_ref[e : e + 1, :] = total / (8.0 * divisor)
    loss_ref[...] = loss / 8.0


def pairing_cost_term(averaged_layer_states, positive_companion, leading_dimension_counts, affinity_divisor):
    vmem = pl.BlockSpec(memory_space=pltpu.VMEM)
    smem = pl.BlockSpec(memory_space=pltpu.SMEM)
    parts = averaged_layer_states.reshape(2, 3, 2, 128).transpose(1, 0, 2, 3).reshape(3, 4, 128)
    demb, loss = pl.pallas_call(
        pairing_kernel,
        out_shape=(jax.ShapeDtypeStruct((2, 768), f32), jax.ShapeDtypeStruct((128, 1), f32)),
        in_specs=[vmem, vmem, smem, smem],
        out_specs=(vmem, vmem),
        scratch_shapes=[
            pltpu.VMEM((3, 4, 4, 2, 4, 4, 128), f32),
            pltpu.SemaphoreType.DMA((3, 3, 3)),
            pltpu.SemaphoreType.DMA((3, 3, 3)),
            pltpu.SemaphoreType.DMA,
            pltpu.SemaphoreType.DMA,
        ],
        compiler_params=pltpu.CompilerParams(
            collective_id=2, has_side_effects=True, vmem_limit_bytes=32 * 1024 * 1024
        ),
    )(parts, positive_companion[:, None], leading_dimension_counts, affinity_divisor)
    row_losses = lax.dynamic_slice_in_dim(loss[:, 0], lax.axis_index("batch") * 4, 4)
    return (row_losses, demb[None])


def body(
    slot_state_vectors,
    sequence_token_counts,
    positive_companion,
    leading_dimension_counts,
    affinity_divisor,
    triple_projection_matrix,
    probe_payload_shift,
    mixer_projection_matrix,
    mixer_projection_shift,
    mixer_scale_factor,
    mixer_shift_term,
    expand_layer_matrix,
    expand_layer_shift,
    shrink_layer_matrix,
    shrink_layer_shift,
    closing_scale_factor,
    closing_shift_term,
):
    weights = (
        triple_projection_matrix,
        probe_payload_shift,
        mixer_projection_matrix,
        mixer_projection_shift,
        mixer_scale_factor,
        mixer_shift_term,
        expand_layer_matrix,
        expand_layer_shift,
        shrink_layer_matrix,
        shrink_layer_shift,
        closing_scale_factor,
        closing_shift_term,
    )
    first = tuple((w[0] for w in weights))
    second = tuple((w[1] for w in weights))
    places = lax.broadcasted_iota(jnp.int32, slot_state_vectors.shape[:2], 1)
    valid = (places < sequence_token_counts[:, None]).astype(jnp.float32)
    keymask = (valid - 1.0) * 1000000000.0
    counts = sequence_token_counts.astype(jnp.float32)[:, None]
    inputs = slot_state_vectors.astype(jnp.float32)
    front, saved_front = layer_forward(inputs, first, keymask)
    behind, saved_behind = layer_forward(front, second, keymask)
    averaged_layer_states = jnp.stack(
        [
            jnp.sum(front * valid[:, :, None], axis=1) / counts,
            jnp.sum(behind * valid[:, :, None], axis=1) / counts,
        ],
        axis=1,
    )
    row_losses, embedding_gradient = pairing_cost_term(
        averaged_layer_states, positive_companion, leading_dimension_counts, affinity_divisor
    )
    spread = valid[:, :, None] / counts[:, :, None]
    dfront, grads_behind, products_behind = layer_backward(
        spread * embedding_gradient[:, 1][:, None, :], saved_behind, second
    )
    dfront = dfront + spread * embedding_gradient[:, 0][:, None, :]
    dinputs, grads_front, products_front = layer_backward(dfront, saved_front, first)
    def joined(qvbias, outbias, attgain, attshift, ffnbias, downbias, fingain, finshift):
        return jnp.concatenate([outbias, attgain, attshift, downbias, fingain, finshift, qvbias, ffnbias])

    qkv, mixer, up, down, kept = reduce_gradients(
        jnp.stack([joined(*grads_front), joined(*grads_behind)]),
        *(jnp.stack([pf, pb]) for pf, pb in zip(products_front, products_behind)),
    )
    outbias, attgain, attshift, downbias, fingain, finshift, qvbias, ffnbias = kept
    return (
        row_losses,
        averaged_layer_states,
        dinputs,
        qkv,
        qvbias,
        mixer,
        outbias,
        attgain,
        attshift,
        up,
        ffnbias,
        down,
        downbias,
        fingain,
        finshift,
    )


def solution(mesh):
    return jax.shard_map(
        body,
        mesh=mesh,
        in_specs=(
            P(("batch", "tile"), None, None),
            P(("batch", "tile")),
            P(),
            P(),
            P(),
            P(),
            P(),
            P(),
            P(),
            P(),
            P(),
            P(),
            P(),
            P(),
            P(),
            P(),
            P(),
        ),
        out_specs=(
            P("batch"),
            P(("batch", "tile"), None, None),
            P(("batch", "tile"), None, None),
            P(None, ("batch", "tile"), None),
            P(None, ("batch", "tile")),
            P(None, ("batch", "tile"), None),
            P(None, ("batch", "tile")),
            P(None, ("batch", "tile")),
            P(None, ("batch", "tile")),
            P(None, ("batch", "tile"), None),
            P(None, ("batch", "tile")),
            P(None, ("batch", "tile"), None),
            P(None, ("batch", "tile")),
            P(None, ("batch", "tile")),
            P(None, ("batch", "tile")),
        ),
        check_vma=False,
    )
```

```python
import jax
import jax.numpy as jnp
import ml_dtypes
import numpy as np
from jax import lax
from jax.experimental import pallas as pl
from jax.experimental.pallas import tpu as pltpu
from jax.sharding import PartitionSpec as P

eps_norm = 1e-06

f32, bf16 = jnp.float32, jnp.bfloat16
MESH = pl.DeviceIdType.MESH
TRIPLES = 12
SLOTS = 3
ORDERS = (("x", "y", "z"), ("y", "z", "x"), ("z", "x", "y"))


def my_place():
    b = lax.axis_index("batch")
    return {"z": b // 8, "x": lax.rem(b // 2, 4), "c": lax.rem(b, 2), "y": lax.axis_index("tile")}


def device_at(place):
    return {"batch": (place["z"] * 4 + place["x"]) * 2 + place["c"], "tile": place["y"]}


def neighbour(place, axis, step):
    there = dict(place)
    if axis == "c":
        there["c"] = 1 - place["c"]
    else:
        there[axis] = lax.rem(place[axis] + step + 4, 4)
    return device_at(there)


GROUP = tuple((flip, step) for flip in (0, 1) for step in range(4) if flip or step)
VECTORS = tuple((768 * k, 768, 6) for k in range(6)) + ((4608, 1536, 12), (6144, 3072, 24))


def in_group(place, flip, step):
    there = dict(place)
    there["c"] = lax.rem(place["c"] + flip, 2)
    there["y"] = lax.rem(place["y"] + step, 4)
    return device_at(there)


def gelu_parts(inner):
    half = 0.5 * (1.0 + lax.erf(inner * 0.7071067811865476))
    return inner * half, half


def lanes_of(j, width):
    return pl.ds(pl.multiple_of(j * width, width), width)


def rows_of(i, height):
    return pl.ds(pl.multiple_of(i * height, height), height)


NT = (((1,), (1,)), ((), ()))
TN = (((0,), (0,)), ((), ()))


def head_halves(pair):
    first = lax.broadcasted_iota(jnp.int32, pair.shape, 1) < 64
    nothing = jnp.zeros_like(pair)
    return jnp.concatenate([jnp.where(first, pair, nothing), jnp.where(first, nothing, pair)], axis=0)


def pair_probs(q, k, keymask):
    scores = lax.dot_general(head_halves(q * 0.125), k, NT, preferred_element_type=f32) + keymask
    expo = jnp.exp(scores - jnp.max(scores, axis=1, keepdims=True))
    return expo * (1.0 / jnp.sum(expo, axis=1, keepdims=True))


def forward_kernel(
    x_ref, count_ref, wq_ref, bq_ref, wo_ref, bo_ref, g1_ref, s1_ref, wu_ref, bu_ref, wd_ref, bd_ref, g2_ref, s2_ref,
    emb_ref, xb_out, qkv_out, ctx_out, n1_out, r1_out, inner_out, n2_out, r2_out,
    wq, wo, wu, wd, vq, vo, v1, t1, vu, vd, v2, t2, xf, mid_f, mid_b, pool,
    act, xb, qkv, ctx, n1, r1, inner, n2, r2, load_sem, save_sem,
):
    def load(k, layer):
        src, dst = ((wq_ref, wq), (wo_ref, wo), (wu_ref, wu), (wd_ref, wd))[k]
        return pltpu.make_async_copy(src.at[layer], dst.at[layer], load_sem.at[k, layer])

    for layer in range(2):
        for k in range(4):
            load(k, layer).start()

    saves = ((xb, xb_out), (qkv, qkv_out), (ctx, ctx_out), (n1, n1_out), (r1, r1_out), (inner, inner_out), (n2, n2_out), (r2, r2_out))

    def save(k, layer):
        src, dst = saves[k]
        return pltpu.make_async_copy(src.at[layer], dst.at[layer], save_sem.at[k, layer])

    for src, dst in ((bo_ref, vo), (g1_ref, v1), (s1_ref, t1), (bu_ref, vu), (bd_ref, vd), (g2_ref, v2), (s2_ref, t2)):
        for layer in range(2):
            dst[layer] = src[layer : layer + 1, :].astype(f32)
    for layer in range(2):
        vq[layer, :, 0:768] = bq_ref[layer : layer + 1, 0:768].astype(f32)
        vq[layer, :, 768:1536] = jnp.zeros((1, 768), f32)
        vq[layer, :, 1536:2304] = bq_ref[layer : layer + 1, 768:1536].astype(f32)
    xf[...] = x_ref[0].astype(f32)
    count = count_ref[0]
    keymask = jnp.where(lax.broadcasted_iota(jnp.int32, (1, 256), 1) < count, 0.0, -1e9)

    def norm(z, layer, normed_ref, scaled_ref, gain, shift, rows):
        center = z - jnp.mean(z, axis=1, keepdims=True)
        scaled = lax.rsqrt(jnp.mean(center * center, axis=1, keepdims=True) + eps_norm)
        normed = center * scaled
        normed_ref[layer, rows, :] = normed
        scaled_ref[layer, rows, :] = scaled
        return normed * gain[layer] + shift[layer]

    def one_layer(layer, _):
        xb[layer] = xf[...].astype(bf16)
        save(0, layer).start()
        load(0, layer).wait()

        def project(j, _):
            cols = lanes_of(j, 2304)
            mixed = jnp.dot(xb[layer], wq[layer, :, cols], preferred_element_type=f32) + vq[layer, :, cols]
            qkv[layer, :, cols] = mixed.astype(bf16)
            return 0

        lax.fori_loop(0, 1, project, 0)
        save(1, layer).start()

        def attend(pair, _):
            q, k, v = (qkv[layer, :, lanes_of(pair + 6 * third, 128)] for third in range(3))
            probs = pair_probs(q, k, keymask).astype(bf16)
            both = jnp.dot(probs, v, preferred_element_type=f32)
            first = lax.broadcasted_iota(jnp.int32, (256, 128), 1) < 64
            ctx[layer, :, lanes_of(pair, 128)] = jnp.where(first, both[:256], both[256:]).astype(bf16)
            return 0

        lax.fori_loop(0, 6, attend, 0, unroll=6)
        save(2, layer).start()
        load(1, layer).wait()

        def mix(j, _):
            cols = lanes_of(j, 768)
            xf[:, cols] += jnp.dot(ctx[layer], wo[layer, :, cols], preferred_element_type=f32) + vo[layer, :, cols]
            return 0

        lax.fori_loop(0, 1, mix, 0)

        def norm_one(i, _):
            rows = rows_of(i, 64)
            mid = norm(xf[rows, :], layer, n1, r1, v1, t1, rows)
            mid_f[rows, :] = mid
            mid_b[rows, :] = mid.astype(bf16)
            return 0

        lax.fori_loop(0, 4, norm_one, 0, unroll=4)
        save(3, layer).start()
        save(4, layer).start()
        load(2, layer).wait()

        def expand(j, _):
            cols = lanes_of(j, 1024)
            value = jnp.dot(mid_b[...], wu[layer, :, cols], preferred_element_type=f32) + vu[layer, :, cols]
            inner[layer, :, cols] = value
            act[:, cols] = gelu_parts(value)[0].astype(bf16)
            return 0

        lax.fori_loop(0, 3, expand, 0)
        save(5, layer).start()
        load(3, layer).wait()

        def shrink(j, _):
            cols = lanes_of(j, 768)
            mid_f[:, cols] += jnp.dot(act[...], wd[layer, :, cols], preferred_element_type=f32) + vd[layer, :, cols]
            return 0

        lax.fori_loop(0, 1, shrink, 0)

        def norm_two(i, total):
            rows = rows_of(i, 64)
            result = norm(mid_f[rows, :], layer, n2, r2, v2, t2, rows)
            xf[rows, :] = result
            place = lax.broadcasted_iota(jnp.int32, (64, 1), 0) + i * 64
            return total + jnp.sum(jnp.where(place < count, result, 0.0), axis=0, keepdims=True)

        total = lax.fori_loop(0, 4, norm_two, jnp.zeros((1, 768), f32), unroll=4)
        pool[layer] = total / count.astype(f32)
        save(6, layer).start()
        save(7, layer).start()
        return 0

    lax.fori_loop(0, 2, one_layer, 0)
    for layer in range(2):
        emb_ref[0, layer : layer + 1, :] = pool[layer]
    for layer in range(2):
        for k in range(8):
            save(k, layer).wait()


SAVED = ((768, "b"), (2304, "b"), (768, "b"), (768, "f"), (1, "f"), (3072, "f"), (768, "f"), (1, "f"))


def run_forward(slots, counts, weights):
    vmem = pl.BlockSpec(memory_space=pltpu.VMEM)
    smem = pl.BlockSpec(memory_space=pltpu.SMEM)
    hbm = pl.BlockSpec(memory_space=pl.ANY)
    kept = [((2, 256, width), bf16 if kind == "b" else f32) for width, kind in SAVED]
    places = [vmem, smem, hbm, vmem, hbm, vmem, vmem, vmem, hbm, vmem, hbm, vmem, vmem, vmem]
    widths = (2304, 768, 768, 768, 3072, 768, 768, 768)
    out = pl.pallas_call(
        forward_kernel,
        out_shape=[jax.ShapeDtypeStruct((1, 2, 768), f32)] + [jax.ShapeDtypeStruct(s, t) for s, t in kept],
        in_specs=places,
        out_specs=[vmem] + [hbm] * len(kept),
        scratch_shapes=[
            pltpu.VMEM((2, 768, 2304), bf16),
            pltpu.VMEM((2, 768, 768), bf16),
            pltpu.VMEM((2, 768, 3072), bf16),
            pltpu.VMEM((2, 3072, 768), bf16),
        ]
        + [pltpu.VMEM((2, 1, width), f32) for width in widths]
        + [pltpu.VMEM((256, 768), f32), pltpu.VMEM((256, 768), f32), pltpu.VMEM((256, 768), bf16), pltpu.VMEM((2, 1, 768), f32)]
        + [pltpu.VMEM((256, 3072), bf16)]
        + [pltpu.VMEM(s, t) for s, t in kept]
        + [pltpu.SemaphoreType.DMA((4, 2)), pltpu.SemaphoreType.DMA((8, 2))],
        compiler_params=pltpu.CompilerParams(vmem_limit_bytes=62 * 1024 * 1024),
    )(slots, counts, *weights)
    return out[0], out[1:]


def pairing_kernel(emb_ref, companion_ref, widths_ref, divisor_ref, demb_ref, loss_ref, every, send_sem, recv_sem, core_s, core_r):
    place = my_place()
    core = place["c"]
    barrier = pltpu.get_barrier_semaphore()
    for axis in ("x", "y", "z"):
        for step in (1, 2, 3):
            pl.semaphore_signal(barrier, inc=1, device_id=neighbour(place, axis, step), device_id_type=MESH)
    pl.semaphore_signal(barrier, inc=1, device_id=neighbour(place, "c", 1), device_id_type=MESH)
    pl.semaphore_wait(barrier, 10)

    def slab(o, phase):
        done = ORDERS[o][:phase]
        at = tuple(pl.ds(0, 4) if axis in done else place[axis] for axis in ("z", "x", "c", "y"))
        return every.at[(o,) + at]

    def copies(o, phase):
        return [
            pltpu.make_async_remote_copy(
                src_ref=slab(o, phase), dst_ref=slab(o, phase),
                send_sem=send_sem.at[o, phase, step - 1], recv_sem=recv_sem.at[o, phase, step - 1],
                device_id=neighbour(place, ORDERS[o][phase], step), device_id_type=MESH,
            )
            for step in (1, 2, 3)
        ]

    for o in range(3):
        for e in range(2):
            for r in range(2):
                at = 256 * o + 128 * r
                every[o, place["z"], place["x"], core, place["y"], e * 2 + r : e * 2 + r + 1, :] = emb_ref[0, e : e + 1, at : at + 128]
        for copy in copies(o, 0):
            copy.start()
    for phase in range(3):
        for o in range(3):
            for copy in copies(o, phase):
                copy.wait()
            if phase < 2:
                for copy in copies(o, phase + 1):
                    copy.start()
    mine = every.at[:, :, :, core]
    swap = pltpu.make_async_remote_copy(
        src_ref=mine, dst_ref=mine, send_sem=core_s, recv_sem=core_r,
        device_id=neighbour(place, "c", 1), device_id_type=MESH,
    )
    swap.start()
    swap.wait()

    me = ((place["z"] * 4 + place["x"]) * 2 + core) * 4 + place["y"]
    row = lax.broadcasted_iota(jnp.int32, (128, 128), 0)
    col = lax.broadcasted_iota(jnp.int32, (128, 128), 1)
    rows = lax.broadcasted_iota(jnp.int32, (128, 1), 0)
    lane = lax.broadcasted_iota(jnp.int32, (1, 768), 1)
    companion = companion_ref[...]
    divisor = divisor_ref[0]
    partner = (col == companion).astype(f32)
    is_me = rows == me
    loss = jnp.zeros((128, 1), f32)
    keeps = [(lane < widths_ref[p]).astype(f32) for p in range(4)]
    for e in range(2):
        embed = jnp.concatenate(
            [every[o].reshape(128, 4, 128)[:, e * 2 + r, :] for o in range(3) for r in range(2)], axis=1
        )
        high = embed.astype(bf16)
        low = (embed - high.astype(f32)).astype(bf16)
        own = jnp.sum(jnp.where(is_me, embed, 0.0), axis=0, keepdims=True)
        total = jnp.zeros((1, 768), f32)
        for p in range(4):
            keep = keeps[p]
            keep_low = keep.astype(bf16)
            high_p, low_p = high * keep_low, low * keep_low
            nt = (((1,), (1,)), ((), ()))
            gram = (
                lax.dot_general(high_p, high, nt, preferred_element_type=f32)
                + lax.dot_general(high_p, low, nt, preferred_element_type=f32)
                + lax.dot_general(low_p, high, nt, preferred_element_type=f32)
            )
            diagonal = jnp.where(row == col, gram, 0.0)
            inverse = lax.rsqrt(jnp.sum(diagonal, axis=1, keepdims=True) + eps_norm)
            inverse_row = lax.rsqrt(jnp.sum(diagonal, axis=0, keepdims=True) + eps_norm)
            sims = gram * inverse * inverse_row / divisor
            sims = jnp.where(row == col, -1e30, sims)
            top = jnp.max(sims, axis=1, keepdims=True)
            lse = top + jnp.log(jnp.sum(jnp.exp(sims - top), axis=1, keepdims=True))
            loss = loss + (lse - jnp.sum(sims * partner, axis=1, keepdims=True))
            to_me = jnp.sum(jnp.where(col == me, sims, 0.0), axis=1, keepdims=True)
            lse_me = jnp.sum(jnp.where(is_me, lse, 0.0), axis=0, keepdims=True)
            chosen = (companion == me).astype(f32)
            weight = jnp.exp(to_me - lse_me) + jnp.exp(to_me - lse) - 2.0 * chosen
            dunit = jnp.sum(embed * (weight * inverse), axis=0, keepdims=True) * keep
            inverse_me = jnp.sum(jnp.where(is_me, inverse, 0.0), axis=0, keepdims=True)
            unit_me = own * keep * inverse_me
            inside = dunit - unit_me * jnp.sum(unit_me * dunit, axis=1, keepdims=True)
            total = total + inside * inverse_me
        demb_ref[e : e + 1, :] = total / (8.0 * divisor)
    loss_ref[...] = loss / 8.0


def pairing_cost_term(averaged_layer_states, positive_companion, leading_dimension_counts, affinity_divisor):
    vmem = pl.BlockSpec(memory_space=pltpu.VMEM)
    smem = pl.BlockSpec(memory_space=pltpu.SMEM)
    demb, loss = pl.pallas_call(
        pairing_kernel,
        out_shape=(jax.ShapeDtypeStruct((2, 768), f32), jax.ShapeDtypeStruct((128, 1), f32)),
        in_specs=[vmem, vmem, smem, smem],
        out_specs=(vmem, vmem),
        scratch_shapes=[
            pltpu.VMEM((3, 4, 4, 2, 4, 4, 128), f32),
            pltpu.SemaphoreType.DMA((3, 3, 3)),
            pltpu.SemaphoreType.DMA((3, 3, 3)),
            pltpu.SemaphoreType.DMA,
            pltpu.SemaphoreType.DMA,
        ],
        compiler_params=pltpu.CompilerParams(
            collective_id=2, has_side_effects=True, vmem_limit_bytes=32 * 1024 * 1024
        ),
    )(averaged_layer_states, positive_companion[:, None], leading_dimension_counts, affinity_divisor)
    return loss, demb


def permutations():
    rows = np.arange(768).reshape(4, 4, 2, 4, 6)
    names = {"z": 0, "x": 1, "c": 2, "y": 3}
    out = np.zeros((3, 768, 768), np.float32)
    for o, (d1, d2, d3) in enumerate(ORDERS):
        taken = rows.transpose(2, names[d1], names[d2], names[d3], 4).reshape(-1)
        out[o, np.arange(768), taken] = 1
    return out.astype(ml_dtypes.bfloat16)


def lane_places():
    out = np.zeros((9216, 128), np.float32)
    lane = 0
    for start, width, keep in VECTORS:
        q = np.arange(width)
        out[start + q, lane + q % keep] = 1
        lane += keep
    return out.astype(ml_dtypes.bfloat16)


def backward_kernel(
    count_ref, demb_ref, g1_ref, t1_ref, g2_ref, wq_ref, wo_ref, wu_ref, wd_ref,
    xb_ref, qkv_ref, ctx_ref, n1_ref, r1_ref, inner_ref, n2_ref, r2_ref, perm_ref, spread_ref,
    out_ref, vec_out_ref, dx_ref,
    weight, perm, spread, xb, qkv, ctx, n1, r1, inner, n2, r2, gains, grad, d_outer, d_att, d_ctx, act_t, d_inner, d_qkv, vectors,
    apt, half, send, got0, got1a, got1b, half2, got2a, got2b, half3, got3a, got3b, rows24,
    vec_src, vec_z, vec_x, vec_mid, vec_cy,
    weight_sem, load_sem, table_sem, sems_s, sems_r, sem0_s, sem0_r, vec_s, vec_r,
):
    place = my_place()
    core = place["c"]
    saved = {
        "xb": (xb_ref, xb, 0), "qkv": (qkv_ref, qkv, 1), "ctx": (ctx_ref, ctx, 2), "n1": (n1_ref, n1, 3), "r1": (r1_ref, r1, 4),
        "inner": (inner_ref, inner, 5), "n2": (n2_ref, n2, 6), "r2": (r2_ref, r2, 7),
    }

    def load(name, layer):
        src, dst, k = saved[name]
        return pltpu.make_async_copy(src.at[layer], dst, load_sem.at[k])

    def weights(k, layer):
        slot = lax.rem((1 - layer) * 3 + k, 2)
        blocks = []
        for m in range(4):
            cols = pl.ds(768 * m, 768)
            if k == 0:
                src = wd_ref.at[layer, cols]
            elif k == 1:
                src = wu_ref.at[layer, :, cols]
            else:
                src = wq_ref.at[layer, :, cols] if m < 3 else wo_ref.at[layer]
            blocks.append(pltpu.make_async_copy(src, weight.at[slot, cols], weight_sem.at[slot, m]))
        return slot, blocks

    def fetch_weights(k, layer):
        for copy in weights(k, layer)[1]:
            copy.start()

    def ready_weights(k, layer):
        slot, blocks = weights(k, layer)
        for copy in blocks:
            copy.wait()
        return slot

    tables = (
        pltpu.make_async_copy(perm_ref, perm, table_sem.at[0]),
        pltpu.make_async_copy(spread_ref, spread, table_sem.at[1]),
    )
    for name in ("n2", "r2", "inner"):
        load(name, 1).start()
    fetch_weights(0, 1)
    for name in ("n1", "r1"):
        load(name, 1).start()
    tables[0].start()
    fetch_weights(1, 1)
    for name in ("xb", "ctx", "qkv"):
        load(name, 1).start()
    tables[1].start()

    barrier = pltpu.get_barrier_semaphore()
    for axis in ("x", "z"):
        for step in (1, 2, 3):
            pl.semaphore_signal(barrier, inc=1, device_id=neighbour(place, axis, step), device_id_type=MESH)
    for flip, step in GROUP:
        pl.semaphore_signal(barrier, inc=1, device_id=in_group(place, flip, step), device_id_type=MESH)

    half3[...] = jnp.zeros_like(half3)
    for k, src in enumerate((g1_ref, t1_ref, g2_ref)):
        for layer in range(2):
            gains[k, layer] = src[layer : layer + 1, :].astype(f32)
    count = count_ref[0]
    keymask = jnp.where(lax.broadcasted_iota(jnp.int32, (1, 256), 1) < count, 0.0, -1e9)
    places = lax.broadcasted_iota(jnp.int32, (256, 1), 0)
    pooled = jnp.where(places < count, 1.0, 0.0) / count.astype(f32)

    def norm_back(normed, scaled, gain, rounded, at_gain, at_shift, at_bias, layer):
        sums = [jnp.zeros((1, 768), f32) for _ in range(3)]
        for i in range(4):
            rows = pl.ds(64 * i, 64)
            dy, n = grad[rows, :], normed[rows, :]
            dn = dy * gain
            inside = dn - jnp.mean(dn, axis=1, keepdims=True) - n * jnp.mean(dn * n, axis=1, keepdims=True)
            dz = scaled[rows, :] * inside
            low = dz.astype(bf16)
            grad[rows, :] = dz
            rounded[rows, :] = low
            for k, term in enumerate((dy * n, dy, low.astype(f32))):
                sums[k] = sums[k] + jnp.sum(term, axis=0, keepdims=True)
        for at, total in zip((at_gain, at_shift, at_bias), sums):
            vectors[layer, :, at : at + 768] = total

    def begin_layer(layer):
        load("n2", layer).wait()
        load("r2", layer).wait()
        own = demb_ref[0:1, :]

        @pl.when(layer == 1)
        def _():
            grad[...] = pooled * demb_ref[1:2, :]

        @pl.when(layer == 0)
        def _():
            grad[...] += pooled * own

        norm_back(n2, r2, gains[2, layer], d_outer, 3072, 3840, 2304, layer)

        @pl.when(layer == 1)
        def _():
            load("n2", 0).start()
            load("r2", 0).start()

        load("inner", layer).wait()

        def turn(j, _):
            value = inner[:, lanes_of(j, 256)]
            act_t[lanes_of(j, 256), :] = gelu_parts(value)[0].T.astype(bf16)
            return 0

        lax.fori_loop(0, 12, turn, 0, unroll=2)

    def through_expand(layer):
        slot = ready_weights(0, layer)

        def chunk(j, _):
            cols = lanes_of(j, 512)
            d_act = lax.dot_general(d_outer[...], weight[slot, cols, :], NT, preferred_element_type=f32)
            value = inner[:, cols]
            slope = gelu_parts(value)[1] + value * (jnp.exp(-0.5 * value * value) * 0.3989422804014327)
            low = (d_act * slope).astype(bf16)
            d_inner[:, cols] = low
            at = pl.ds(pl.multiple_of(6144 + j * 512, 512), 512)
            vectors[layer, :, at] = jnp.sum(low.astype(f32), axis=0, keepdims=True)
            return 0

        lax.fori_loop(0, 6, chunk, 0, unroll=2)

        @pl.when(layer == 1)
        def _():
            load("inner", 0).start()

        fetch_weights(2, layer)
        load("n1", layer).wait()
        load("r1", layer).wait()
        permute((n1[...] * gains[0, layer] + gains[1, layer]).astype(bf16), 0)

    def permute(operand, which):
        for o in range(3):
            apt[o, which] = lax.dot_general(perm[o], operand, NT, preferred_element_type=f32).astype(bf16)

    def through_mixer(layer):
        slot = ready_weights(1, layer)
        for m in range(4):
            cols = pl.ds(768 * m, 768)
            grad[...] += lax.dot_general(d_inner[:, cols], weight[slot, cols, :], NT, preferred_element_type=f32)
        norm_back(n1, r1, gains[0, layer], d_att, 768, 1536, 0, layer)

        @pl.when(layer == 1)
        def _():
            fetch_weights(0, 0)
            load("n1", 0).start()
            load("r1", 0).start()

        slot = ready_weights(2, layer)
        d_ctx[...] = lax.dot_general(d_att[...], weight[slot, 2304:3072, :], NT, preferred_element_type=f32).astype(bf16)

    def through_attention(layer, first_pair, pairs):
        def pair_back(i, _):
            pair = first_pair + i
            at = [lanes_of(pair + 6 * third, 128) for third in range(3)]
            q, k, v = (qkv[:, cols] for cols in at)
            probs = pair_probs(q, k, keymask)
            dc = head_halves(d_ctx[:, at[0]])
            dp = lax.dot_general(dc, v, NT, preferred_element_type=f32)
            ds = (probs * (dp - jnp.sum(dp * probs, axis=1, keepdims=True))).astype(bf16)
            dq = jnp.dot(
                jnp.concatenate([ds[:256], ds[256:]], axis=1), head_halves(k * 0.125), preferred_element_type=f32
            ).astype(bf16)
            dk = lax.dot_general(ds, head_halves(q * 0.125), TN, preferred_element_type=f32).astype(bf16)
            dv = lax.dot_general(probs.astype(bf16), dc, TN, preferred_element_type=f32).astype(bf16)
            for cols, value in zip(at, (dq, dk, dv)):
                d_qkv[:, cols] = value
            for start, value in ((4608, dq), (5376, dv)):
                where = pl.ds(pl.multiple_of(start + pair * 128, 128), 128)
                vectors[layer, :, where] = jnp.sum(value.astype(f32), axis=0, keepdims=True)
            return 0

        lax.fori_loop(0, pairs, pair_back, 0, unroll=2)

    def through_projection(layer):
        slot = lax.rem((1 - layer) * 3 + 2, 2)
        for m in range(3):
            cols = pl.ds(768 * m, 768)
            grad[...] += lax.dot_general(d_qkv[:, cols], weight[slot, cols, :], NT, preferred_element_type=f32)

        @pl.when(layer == 1)
        def _():
            fetch_weights(1, 0)
            load("qkv", 0).start()

        @pl.when(layer == 0)
        def _():
            dx_ref[0] = grad[...]

    def store_rows(o, slot, mine, tile0, value):
        for j in range(value.shape[1] // 128):
            part = value[:, 128 * j : 128 * (j + 1)].reshape(16, 3, 8, 128)
            if mine:
                half[o, slot, :, tile0 + 3 * j : tile0 + 3 * j + 3] = part
            else:
                send[o, :, tile0 + 3 * j : tile0 + 3 * j + 3] = part

    def product(o, slot, which, ref, at, width, tile0):
        for mine in (True, False):
            c = core if mine else 1 - core
            lhs = apt[o, which, pl.ds(pl.multiple_of(c * 384, 128), 384), :]
            for w in range(0, width, 256):
                value = jnp.dot(lhs, ref[:, at + w : at + w + 256], preferred_element_type=f32)
                store_rows(o, slot, mine, tile0 + 3 * (w // 128), value)

    def product_shrink(slot, k):
        def block(z, _):
            for mine in (True, False):
                c = core if mine else 1 - core
                lhs = jnp.concatenate(
                    [act_t[pl.ds(pl.multiple_of(z * 768 + x * 192 + c * 96, 32), 96), :] for x in range(4)], axis=0
                )
                value = jnp.dot(lhs, d_outer[:, 384 * k : 384 * (k + 1)], preferred_element_type=f32)
                for x in range(4):
                    for y in range(4):
                        for j in range(3):
                            p = {"x": x, "y": y, "z": z}
                            d1, d2, d3 = (p[axis] for axis in ORDERS[j])
                            row = x * 96 + (y * 3 + j) * 8
                            for ct in range(3):
                                tile = value[row : row + 8, 128 * ct : 128 * ct + 128]
                                if mine:
                                    half[j, slot, d1 * 4 + d2, d3 * 3 + ct] = tile
                                else:
                                    send[j, d1 * 4 + d2, d3 * 3 + ct] = tile
            return 0

        lax.fori_loop(0, 4, block, 0)

    def make(u):
        slot = lax.rem(u, 4)
        layer = 1 - u // 6
        kind = lax.rem(u, 6)

        def to_other_core():
            for o in range(3):
                copy0(o, u).start()

        @pl.when(kind == 0)
        def _():
            begin_layer(layer)
            product_shrink(slot, 0)
            to_other_core()

        @pl.when(kind == 1)
        def _():
            product_shrink(slot, 1)
            to_other_core()

            @pl.when(u == 1)
            def _():
                tables[0].wait()

            through_expand(layer)

        @pl.when(kind == 2)
        def _():
            for o in range(3):
                product(o, slot, 0, d_inner, o * 512, 512, 0)
            to_other_core()
            through_mixer(layer)

        @pl.when(kind == 3)
        def _():
            for o in range(3):
                product(o, slot, 0, d_inner, (3 + o) * 512, 512, 0)
            to_other_core()
            load("xb", layer).wait()
            permute(xb[...], 0)
            load("ctx", layer).wait()
            permute(ctx[...], 1)

            @pl.when(layer == 1)
            def _():
                load("xb", 0).start()
                load("ctx", 0).start()

            load("qkv", layer).wait()
            through_attention(layer, 0, 4)

        @pl.when(kind == 4)
        def _():
            for o in range(3):
                product(o, slot, 0, d_qkv, o * 768, 512, 0)
            to_other_core()
            through_attention(layer, 4, 2)
            through_projection(layer)

        @pl.when(kind == 5)
        def _():
            for o in range(3):
                product(o, slot, 0, d_qkv, o * 768 + 512, 256, 0)
                product(o, slot, 1, d_att, o * 256, 256, 6)
            to_other_core()

    def exchange(o, k, slot, src_up, src_down, got):
        axis = ORDERS[o][k // 2]
        return [
            pltpu.make_async_remote_copy(
                src_ref=src, dst_ref=got.at[o, slot, way],
                send_sem=sems_s.at[o, k, way, slot], recv_sem=sems_r.at[o, k, way, slot],
                device_id=neighbour(place, axis, step), device_id_type=MESH,
            )
            for way, (src, step) in enumerate(((src_up, 1), (src_down, -1)))
        ]

    def spots(o, phase):
        a = place[ORDERS[o][phase]]
        return a, lax.rem(a + 1, 4), lax.rem(a + 2, 4), lax.rem(a + 3, 4)

    def copy0(o, u):
        slot = lax.rem(u, 2)
        return pltpu.make_async_remote_copy(
            src_ref=send.at[o], dst_ref=got0.at[o, slot], send_sem=sem0_s.at[o], recv_sem=sem0_r.at[o, slot],
            device_id=neighbour(place, "c", 1), device_id_type=MESH,
        )

    def step_a(o, phase, u):
        slot = lax.rem(u, SLOTS)
        a, up, far, down = spots(o, phase)
        if phase == 0:
            src, got = (half.at[o, lax.rem(u, 4), pl.ds(far * 4, 2)], half.at[o, lax.rem(u, 4), pl.ds(far * 4 + 2, 2)]), got1a
        elif phase == 1:
            src, got = (half2.at[o, slot, far, pl.ds(0, 6)], half2.at[o, slot, far, pl.ds(6, 6)]), got2a
        else:
            src, got = (half3.at[o, slot, far, pl.ds(0, 2)], half3.at[o, slot, far, pl.ds(2, 2)]), got3a
        return exchange(o, 2 * phase, slot, src[0], src[1], got)

    def step_b(o, phase, u):
        slot = lax.rem(u, SLOTS)
        a, up, far, down = spots(o, phase)
        if phase == 0:
            src, got = (half.at[o, lax.rem(u, 4), pl.ds(up * 4, 4)], half.at[o, lax.rem(u, 4), pl.ds(down * 4, 4)]), got1b
        elif phase == 1:
            src, got = (half2.at[o, slot, up], half2.at[o, slot, down]), got2b
        else:
            src, got = (half3.at[o, slot, up], half3.at[o, slot, down]), got3b
        return exchange(o, 2 * phase + 1, slot, src[0], src[1], got)

    def add_a(o, phase, u):
        slot = lax.rem(u, SLOTS)
        a, up, far, down = spots(o, phase)
        if phase == 0:
            for i in range(2):
                half[o, lax.rem(u, 4), up * 4 + i] += got1a[o, slot, 0, i]
                half[o, lax.rem(u, 4), down * 4 + 2 + i] += got1a[o, slot, 1, i]
        elif phase == 1:
            half2[o, slot, up, 0:6] += got2a[o, slot, 0]
            half2[o, slot, down, 6:12] += got2a[o, slot, 1]
        else:
            half3[o, slot, up, 0:2] += got3a[o, slot, 0]
            half3[o, slot, down, 2:4] += got3a[o, slot, 1]

    def add_b(o, phase, u):
        slot = lax.rem(u, SLOTS)
        a, up, far, down = spots(o, phase)
        if phase == 0:
            for i in range(4):
                half2[o, slot, i] = half[o, lax.rem(u, 4), a * 4 + i] + got1b[o, slot, 0, i] + got1b[o, slot, 1, i]
        elif phase == 1:
            total = half2[o, slot, a] + got2b[o, slot, 0] + got2b[o, slot, 1]

            @pl.when(lax.rem(u, 6) < 2)
            def _():
                for k in range(4):
                    half3[o, slot, k, 0:3] = total[3 * k : 3 * k + 3]

            @pl.when(lax.rem(u, 6) >= 2)
            def _():
                for ct in range(4):
                    rows24[o, ct] = total[3 * ct : 3 * ct + 3].reshape(24, 128)
                for k in range(4):
                    for ct in range(4):
                        half3[o, slot, k, ct, 0:6, :] = rows24[o, ct, 6 * k : 6 * k + 6, :]
        else:
            out_ref[u, o] = half3[o, slot, a] + got3b[o, slot, 0] + got3b[o, slot, 1]

    def spread_vectors():
        for layer in range(2):
            total = jnp.zeros((128, 128), f32)
            for start, width, keep in VECTORS:
                d = lax.broadcasted_iota(jnp.int32, (128, width), 0) * keep
                q = lax.broadcasted_iota(jnp.int32, (128, width), 1)
                own = jnp.where((q >= d) & (q < d + keep), vectors[layer, :, start : start + width], 0.0)
                high = own.astype(bf16)
                low = (own - high.astype(f32)).astype(bf16)
                lanes = spread[start : start + width, :]
                total += jnp.dot(high, lanes, preferred_element_type=f32)
                total += jnp.dot(low, lanes, preferred_element_type=f32)
            total = total.reshape(4, 4, 8, 128)
            for z in range(4):
                for x in range(4):
                    vec_src[z, x, layer] = total[z, x]

    def vector_copy(k, src, dst, device):
        return pltpu.make_async_remote_copy(
            src_ref=src, dst_ref=dst, send_sem=vec_s.at[k], recv_sem=vec_r.at[k], device_id=device, device_id_type=MESH
        )

    def copies_z():
        return [
            vector_copy(i, vec_src.at[lax.rem(place["z"] + i + 1, 4)], vec_z.at[i], neighbour(place, "z", i + 1))
            for i in range(3)
        ]

    def copies_x():
        return [
            vector_copy(3 + i, vec_src.at[place["z"], lax.rem(place["x"] + i + 1, 4)], vec_x.at[i], neighbour(place, "x", i + 1))
            for i in range(3)
        ]

    def copies_group():
        return [
            vector_copy(6 + i, vec_mid, vec_cy.at[i], in_group(place, flip, step))
            for i, (flip, step) in enumerate(GROUP)
        ]

    def vectors_start():
        tables[1].wait()
        spread_vectors()
        for copy in copies_z():
            copy.start()

    def vectors_second():
        for copy in copies_z():
            copy.wait()
        for x in range(4):
            vec_src[place["z"], x] += vec_z[0, x] + vec_z[1, x] + vec_z[2, x]
        for copy in copies_x():
            copy.start()

    def vectors_third():
        for copy in copies_x():
            copy.wait()
        vec_mid[...] = vec_src[place["z"], place["x"]] + vec_x[0] + vec_x[1] + vec_x[2]
        for copy in copies_group():
            copy.start()

    def vectors_last():
        for copy in copies_group():
            copy.wait()
        total = vec_mid[...]
        for i in range(7):
            total += vec_cy[i]
        mine = lax.broadcasted_iota(jnp.int32, (2, 8, 128), 1) == core * 4 + place["y"]
        vec_out_ref[...] = jnp.sum(jnp.where(mine, total, 0.0), axis=1)

    def when(u, job):
        @pl.when((u >= 0) & (u < TRIPLES))
        def _():
            job(u)

    def tick(now, _):
        t = now - 3

        def enter(u):
            slot = lax.rem(u, SLOTS)
            for o in range(3):
                copy0(o, u).wait()

                def add(i, _):
                    half[o, lax.rem(u, 4), i] += got0[o, lax.rem(u, 2), i]
                    return 0

                lax.fori_loop(0, 16, add, 0)
                for copy in step_a(o, 0, u):
                    copy.start()

        def second(phase):
            def job(u):
                for o in range(3):
                    for copy in step_a(o, phase, u):
                        copy.wait()
                    add_a(o, phase, u)
                    for copy in step_b(o, phase, u):
                        copy.start()
            return job

        def third(phase):
            def job(u):
                for o in range(3):
                    for copy in step_b(o, phase, u):
                        copy.wait()
                    add_b(o, phase, u)
                    if phase < 2:
                        for copy in step_a(o, phase + 1, u):
                            copy.start()
            return job

        when(t + 3, make)
        when(t + 1, second(0))
        when(t, third(0))
        when(t - 1, second(1))
        when(t - 2, third(1))
        when(t - 3, second(2))
        when(t - 4, third(2))

        when(t + 3, enter)
        for k, job in enumerate((vectors_start, vectors_second, vectors_third, vectors_last)):
            pl.when(now == TRIPLES + k)(job)
        return 0

    pl.semaphore_wait(barrier, 13)
    lax.fori_loop(0, TRIPLES + 7, tick, 0)


def finish_kernel(out_ref, vec_ref, loss_ref, dx_ref, *outs):
    loss_out, dx_out, qkv_out, qv_out, mixer_out, bias_out, gain_out, shift_out, up_out, ffn_out, down_out, downbias_out, fingain_out, finshift_out, sem = outs
    copy = pltpu.make_async_copy(dx_ref, dx_out, sem)
    copy.start()
    for layer in range(2):
        first = 6 * (1 - layer)
        for k in range(2):
            for o in range(3):
                for ct in range(3):
                    down_out[layer, 8 * o : 8 * o + 8, 384 * k + 128 * ct : 384 * k + 128 * ct + 128] = out_ref[first + k, o, ct]
                for ct in range(4):
                    at = (k * 3 + o) * 512 + 128 * ct
                    up_out[layer, :, at : at + 128] = out_ref[first + 2 + k, o, ct, 0:6, :]
        for o in range(3):
            for ct in range(4):
                at = o * 768 + 128 * ct
                qkv_out[layer, :, at : at + 128] = out_ref[first + 4, o, ct, 0:6, :]
            for ct in range(2):
                at = o * 768 + 512 + 128 * ct
                qkv_out[layer, :, at : at + 128] = out_ref[first + 5, o, ct, 0:6, :]
                at = o * 256 + 128 * ct
                mixer_out[layer, :, at : at + 128] = out_ref[first + 5, o, 2 + ct, 0:6, :]
    lane = 0
    for (_, _, keep), dst in zip(
        VECTORS, (bias_out, gain_out, shift_out, downbias_out, fingain_out, finshift_out, qv_out, ffn_out)
    ):
        dst[...] = vec_ref[:, lane : lane + keep]
        lane += keep
    rows = lax.broadcasted_iota(jnp.int32, (128, 1), 0)
    for k in range(4):
        loss_out[k] = jnp.sum(jnp.where(rows == lax.axis_index("batch") * 4 + k, loss_ref[...], 0.0))
    copy.wait()


def run_backward(counts, demb, loss, weights, saved):
    triple, _, mixer, _, gain_one, shift_one, expand, _, shrink, _, gain_two, _ = weights
    xb, qkv, ctx, n1, r1, inner, n2, r2 = saved
    tile = (8, 128)
    vmem = pl.BlockSpec(memory_space=pltpu.VMEM)
    smem = pl.BlockSpec(memory_space=pltpu.SMEM)
    hbm = pl.BlockSpec(memory_space=pl.ANY)
    out, vec_out, dx = pl.pallas_call(
        backward_kernel,
        out_shape=(
            jax.ShapeDtypeStruct((TRIPLES, 3, 4) + tile, f32),
            jax.ShapeDtypeStruct((2, 128), f32),
            jax.ShapeDtypeStruct((1, 256, 768), f32),
        ),
        in_specs=[smem] + [vmem] * 4 + [hbm] * 14,
        out_specs=(vmem, vmem, vmem),
        scratch_shapes=[
            pltpu.VMEM((2, 3072, 768), bf16),
            pltpu.VMEM((3, 768, 768), bf16),
            pltpu.VMEM((9216, 128), bf16),
            pltpu.VMEM((256, 768), bf16),
            pltpu.VMEM((256, 2304), bf16),
            pltpu.VMEM((256, 768), bf16),
            pltpu.VMEM((256, 768), f32),
            pltpu.VMEM((256, 1), f32),
            pltpu.VMEM((256, 3072), f32),
            pltpu.VMEM((256, 768), f32),
            pltpu.VMEM((256, 1), f32),
            pltpu.VMEM((3, 2, 1, 768), f32),
            pltpu.VMEM((256, 768), f32),
            pltpu.VMEM((256, 768), bf16),
            pltpu.VMEM((256, 768), bf16),
            pltpu.VMEM((256, 768), bf16),
            pltpu.VMEM((3072, 256), bf16),
            pltpu.VMEM((256, 3072), bf16),
            pltpu.VMEM((256, 2304), bf16),
            pltpu.VMEM((2, 1, 9216), f32),
            pltpu.VMEM((3, 2, 768, 256), bf16),
            pltpu.VMEM((3, 4, 16, 12) + tile, f32),
            pltpu.VMEM((3, 16, 12) + tile, f32),
            pltpu.VMEM((3, 2, 16, 12) + tile, f32),
            pltpu.VMEM((3, SLOTS, 2, 2, 12) + tile, f32),
            pltpu.VMEM((3, SLOTS, 2, 4, 12) + tile, f32),
            pltpu.VMEM((3, SLOTS, 4, 12) + tile, f32),
            pltpu.VMEM((3, SLOTS, 2, 6) + tile, f32),
            pltpu.VMEM((3, SLOTS, 2, 12) + tile, f32),
            pltpu.VMEM((3, SLOTS, 4, 4) + tile, f32),
            pltpu.VMEM((3, SLOTS, 2, 2) + tile, f32),
            pltpu.VMEM((3, SLOTS, 2, 4) + tile, f32),
            pltpu.VMEM((3, 4, 24, 128), f32),
            pltpu.VMEM((4, 4, 2) + tile, f32),
            pltpu.VMEM((3, 4, 2) + tile, f32),
            pltpu.VMEM((3, 2) + tile, f32),
            pltpu.VMEM((2,) + tile, f32),
            pltpu.VMEM((7, 2) + tile, f32),
            pltpu.SemaphoreType.DMA((2, 4)),
            pltpu.SemaphoreType.DMA((8,)),
            pltpu.SemaphoreType.DMA((2,)),
            pltpu.SemaphoreType.DMA((3, 6, 2, SLOTS)),
            pltpu.SemaphoreType.DMA((3, 6, 2, SLOTS)),
            pltpu.SemaphoreType.DMA((3,)),
            pltpu.SemaphoreType.DMA((3, 2)),
            pltpu.SemaphoreType.DMA((13,)),
            pltpu.SemaphoreType.DMA((13,)),
        ],
        compiler_params=pltpu.CompilerParams(
            collective_id=1, has_side_effects=True, vmem_limit_bytes=63 * 1024 * 1024
        ),
    )(
        counts, demb, gain_one, shift_one, gain_two, triple, mixer, expand, shrink,
        xb, qkv, ctx, n1, r1, inner, n2, r2, jnp.asarray(permutations()), jnp.asarray(lane_places()),
    )
    shapes = [(4,), (1, 256, 768), (2, 6, 2304), (2, 12), (2, 6, 768), (2, 6), (2, 6), (2, 6), (2, 6, 3072), (2, 24), (2, 24, 768), (2, 6), (2, 6), (2, 6)]
    return pl.pallas_call(
        finish_kernel,
        out_shape=[jax.ShapeDtypeStruct(s, f32) for s in shapes],
        in_specs=[vmem, vmem, vmem, hbm],
        out_specs=[smem, hbm] + [vmem] * 12,
        scratch_shapes=[pltpu.SemaphoreType.DMA],
        compiler_params=pltpu.CompilerParams(vmem_limit_bytes=32 * 1024 * 1024),
    )(out, vec_out, loss, dx)


def body(
    slot_state_vectors,
    sequence_token_counts,
    positive_companion,
    leading_dimension_counts,
    affinity_divisor,
    triple_projection_matrix,
    probe_payload_shift,
    mixer_projection_matrix,
    mixer_projection_shift,
    mixer_scale_factor,
    mixer_shift_term,
    expand_layer_matrix,
    expand_layer_shift,
    shrink_layer_matrix,
    shrink_layer_shift,
    closing_scale_factor,
    closing_shift_term,
):
    weights = (
        triple_projection_matrix,
        probe_payload_shift,
        mixer_projection_matrix,
        mixer_projection_shift,
        mixer_scale_factor,
        mixer_shift_term,
        expand_layer_matrix,
        expand_layer_shift,
        shrink_layer_matrix,
        shrink_layer_shift,
        closing_scale_factor,
        closing_shift_term,
    )
    averaged_layer_states, saved = run_forward(slot_state_vectors, sequence_token_counts, weights)
    loss, demb = pairing_cost_term(
        averaged_layer_states, positive_companion, leading_dimension_counts, affinity_divisor
    )
    row_losses, *grads = run_backward(sequence_token_counts, demb, loss, weights, saved)
    return (row_losses, averaged_layer_states, *grads)


def solution(mesh):
    return jax.shard_map(
        body,
        mesh=mesh,
        in_specs=(
            P(("batch", "tile"), None, None),
            P(("batch", "tile")),
            P(),
            P(),
            P(),
            P(),
            P(),
            P(),
            P(),
            P(),
            P(),
            P(),
            P(),
            P(),
            P(),
            P(),
            P(),
        ),
        out_specs=(
            P("batch"),
            P(("batch", "tile"), None, None),
            P(("batch", "tile"), None, None),
            P(None, ("batch", "tile"), None),
            P(None, ("batch", "tile")),
            P(None, ("batch", "tile"), None),
            P(None, ("batch", "tile")),
            P(None, ("batch", "tile")),
            P(None, ("batch", "tile")),
            P(None, ("batch", "tile"), None),
            P(None, ("batch", "tile")),
            P(None, ("batch", "tile"), None),
            P(None, ("batch", "tile")),
            P(None, ("batch", "tile")),
            P(None, ("batch", "tile")),
        ),
        check_vma=False,
    )
```

```python
import jax
import jax.numpy as jnp
import ml_dtypes
import numpy as np
from jax import lax
from jax.experimental import pallas as pl
from jax.experimental.pallas import tpu as pltpu
from jax.sharding import PartitionSpec as P

eps_norm = 1e-06

f32, bf16 = jnp.float32, jnp.bfloat16
MESH = pl.DeviceIdType.MESH
TRIPLES = 12
SLOTS = 3
DIRECT = 10
ORDERS = (("x", "y", "z"), ("y", "z", "x"), ("z", "x", "y"))


def my_place():
    b = lax.axis_index("batch")
    return {"z": b // 8, "x": lax.rem(b // 2, 4), "c": lax.rem(b, 2), "y": lax.axis_index("tile")}


def device_at(place):
    return {"batch": (place["z"] * 4 + place["x"]) * 2 + place["c"], "tile": place["y"]}


def neighbour(place, axis, step):
    there = dict(place)
    if axis == "c":
        there["c"] = 1 - place["c"]
    else:
        there[axis] = lax.rem(place[axis] + step + 4, 4)
    return device_at(there)


GROUP = tuple((flip, step) for flip in (0, 1) for step in range(4) if flip or step)
VECTORS = tuple((768 * k, 768, 6) for k in range(6)) + ((4608, 1536, 12), (6144, 3072, 24))


def in_group(place, flip, step):
    there = dict(place)
    there["c"] = lax.rem(place["c"] + flip, 2)
    there["y"] = lax.rem(place["y"] + step, 4)
    return device_at(there)


def gelu_parts(inner):
    half = 0.5 * (1.0 + lax.erf(inner * 0.7071067811865476))
    return inner * half, half


def lanes_of(j, width):
    return pl.ds(pl.multiple_of(j * width, width), width)


def rows_of(i, height):
    return pl.ds(pl.multiple_of(i * height, height), height)


NT = (((1,), (1,)), ((), ()))
TN = (((0,), (0,)), ((), ()))


def head_halves(pair):
    first = lax.broadcasted_iota(jnp.int32, pair.shape, 1) < 64
    nothing = jnp.zeros_like(pair)
    return jnp.concatenate([jnp.where(first, pair, nothing), jnp.where(first, nothing, pair)], axis=0)


def pair_probs(q, k, keymask):
    scores = lax.dot_general(head_halves(q * 0.125), k, NT, preferred_element_type=f32) + keymask
    expo = jnp.exp(scores - jnp.max(scores, axis=1, keepdims=True))
    return expo * (1.0 / jnp.sum(expo, axis=1, keepdims=True))


def whole_kernel(
    count_ref, companion_ref, widths_ref, divisor_ref,
    bq_ref, bo_ref, g1_ref, t1_ref, bu_ref, bd_ref, g2_ref, t2_ref,
    x_ref, wq_ref, wo_ref, wu_ref, wd_ref, perm_ref, spread_ref,
    out_ref, vec_out_ref, loss_ref, emb_ref, dx_ref,
    qkv_keep, ctx_keep, n1_keep, r1_keep, inner_keep, n2_keep, r2_keep,
    weight, perm, xb, qkv, ctx, n1, r1, inner, n2, r2, grad, d_outer, d_att, d_ctx, act_t, d_inner, d_qkv, vectors, apt,
    vq, vo, v1, t1, vu, vd, v2, t2, pool, d_emb, every,
    half, send, got0, got1a, got1b, half2, got2a, got2b, half3, got3a, got3b, rows24, got2d, got3d,
    vec_src, vec_z, vec_x, vec_mid, vec_cy,
    weight_sem, keep_sem, load_sem, table_sem, every_s, every_r, swap_s, swap_r,
    sems_s, sems_r, sem0_s, sem0_r, direct_s, direct_r, vec_s, vec_r,
):
    place = my_place()
    core = place["c"]


    kept = {
        "qkv": (qkv, qkv_keep, 0), "ctx": (ctx, ctx_keep, 1), "n1": (n1, n1_keep, 2), "r1": (r1, r1_keep, 3),
        "inner": (inner, inner_keep, 4), "n2": (n2, n2_keep, 5), "r2": (r2, r2_keep, 6),
    }

    def keep(name):
        here, there, k = kept[name]
        return pltpu.make_async_copy(here, there, keep_sem.at[k])

    def load(name):
        if name == "xb":
            return pltpu.make_async_copy(x_ref.at[0], xb, load_sem.at[7])
        here, there, k = kept[name]
        return pltpu.make_async_copy(there, here, load_sem.at[k])

    def weights(k, layer, slot):
        blocks = []
        for m in range(4):
            cols = pl.ds(768 * m, 768)
            if k == 0:
                src = wd_ref.at[layer, cols]
            elif k == 1:
                src = wu_ref.at[layer, :, cols]
            else:
                src = wq_ref.at[layer, :, cols] if m < 3 else wo_ref.at[layer]
            blocks.append(pltpu.make_async_copy(src, weight.at[slot, cols], weight_sem.at[slot, m]))
        return blocks

    def fetch_weights(k, layer, slot):
        for copy in weights(k, layer, slot):
            copy.start()

    def ready_weights(k, layer, slot):
        for copy in weights(k, layer, slot):
            copy.wait()

    def back_slot(k, layer):
        return lax.rem((1 - layer) * 3 + k + 1, 2)

    load("xb").start()
    fetch_weights(2, 0, 0)
    fetch_weights(1, 0, 1)
    perm_copy = pltpu.make_async_copy(perm_ref, perm, table_sem.at[0])
    spread_copy = pltpu.make_async_copy(spread_ref, weight.at[1, pl.ds(0, 1536)], table_sem.at[1])
    perm_copy.start()

    barrier = pltpu.get_barrier_semaphore()
    for axis in ("x", "z"):
        for step in (1, 2, 3):
            pl.semaphore_signal(barrier, inc=1, device_id=neighbour(place, axis, step), device_id_type=MESH)
    for flip, step in GROUP:
        pl.semaphore_signal(barrier, inc=1, device_id=in_group(place, flip, step), device_id_type=MESH)

    for src, dst in ((bo_ref, vo), (g1_ref, v1), (t1_ref, t1), (bu_ref, vu), (bd_ref, vd), (g2_ref, v2), (t2_ref, t2)):
        for layer in range(2):
            dst[layer] = src[layer : layer + 1, :].astype(f32)
    for layer in range(2):
        vq[layer, :, 0:768] = bq_ref[layer : layer + 1, 0:768].astype(f32)
        vq[layer, :, 768:1536] = jnp.zeros((1, 768), f32)
        vq[layer, :, 1536:2304] = bq_ref[layer : layer + 1, 768:1536].astype(f32)
    count = count_ref[0]
    keymask = jnp.where(lax.broadcasted_iota(jnp.int32, (1, 256), 1) < count, 0.0, -1e9)


    def slab(e, o, phase):
        done = ORDERS[o][:phase]
        at = tuple(pl.ds(0, 4) if axis in done else place[axis] for axis in ("z", "x", "c", "y"))
        return every.at[(e, o) + at]

    def gather_copies(e, o, phase):
        return [
            pltpu.make_async_remote_copy(
                src_ref=slab(e, o, phase), dst_ref=slab(e, o, phase),
                send_sem=every_s.at[e, o, phase, step - 1], recv_sem=every_r.at[e, o, phase, step - 1],
                device_id=neighbour(place, ORDERS[o][phase], step), device_id_type=MESH,
            )
            for step in (1, 2, 3)
        ]

    def swap_copy(e):
        mine = every.at[e, :, :, :, core]
        return pltpu.make_async_remote_copy(
            src_ref=mine, dst_ref=mine, send_sem=swap_s.at[e], recv_sem=swap_r.at[e],
            device_id=neighbour(place, "c", 1), device_id_type=MESH,
        )

    def gather_start(e):
        for o in range(3):
            for r in range(2):
                at = 256 * o + 128 * r
                every[e, o, place["z"], place["x"], core, place["y"], r : r + 1, :] = pool[e, :, at : at + 128]
            for copy in gather_copies(e, o, 0):
                copy.start()

    def gather_next(e, phase):
        for o in range(3):
            for copy in gather_copies(e, o, phase):
                copy.wait()
            if phase < 2:
                for copy in gather_copies(e, o, phase + 1):
                    copy.start()
        if phase == 2:
            swap_copy(e).start()


    def norm(z, layer, normed_ref, scaled_ref, gain, shift, rows):
        center = z - jnp.mean(z, axis=1, keepdims=True)
        scaled = lax.rsqrt(jnp.mean(center * center, axis=1, keepdims=True) + eps_norm)
        normed = center * scaled
        normed_ref[rows, :] = normed
        scaled_ref[rows, :] = scaled
        return normed * gain[layer] + shift[layer]

    def run_if(wanted):
        return (lambda job: job()) if wanted else (lambda job: None)

    def forward_layer(layer):
        is_first, is_last = layer == 0, layer == 1

        def free(*names):
            @run_if(is_last)
            def _():
                for name in names:
                    keep(name).wait()

        def store(*names):
            @run_if(is_first)
            def _():
                for name in names:
                    keep(name).start()

        @run_if(is_first)
        def _():
            load("xb").wait()
            grad[...] = xb[...].astype(f32)

        @run_if(is_last)
        def _():
            xb[...] = grad[...].astype(bf16)

        free("qkv")
        slot = (layer * 3) % 2
        blocks = weights(2, layer, slot)
        for m in range(3):
            cols = pl.ds(768 * m, 768)
            blocks[m].wait()
            mixed = jnp.dot(xb[...], weight[slot, cols, :], preferred_element_type=f32) + vq[layer, :, cols]
            qkv[:, cols] = mixed.astype(bf16)
        store("qkv")

        @run_if(is_last)
        def _():
            gather_next(0, 0)

        free("ctx")

        def attend(pair, _):
            q, k, v = (qkv[:, lanes_of(pair + 6 * third, 128)] for third in range(3))
            probs = pair_probs(q, k, keymask).astype(bf16)
            both = jnp.dot(probs, v, preferred_element_type=f32)
            first = lax.broadcasted_iota(jnp.int32, (256, 128), 1) < 64
            ctx[:, lanes_of(pair, 128)] = jnp.where(first, both[:256], both[256:]).astype(bf16)
            return 0

        lax.fori_loop(0, 6, attend, 0, unroll=6)
        store("ctx")

        @run_if(is_last)
        def _():
            gather_next(0, 1)

        blocks[3].wait()
        grad[...] += jnp.dot(ctx[...], weight[slot, 2304:3072, :], preferred_element_type=f32) + vo[layer]
        fetch_weights(0, layer, slot)
        free("n1", "r1", "n2", "r2")

        def norm_one(i, _):
            rows = rows_of(i, 64)
            mid = norm(grad[rows, :], layer, n1, r1, v1, t1, rows)
            n2[rows, :] = mid
            d_att[rows, :] = mid.astype(bf16)
            return 0

        lax.fori_loop(0, 4, norm_one, 0, unroll=4)
        store("n1", "r1")
        free("inner")
        slot = (layer * 3 + 1) % 2
        blocks = weights(1, layer, slot)
        for m in range(4):
            cols = pl.ds(768 * m, 768)
            blocks[m].wait()
            value = jnp.dot(d_att[...], weight[slot, cols, :], preferred_element_type=f32) + vu[layer, :, cols]
            inner[:, cols] = value
            d_inner[:, cols] = gelu_parts(value)[0].astype(bf16)
        store("inner")

        @run_if(is_first)
        def _():
            fetch_weights(2, 1, slot)

        @run_if(is_last)
        def _():
            gather_next(0, 2)

        slot = (layer * 3 + 2) % 2
        ready_weights(0, layer, slot)
        n2[...] += jnp.dot(d_inner[...], weight[slot], preferred_element_type=f32) + vd[layer]

        @run_if(is_first)
        def _():
            fetch_weights(1, 1, slot)

        def norm_two(i, total):
            rows = rows_of(i, 64)
            result = norm(n2[rows, :], layer, n2, r2, v2, t2, rows)
            grad[rows, :] = result
            spot = lax.broadcasted_iota(jnp.int32, (64, 1), 0) + i * 64
            return total + jnp.sum(jnp.where(spot < count, result, 0.0), axis=0, keepdims=True)

        total = lax.fori_loop(0, 4, norm_two, jnp.zeros((1, 768), f32), unroll=4)
        pool[layer] = total / count.astype(f32)
        store("n2", "r2")

        @run_if(is_first)
        def _():
            pl.semaphore_wait(barrier, 13)
            gather_start(0)

        @run_if(is_last)
        def _():
            swap_copy(0).wait()
            gather_start(1)


    def pairing(e, loss):
        me = ((place["z"] * 4 + place["x"]) * 2 + core) * 4 + place["y"]
        row = lax.broadcasted_iota(jnp.int32, (128, 128), 0)
        col = lax.broadcasted_iota(jnp.int32, (128, 128), 1)
        rows = lax.broadcasted_iota(jnp.int32, (128, 1), 0)
        lane = lax.broadcasted_iota(jnp.int32, (1, 768), 1)
        companion = companion_ref[...]
        divisor = divisor_ref[0]
        partner = (row == companion).astype(f32)
        mine = jnp.sum(jnp.where(lax.broadcasted_iota(jnp.int32, (1, 128), 1) == me, companion, 0), axis=1, keepdims=True)
        chosen = (rows == mine).astype(f32)
        is_me = rows == me
        embed = jnp.concatenate(
            [every[e, o].reshape(128, 2, 128)[:, r, :] for o in range(3) for r in range(2)], axis=1
        )
        high = embed.astype(bf16)
        low = (embed - high.astype(f32)).astype(bf16)
        own = pool[e]
        total = jnp.zeros((1, 768), f32)
        for p in range(4):
            keep_p = (lane < widths_ref[p]).astype(f32)
            keep_low = keep_p.astype(bf16)
            high_p, low_p = high * keep_low, low * keep_low
            gram = (
                lax.dot_general(high_p, high, NT, preferred_element_type=f32)
                + lax.dot_general(high_p, low, NT, preferred_element_type=f32)
                + lax.dot_general(low_p, high, NT, preferred_element_type=f32)
            )
            diagonal = jnp.where(row == col, gram, 0.0)
            inverse = lax.rsqrt(jnp.sum(diagonal, axis=1, keepdims=True) + eps_norm)
            inverse_row = lax.rsqrt(jnp.sum(diagonal, axis=0, keepdims=True) + eps_norm)
            sims = gram * inverse * inverse_row / divisor
            sims = jnp.where(row == col, -1e30, sims)
            top = jnp.max(sims, axis=1, keepdims=True)
            lse = top + jnp.log(jnp.sum(jnp.exp(sims - top), axis=1, keepdims=True))
            loss = loss + (lse - jnp.sum(sims * partner, axis=1, keepdims=True))
            to_me = jnp.sum(jnp.where(col == me, sims, 0.0), axis=1, keepdims=True)
            lse_me = jnp.sum(jnp.where(is_me, lse, 0.0), axis=0, keepdims=True)
            weight_j = jnp.exp(to_me - lse_me) + jnp.exp(to_me - lse) - 2.0 * chosen
            dunit = jnp.sum(embed * (weight_j * inverse), axis=0, keepdims=True) * keep_p
            inverse_me = jnp.sum(jnp.where(is_me, inverse, 0.0), axis=0, keepdims=True)
            unit_me = own * keep_p * inverse_me
            inside = dunit - unit_me * jnp.sum(unit_me * dunit, axis=1, keepdims=True)
            total = total + inside * inverse_me
        d_emb[e] = total / (8.0 * divisor)
        return loss


    def norm_back(normed, scaled, gain, rounded, at_gain, at_shift, at_bias, layer):
        sums = [jnp.zeros((1, 768), f32) for _ in range(3)]
        for i in range(4):
            rows = pl.ds(64 * i, 64)
            dy, n = grad[rows, :], normed[rows, :]
            dn = dy * gain
            inside = dn - jnp.mean(dn, axis=1, keepdims=True) - n * jnp.mean(dn * n, axis=1, keepdims=True)
            dz = scaled[rows, :] * inside
            low = dz.astype(bf16)
            grad[rows, :] = dz
            rounded[rows, :] = low
            for k, term in enumerate((dy * n, dy, low.astype(f32))):
                sums[k] = sums[k] + jnp.sum(term, axis=0, keepdims=True)
        for at, total in zip((at_gain, at_shift, at_bias), sums):
            vectors[layer, :, at : at + 768] = total

    def turn_active():
        def turn(j, _):
            value = inner[:, lanes_of(j, 256)]
            act_t[lanes_of(j, 256), :] = gelu_parts(value)[0].T.astype(bf16)
            return 0

        lax.fori_loop(0, 12, turn, 0, unroll=2)

    def permute(operand, which):
        for o in range(3):
            apt[o, which] = lax.dot_general(perm[o], operand, NT, preferred_element_type=f32).astype(bf16)

    def begin_layer(layer):
        spots = lax.broadcasted_iota(jnp.int32, (256, 1), 0)
        pooled = jnp.where(spots < count, 1.0, 0.0) / count.astype(f32)

        @pl.when(layer == 1)
        def _():
            grad[...] = pooled * d_emb[1]

        @pl.when(layer == 0)
        def _():
            grad[...] += pooled * d_emb[0]
            load("n2").wait()
            load("r2").wait()
            load("inner").wait()
            turn_active()

        norm_back(n2, r2, v2[layer], d_outer, 3072, 3840, 2304, layer)

        @pl.when(layer == 1)
        def _():
            load("n2").start()
            load("r2").start()

    def through_expand(layer):
        slot = back_slot(0, layer)

        @pl.when(layer == 0)
        def _():
            ready_weights(0, 0, slot)

        def chunk(j, _):
            cols = lanes_of(j, 512)
            d_act = lax.dot_general(d_outer[...], weight[slot, cols, :], NT, preferred_element_type=f32)
            value = inner[:, cols]
            slope = gelu_parts(value)[1] + value * (jnp.exp(-0.5 * value * value) * 0.3989422804014327)
            low = (d_act * slope).astype(bf16)
            d_inner[:, cols] = low
            at = pl.ds(pl.multiple_of(6144 + j * 512, 512), 512)
            vectors[layer, :, at] = jnp.sum(low.astype(f32), axis=0, keepdims=True)
            return 0

        lax.fori_loop(0, 6, chunk, 0, unroll=2)
        fetch_weights(2, layer, slot)

        @pl.when(layer == 1)
        def _():
            load("inner").start()

        @pl.when(layer == 0)
        def _():
            load("n1").wait()
            load("r1").wait()
            permute((n1[...] * v1[0] + t1[0]).astype(bf16), 0)

    def through_mixer(layer):
        slot = back_slot(1, layer)

        @pl.when(layer == 0)
        def _():
            ready_weights(1, 0, slot)

        for m in range(4):
            cols = pl.ds(768 * m, 768)
            grad[...] += lax.dot_general(d_inner[:, cols], weight[slot, cols, :], NT, preferred_element_type=f32)
        norm_back(n1, r1, v1[layer], d_att, 768, 1536, 0, layer)

        @pl.when(layer == 1)
        def _():
            fetch_weights(0, 0, slot)
            load("n1").start()
            load("r1").start()

        slot = back_slot(2, layer)
        ready_weights(2, layer, slot)
        d_ctx[...] = lax.dot_general(d_att[...], weight[slot, 2304:3072, :], NT, preferred_element_type=f32).astype(bf16)

    def through_attention(layer, first_pair, pairs):
        def pair_back(i, _):
            pair = first_pair + i
            at = [lanes_of(pair + 6 * third, 128) for third in range(3)]
            q, k, v = (qkv[:, cols] for cols in at)
            probs = pair_probs(q, k, keymask)
            dc = head_halves(d_ctx[:, at[0]])
            dp = lax.dot_general(dc, v, NT, preferred_element_type=f32)
            ds = (probs * (dp - jnp.sum(dp * probs, axis=1, keepdims=True))).astype(bf16)
            dq = jnp.dot(
                jnp.concatenate([ds[:256], ds[256:]], axis=1), head_halves(k * 0.125), preferred_element_type=f32
            ).astype(bf16)
            dk = lax.dot_general(ds, head_halves(q * 0.125), TN, preferred_element_type=f32).astype(bf16)
            dv = lax.dot_general(probs.astype(bf16), dc, TN, preferred_element_type=f32).astype(bf16)
            for cols, value in zip(at, (dq, dk, dv)):
                d_qkv[:, cols] = value
            for start, value in ((4608, dq), (5376, dv)):
                where = pl.ds(pl.multiple_of(start + pair * 128, 128), 128)
                vectors[layer, :, where] = jnp.sum(value.astype(f32), axis=0, keepdims=True)
            return 0

        lax.fori_loop(0, pairs, pair_back, 0, unroll=2)

    def through_projection(layer):
        slot = back_slot(2, layer)
        for m in range(3):
            cols = pl.ds(768 * m, 768)
            grad[...] += lax.dot_general(d_qkv[:, cols], weight[slot, cols, :], NT, preferred_element_type=f32)

        @pl.when(layer == 1)
        def _():
            fetch_weights(1, 0, slot)
            load("qkv").start()

        @pl.when(layer == 0)
        def _():
            dx_copy.start()

    dx_copy = pltpu.make_async_copy(grad, dx_ref.at[0], table_sem.at[2])

    def store_rows(o, slot, mine, tile0, value):
        for j in range(value.shape[1] // 128):
            part = value[:, 128 * j : 128 * (j + 1)].reshape(16, 3, 8, 128)
            if mine:
                half[o, slot, :, tile0 + 3 * j : tile0 + 3 * j + 3] = part
            else:
                send[o, :, tile0 + 3 * j : tile0 + 3 * j + 3] = part

    def product(o, slot, which, ref, at, width, tile0):
        for mine in (False, True):
            c = core if mine else 1 - core
            lhs = apt[o, which, pl.ds(pl.multiple_of(c * 384, 128), 384), :]
            for w in range(0, width, 256):
                value = jnp.dot(lhs, ref[:, at + w : at + w + 256], preferred_element_type=f32)
                store_rows(o, slot, mine, tile0 + 3 * (w // 128), value)

    def product_shrink(slot, k):
        def block(z, _):
            for mine in (False, True):
                c = core if mine else 1 - core
                lhs = jnp.concatenate(
                    [act_t[pl.ds(pl.multiple_of(z * 768 + x * 192 + c * 96, 32), 96), :] for x in range(4)], axis=0
                )
                value = jnp.dot(lhs, d_outer[:, 384 * k : 384 * (k + 1)], preferred_element_type=f32)
                for x in range(4):
                    for y in range(4):
                        for j in range(3):
                            p = {"x": x, "y": y, "z": z}
                            d1, d2, d3 = (p[axis] for axis in ORDERS[j])
                            row = x * 96 + (y * 3 + j) * 8
                            for ct in range(3):
                                tile = value[row : row + 8, 128 * ct : 128 * ct + 128]
                                if mine:
                                    half[j, slot, d1 * 4 + d2, d3 * 3 + ct] = tile
                                else:
                                    send[j, d1 * 4 + d2, d3 * 3 + ct] = tile
            return 0

        lax.fori_loop(0, 4, block, 0)

    def make(u):
        slot = lax.rem(u, SLOTS)
        layer = 1 - u // 6
        kind = lax.rem(u, 6)

        def to_other_core(o):
            copy0(o, u).start()

        @pl.when(kind == 0)
        def _():
            begin_layer(layer)
            product_shrink(slot, 0)
            for o in range(3):
                to_other_core(o)

        @pl.when(kind == 1)
        def _():
            product_shrink(slot, 1)
            for o in range(3):
                to_other_core(o)

        for k in range(2):
            @pl.when(kind == 2 + k)
            def _():
                for o in range(3):
                    product(o, slot, 0, d_inner, (k * 3 + o) * 512, 512, 0)
                    to_other_core(o)

        @pl.when(kind == 4)
        def _():
            for o in range(3):
                product(o, slot, 0, d_qkv, o * 768, 512, 0)
                to_other_core(o)

        @pl.when(kind == 5)
        def _():
            for o in range(3):
                product(o, slot, 0, d_qkv, o * 768 + 512, 256, 0)
                product(o, slot, 1, d_att, o * 256, 256, 6)
                to_other_core(o)

    def follow(u):
        layer = 1 - u // 6
        kind = lax.rem(u, 6)

        @pl.when(kind == 1)
        def _():
            through_expand(layer)

        @pl.when(kind == 2)
        def _():
            through_mixer(layer)

        @pl.when(kind == 3)
        def _():
            @pl.when(layer == 0)
            def _():
                load("xb").wait()
                load("ctx").wait()

            permute(xb[...], 0)
            permute(ctx[...], 1)

            @pl.when(layer == 1)
            def _():
                load("xb").start()
                load("ctx").start()

            @pl.when(layer == 0)
            def _():
                load("qkv").wait()

            through_attention(layer, 0, 4)

        @pl.when(kind == 4)
        def _():
            through_attention(layer, 4, 2)
            through_projection(layer)


    def exchange(o, k, slot, src_up, src_down, got):
        axis = ORDERS[o][k // 2]
        return [
            pltpu.make_async_remote_copy(
                src_ref=src, dst_ref=got.at[o, slot, way],
                send_sem=sems_s.at[o, k, way, slot], recv_sem=sems_r.at[o, k, way, slot],
                device_id=neighbour(place, axis, step), device_id_type=MESH,
            )
            for way, (src, step) in enumerate(((src_up, 1), (src_down, -1)))
        ]

    def spots(o, phase):
        a = place[ORDERS[o][phase]]
        return a, lax.rem(a + 1, 4), lax.rem(a + 2, 4), lax.rem(a + 3, 4)

    def copy0(o, u):
        slot = lax.rem(u, 2)
        return pltpu.make_async_remote_copy(
            src_ref=send.at[o], dst_ref=got0.at[o, slot], send_sem=sem0_s.at[o], recv_sem=sem0_r.at[o, slot],
            device_id=neighbour(place, "c", 1), device_id_type=MESH,
        )

    def step_a(o, phase, u):
        slot = lax.rem(u, SLOTS)
        a, up, far, down = spots(o, phase)
        if phase == 0:
            src, got = (half.at[o, slot, pl.ds(far * 4, 2)], half.at[o, slot, pl.ds(far * 4 + 2, 2)]), got1a
        elif phase == 1:
            src, got = (half2.at[o, slot, far, pl.ds(0, 6)], half2.at[o, slot, far, pl.ds(6, 6)]), got2a
        else:
            src, got = (half3.at[o, slot, far, pl.ds(0, 2)], half3.at[o, slot, far, pl.ds(2, 2)]), got3a
        return exchange(o, 2 * phase, slot, src[0], src[1], got)

    def step_b(o, phase, u):
        slot = lax.rem(u, SLOTS)
        a, up, far, down = spots(o, phase)
        if phase == 0:
            src, got = (half.at[o, slot, pl.ds(up * 4, 4)], half.at[o, slot, pl.ds(down * 4, 4)]), got1b
        elif phase == 1:
            src, got = (half2.at[o, slot, up], half2.at[o, slot, down]), got2b
        else:
            src, got = (half3.at[o, slot, up], half3.at[o, slot, down]), got3b
        return exchange(o, 2 * phase + 1, slot, src[0], src[1], got)

    def add_a(o, phase, u):
        slot = lax.rem(u, SLOTS)
        a, up, far, down = spots(o, phase)
        if phase == 0:
            for i in range(2):
                half[o, slot, up * 4 + i] += got1a[o, slot, 0, i]
                half[o, slot, down * 4 + 2 + i] += got1a[o, slot, 1, i]
        elif phase == 1:
            half2[o, slot, up, 0:6] += got2a[o, slot, 0]
            half2[o, slot, down, 6:12] += got2a[o, slot, 1]
        else:
            half3[o, slot, up, 0:2] += got3a[o, slot, 0]
            half3[o, slot, down, 2:4] += got3a[o, slot, 1]

    def add_b(o, phase, u):
        slot = lax.rem(u, SLOTS)
        a, up, far, down = spots(o, phase)
        if phase == 0:
            for i in range(4):
                half2[o, slot, i] = half[o, slot, a * 4 + i] + got1b[o, slot, 0, i] + got1b[o, slot, 1, i]
        elif phase == 1:
            to_third(o, slot, u, half2[o, slot, a] + got2b[o, slot, 0] + got2b[o, slot, 1])
        else:
            out_ref[u, o] = half3[o, slot, a] + got3b[o, slot, 0] + got3b[o, slot, 1]

    def to_third(o, slot, u, total):
        @pl.when(lax.rem(u, 6) < 2)
        def _():
            for k in range(4):
                half3[o, slot, k, 0:3] = total[3 * k : 3 * k + 3]

        @pl.when(lax.rem(u, 6) >= 2)
        def _():
            for ct in range(4):
                rows24[o, ct] = total[3 * ct : 3 * ct + 3].reshape(24, 128)
            for k in range(4):
                for ct in range(4):
                    half3[o, slot, k, ct, 0:6, :] = rows24[o, ct, 6 * k : 6 * k + 6, :]

    def direct(o, phase, u):
        slot, way = lax.rem(u, SLOTS), lax.rem(u, 2)
        a = place[ORDERS[o][phase]]
        src, got = ((half2, got2d), (half3, got3d))[phase - 1]
        return [
            pltpu.make_async_remote_copy(
                src_ref=src.at[o, slot, lax.rem(a + step, 4)], dst_ref=got.at[o, way, step - 1],
                send_sem=direct_s.at[o, phase - 1, way, step - 1], recv_sem=direct_r.at[o, phase - 1, way, step - 1],
                device_id=neighbour(place, ORDERS[o][phase], step), device_id_type=MESH,
            )
            for step in (1, 2, 3)
        ]

    def direct_second(u):
        slot, way = lax.rem(u, SLOTS), lax.rem(u, 2)
        for o in range(3):
            for copy in direct(o, 1, u):
                copy.wait()
            total = half2[o, slot, place[ORDERS[o][1]]]
            for i in range(3):
                total += got2d[o, way, i]
            to_third(o, slot, u, total)
            for copy in direct(o, 2, u):
                copy.start()

    def direct_third(u):
        slot, way = lax.rem(u, SLOTS), lax.rem(u, 2)
        for o in range(3):
            for copy in direct(o, 2, u):
                copy.wait()
            total = half3[o, slot, place[ORDERS[o][2]]]
            for i in range(3):
                total += got3d[o, way, i]
            out_ref[u, o] = total

    def spread_vectors():
        for layer in range(2):
            total = jnp.zeros((128, 128), f32)
            for start, width, keep in VECTORS:
                d = lax.broadcasted_iota(jnp.int32, (128, width), 0) * keep
                q = lax.broadcasted_iota(jnp.int32, (128, width), 1)
                own = jnp.where((q >= d) & (q < d + keep), vectors[layer, :, start : start + width], 0.0)
                high = own.astype(bf16)
                low = (own - high.astype(f32)).astype(bf16)
                for part in range(width // 768):
                    k = start // 768 + part
                    lanes = weight[1, 768 * (k // 6) : 768 * (k // 6 + 1), 128 * (k % 6) : 128 * (k % 6 + 1)]
                    at = slice(768 * part, 768 * (part + 1))
                    total += jnp.dot(high[:, at], lanes, preferred_element_type=f32)
                    total += jnp.dot(low[:, at], lanes, preferred_element_type=f32)
            total = total.reshape(4, 4, 8, 128)
            for z in range(4):
                for x in range(4):
                    vec_src[z, x, layer] = total[z, x]

    def vector_copy(k, src, dst, device):
        return pltpu.make_async_remote_copy(
            src_ref=src, dst_ref=dst, send_sem=vec_s.at[k], recv_sem=vec_r.at[k], device_id=device, device_id_type=MESH
        )

    def copies_z():
        return [
            vector_copy(i, vec_src.at[lax.rem(place["z"] + i + 1, 4)], vec_z.at[i], neighbour(place, "z", i + 1))
            for i in range(3)
        ]

    def copies_x():
        return [
            vector_copy(3 + i, vec_src.at[place["z"], lax.rem(place["x"] + i + 1, 4)], vec_x.at[i], neighbour(place, "x", i + 1))
            for i in range(3)
        ]

    def copies_group():
        return [
            vector_copy(6 + i, vec_mid, vec_cy.at[i], in_group(place, flip, step))
            for i, (flip, step) in enumerate(GROUP)
        ]

    def vectors_start():
        spread_copy.wait()
        spread_vectors()
        for copy in copies_z():
            copy.start()

    def vectors_second():
        for copy in copies_z():
            copy.wait()
        for x in range(4):
            vec_src[place["z"], x] += vec_z[0, x] + vec_z[1, x] + vec_z[2, x]
        for copy in copies_x():
            copy.start()

    def vectors_third():
        for copy in copies_x():
            copy.wait()
        vec_mid[...] = vec_src[place["z"], place["x"]] + vec_x[0] + vec_x[1] + vec_x[2]
        for copy in copies_group():
            copy.start()

    def vectors_last():
        for copy in copies_group():
            copy.wait()
        total = vec_mid[...]
        for i in range(7):
            total += vec_cy[i]
        mine = lax.broadcasted_iota(jnp.int32, (2, 8, 128), 1) == core * 4 + place["y"]
        vec_out_ref[...] = jnp.sum(jnp.where(mine, total, 0.0), axis=1)

    def when(u, first, last, job):
        @pl.when((u >= first) & (u < last))
        def _():
            job(u)

    def enter(u):
        slot = lax.rem(u, SLOTS)
        for o in range(3):
            copy0(o, u).wait()

            def add(i, _):
                half[o, slot, i] += got0[o, lax.rem(u, 2), i]
                return 0

            lax.fori_loop(0, 16, add, 0)
            for copy in step_a(o, 0, u):
                copy.start()

    def second(phase):
        def job(u):
            for o in range(3):
                for copy in step_a(o, phase, u):
                    copy.wait()
                add_a(o, phase, u)
                for copy in step_b(o, phase, u):
                    copy.start()
        return job

    def third(phase):
        def job(u):
            for o in range(3):
                for copy in step_b(o, phase, u):
                    copy.wait()
                add_b(o, phase, u)
                if phase == 0:
                    @pl.when(u < DIRECT)
                    def _():
                        for copy in step_a(o, 1, u):
                            copy.start()

                    @pl.when(u >= DIRECT)
                    def _():
                        for copy in direct(o, 1, u):
                            copy.start()
                elif phase == 1:
                    for copy in step_a(o, 2, u):
                        copy.start()
        return job

    def tick(u, _):
        when(u, 0, TRIPLES, make)
        when(u - 1, 0, TRIPLES, second(0))
        when(u - 2, 0, TRIPLES, third(0))
        when(u - 3, 0, DIRECT, second(1))
        when(u - 6, 0, DIRECT, third(2))
        when(u - 3, DIRECT, TRIPLES, direct_second)
        when(u - 4, 0, DIRECT, third(1))
        when(u - 4, DIRECT, TRIPLES, direct_third)
        when(u - 5, 0, DIRECT, second(2))
        when(u, 0, TRIPLES, enter)
        when(u, 0, TRIPLES, follow)

        @pl.when(u == TRIPLES - 1)
        def _():
            spread_copy.start()

        for k, job in enumerate((vectors_start, vectors_second, vectors_third, vectors_last)):
            pl.when(u == TRIPLES + k)(job)
        return 0


    forward_layer(0)
    forward_layer(1)
    for layer in range(2):
        emb_ref[0, layer : layer + 1, :] = pool[layer]
    half3[...] = jnp.zeros_like(half3)
    loss = pairing(0, jnp.zeros((128, 1), f32))
    gather_next(1, 0)
    turn_active()
    gather_next(1, 1)
    perm_copy.wait()
    permute(d_att[...], 0)
    gather_next(1, 2)
    swap_copy(1).wait()
    loss = pairing(1, loss)
    loss_ref[...] = loss / 8.0
    lax.fori_loop(0, DIRECT + 6, tick, 0)
    dx_copy.wait()


def permutations():
    rows = np.arange(768).reshape(4, 4, 2, 4, 6)
    names = {"z": 0, "x": 1, "c": 2, "y": 3}
    out = np.zeros((3, 768, 768), np.float32)
    for o, (d1, d2, d3) in enumerate(ORDERS):
        taken = rows.transpose(2, names[d1], names[d2], names[d3], 4).reshape(-1)
        out[o, np.arange(768), taken] = 1
    return out.astype(ml_dtypes.bfloat16)


def lane_places():
    out = np.zeros((9216, 128), np.float32)
    lane = 0
    for start, width, keep in VECTORS:
        q = np.arange(width)
        out[start + q, lane + q % keep] = 1
        lane += keep
    out = out.reshape(2, 6, 768, 128).transpose(0, 2, 1, 3).reshape(1536, 768)
    return out.astype(ml_dtypes.bfloat16)


def finish_kernel(out_hbm, vec_hbm, loss_hbm, dx_hbm, *refs):
    loss_out, dx_out, qkv_out, qv_out, mixer_out, bias_out, gain_out, shift_out, up_out, ffn_out, down_out, downbias_out, fingain_out, finshift_out = refs[:14]
    out_ref, vec_ref, loss_ref, sem = refs[14:]
    copies = [
        pltpu.make_async_copy(src, dst, sem.at[k])
        for k, (src, dst) in enumerate(((out_hbm, out_ref), (vec_hbm, vec_ref), (loss_hbm, loss_ref), (dx_hbm, dx_out)))
    ]
    for copy in copies:
        copy.start()
    for copy in copies[:3]:
        copy.wait()
    for layer in range(2):
        first = 6 * (1 - layer)
        for k in range(2):
            for o in range(3):
                for ct in range(3):
                    down_out[layer, 8 * o : 8 * o + 8, 384 * k + 128 * ct : 384 * k + 128 * ct + 128] = out_ref[first + k, o, ct]
                for ct in range(4):
                    at = (k * 3 + o) * 512 + 128 * ct
                    up_out[:, layer, at : at + 128] = out_ref[first + 2 + k, o, ct, 0:6, :]
        for o in range(3):
            for ct in range(4):
                at = o * 768 + 128 * ct
                qkv_out[:, layer, at : at + 128] = out_ref[first + 4, o, ct, 0:6, :]
            for ct in range(2):
                at = o * 768 + 512 + 128 * ct
                qkv_out[:, layer, at : at + 128] = out_ref[first + 5, o, ct, 0:6, :]
                at = o * 256 + 128 * ct
                mixer_out[:, layer, at : at + 128] = out_ref[first + 5, o, 2 + ct, 0:6, :]
    lane = 0
    for (_, _, keep), dst in zip(
        VECTORS, (bias_out, gain_out, shift_out, downbias_out, fingain_out, finshift_out, qv_out, ffn_out)
    ):
        dst[...] = vec_ref[:, lane : lane + keep]
        lane += keep
    rows = lax.broadcasted_iota(jnp.int32, (128, 1), 0)
    for k in range(4):
        loss_out[k] = jnp.sum(jnp.where(rows == lax.axis_index("batch") * 4 + k, loss_ref[...], 0.0))
    copies[3].wait()


def body(slots, counts, companion, widths, divisor, triple, bias_qv, mixer, bias_mixer, gain_one, shift_one, expand, bias_expand, shrink, bias_shrink, gain_two, shift_two):
    tile = (8, 128)
    vmem = pl.BlockSpec(memory_space=pltpu.VMEM)
    smem = pl.BlockSpec(memory_space=pltpu.SMEM)
    hbm = pl.BlockSpec(memory_space=pl.ANY)

    def vm(*shape, dtype=f32):
        return pltpu.VMEM(shape, dtype)

    dma = pltpu.SemaphoreType.DMA
    saved = [((256, 2304), bf16), ((256, 768), bf16), ((256, 768), f32), ((256, 1), f32), ((256, 3072), f32), ((256, 768), f32), ((256, 1), f32)]
    shapes = [((TRIPLES, 3, 4) + tile, f32), ((2, 128), f32), ((128, 1), f32), ((1, 2, 768), f32), ((1, 256, 768), f32)] + saved
    results = pl.pallas_call(
        whole_kernel,
        out_shape=[jax.ShapeDtypeStruct(s, t) for s, t in shapes],
        in_specs=[smem, vmem, smem, smem] + [vmem] * 8 + [hbm] * 7,
        out_specs=[vmem] * 4 + [hbm] * 8,
        scratch_shapes=[
            vm(2, 3072, 768, dtype=bf16), vm(3, 768, 768, dtype=bf16), vm(256, 768, dtype=bf16), vm(256, 2304, dtype=bf16),
            vm(256, 768, dtype=bf16), vm(256, 768), vm(256, 1), vm(256, 3072), vm(256, 768), vm(256, 1), vm(256, 768),
            vm(256, 768, dtype=bf16), vm(256, 768, dtype=bf16), vm(256, 768, dtype=bf16), vm(3072, 256, dtype=bf16),
            vm(256, 3072, dtype=bf16), vm(256, 2304, dtype=bf16), vm(2, 1, 9216), vm(3, 2, 768, 256, dtype=bf16),
            vm(2, 1, 2304), vm(2, 1, 768), vm(2, 1, 768), vm(2, 1, 768), vm(2, 1, 3072), vm(2, 1, 768), vm(2, 1, 768), vm(2, 1, 768),
            vm(2, 1, 768), vm(2, 1, 768), vm(2, 3, 4, 4, 2, 4, 2, 128),
            vm(3, SLOTS, 16, 12, *tile), vm(3, 16, 12, *tile), vm(3, 2, 16, 12, *tile),
            vm(3, SLOTS, 2, 2, 12, *tile), vm(3, SLOTS, 2, 4, 12, *tile),
            vm(3, SLOTS, 4, 12, *tile), vm(3, SLOTS, 2, 6, *tile), vm(3, SLOTS, 2, 12, *tile),
            vm(3, SLOTS, 4, 4, *tile), vm(3, SLOTS, 2, 2, *tile), vm(3, SLOTS, 2, 4, *tile), vm(3, 4, 24, 128),
            vm(3, 2, 3, 12, *tile), vm(3, 2, 3, 4, *tile),
            vm(4, 4, 2, *tile), vm(3, 4, 2, *tile), vm(3, 2, *tile), vm(2, *tile), vm(7, 2, *tile),
            dma((2, 4)), dma((7,)), dma((8,)), dma((3,)), dma((2, 3, 3, 3)), dma((2, 3, 3, 3)), dma((2,)), dma((2,)),
            dma((3, 6, 2, SLOTS)), dma((3, 6, 2, SLOTS)), dma((3,)), dma((3, 2)), dma((3, 2, 2, 3)), dma((3, 2, 2, 3)),
            dma((13,)), dma((13,)),
        ],
        compiler_params=pltpu.CompilerParams(
            collective_id=1, has_side_effects=True, vmem_limit_bytes=63 * 1024 * 1024
        ),
    )(
        counts, companion[None], widths, divisor,
        bias_qv, bias_mixer, gain_one, shift_one, bias_expand, bias_shrink, gain_two, shift_two,
        slots, triple, mixer, expand, shrink, jnp.asarray(permutations()), jnp.asarray(lane_places()),
    )
    out, vec_out, loss, embeddings, dx = results[:5]
    shapes = [(4,), (1, 256, 768), (6, 2, 2304), (2, 12), (6, 2, 768), (2, 6), (2, 6), (2, 6), (6, 2, 3072), (2, 24), (2, 24, 768), (2, 6), (2, 6), (2, 6)]
    loss, *rest = pl.pallas_call(
        finish_kernel,
        out_shape=[jax.ShapeDtypeStruct(s, f32) for s in shapes],
        in_specs=[hbm] * 4,
        out_specs=[smem, hbm] + [vmem] * 12,
        scratch_shapes=[vm(TRIPLES, 3, 4, *tile), vm(2, 128), vm(128, 1), dma((4,))],
        compiler_params=pltpu.CompilerParams(vmem_limit_bytes=32 * 1024 * 1024),
    )(out, vec_out, loss, dx)
    rest = [r.transpose(1, 0, 2) if r.shape[:2] == (6, 2) else r for r in rest]
    return (loss, embeddings, *rest)


def solution(mesh):
    return jax.shard_map(
        body,
        mesh=mesh,
        in_specs=(
            P(("batch", "tile"), None, None),
            P(("batch", "tile")),
            P(),
            P(),
            P(),
            P(),
            P(),
            P(),
            P(),
            P(),
            P(),
            P(),
            P(),
            P(),
            P(),
            P(),
            P(),
        ),
        out_specs=(
            P("batch"),
            P(("batch", "tile"), None, None),
            P(("batch", "tile"), None, None),
            P(None, ("batch", "tile"), None),
            P(None, ("batch", "tile")),
            P(None, ("batch", "tile"), None),
            P(None, ("batch", "tile")),
            P(None, ("batch", "tile")),
            P(None, ("batch", "tile")),
            P(None, ("batch", "tile"), None),
            P(None, ("batch", "tile")),
            P(None, ("batch", "tile"), None),
            P(None, ("batch", "tile")),
            P(None, ("batch", "tile")),
            P(None, ("batch", "tile")),
        ),
        check_vma=False,
    )
```

```python
import jax
import jax.numpy as jnp
import ml_dtypes
import numpy as np
from jax import lax
from jax.experimental import pallas as pl
from jax.experimental.pallas import tpu as pltpu
from jax.sharding import PartitionSpec as P

eps_norm = 1e-06

f32, bf16 = jnp.float32, jnp.bfloat16
MESH = pl.DeviceIdType.MESH
TRIPLES = 12
SLOTS = 3
DIRECT = 10
ORDERS = (("x", "y", "z"), ("y", "z", "x"), ("z", "x", "y"))


def my_place():
    b = lax.axis_index("batch")
    return {"z": b // 8, "x": lax.rem(b // 2, 4), "c": lax.rem(b, 2), "y": lax.axis_index("tile")}


def device_at(place):
    return {"batch": (place["z"] * 4 + place["x"]) * 2 + place["c"], "tile": place["y"]}


def neighbour(place, axis, step):
    there = dict(place)
    if axis == "c":
        there["c"] = 1 - place["c"]
    else:
        there[axis] = lax.rem(place[axis] + step + 4, 4)
    return device_at(there)


GROUP = tuple((flip, step) for flip in (0, 1) for step in range(4) if flip or step)
VECTORS = tuple((768 * k, 768, 6) for k in range(6)) + ((4608, 1536, 12), (6144, 3072, 24))


CHIPS = sorted(
    ((z, x, y) for z in range(4) for x in range(4) for y in range(4) if z or x or y),
    key=lambda steps: -sum(min(step, 4 - step) for step in steps),
)


def chip_at(place, steps):
    there = dict(place)
    for axis, step in zip("zxy", steps):
        there[axis] = lax.rem(place[axis] + step, 4)
    return device_at(there)


def in_group(place, flip, step):
    there = dict(place)
    there["c"] = lax.rem(place["c"] + flip, 2)
    there["y"] = lax.rem(place["y"] + step, 4)
    return device_at(there)


def gelu_parts(inner):
    half = 0.5 * (1.0 + lax.erf(inner * 0.7071067811865476))
    return inner * half, half


def lanes_of(j, width):
    return pl.ds(pl.multiple_of(j * width, width), width)


def rows_of(i, height):
    return pl.ds(pl.multiple_of(i * height, height), height)


NT = (((1,), (1,)), ((), ()))
TN = (((0,), (0,)), ((), ()))


def head_halves(pair):
    first = lax.broadcasted_iota(jnp.int32, pair.shape, 1) < 64
    nothing = jnp.zeros_like(pair)
    return jnp.concatenate([jnp.where(first, pair, nothing), jnp.where(first, nothing, pair)], axis=0)


def pair_probs(q, k, keymask):
    scores = lax.dot_general(head_halves(q * 0.125), k, NT, preferred_element_type=f32) + keymask
    expo = jnp.exp(scores - jnp.max(scores, axis=1, keepdims=True))
    return expo * (1.0 / jnp.sum(expo, axis=1, keepdims=True))


def whole_kernel(
    count_ref, companion_ref, widths_ref, divisor_ref,
    bq_ref, bo_ref, g1_ref, t1_ref, bu_ref, bd_ref, g2_ref, t2_ref,
    x_ref, wq_ref, wo_ref, wu_ref, wd_ref, perm_ref, spread_ref,
    out_hbm, vec_hbm, loss_hbm, emb_hbm, dx_ref,
    qkv_keep, ctx_keep, n1_keep, r1_keep, inner_keep, n2_keep, r2_keep,
    weight, perm, xb, qkv, ctx, n1, r1, inner, n2, r2, grad, d_outer, d_att, d_ctx, act_t, d_inner, d_qkv, vectors, apt,
    vq, vo, v1, t1, vu, vd, v2, t2, pool, d_emb, every, out_ref, vec_out_ref, loss_row,
    got0, got1a, got1b, half2, got2a, got2b, half3, got3a, got3b, rows24, got2d, got3d,
    vec_src, vec_z, vec_x, vec_mid, vec_cy,
    weight_sem, keep_sem, load_sem, table_sem, every_s, every_r, swap_s, swap_r,
    sems_s, sems_r, sem0_s, sem0_r, direct_s, direct_r, vec_s, vec_r,
):
    place = my_place()
    core = place["c"]
    half = send = None


    kept = {
        "qkv": (qkv, qkv_keep, 0), "ctx": (ctx, ctx_keep, 1), "n1": (n1, n1_keep, 2), "r1": (r1, r1_keep, 3),
        "inner": (inner, inner_keep, 4), "n2": (n2, n2_keep, 5), "r2": (r2, r2_keep, 6),
    }

    def keep(name):
        here, there, k = kept[name]
        return pltpu.make_async_copy(here, there, keep_sem.at[k])

    def load(name):
        if name == "xb":
            return pltpu.make_async_copy(x_ref.at[0], xb, load_sem.at[7])
        here, there, k = kept[name]
        return pltpu.make_async_copy(there, here, load_sem.at[k])

    def weights(k, layer, slot, extra=None):
        blocks = []
        for m in range(4):
            cols = pl.ds(768 * m, 768)
            if k == 0:
                src = wd_ref.at[layer, cols]
            elif k == 1:
                src = wu_ref.at[layer, :, cols]
            else:
                src = wq_ref.at[layer, :, cols] if m < 3 else wo_ref.at[layer]
            dst, sem = (weight.at[slot, cols], weight_sem.at[slot, m]) if extra is None else (extra.at[slot, cols], weight_sem.at[2 + slot, m])
            blocks.append(pltpu.make_async_copy(src, dst, sem))
        return blocks

    def fetch_weights(*use):
        for copy in weights(*use):
            copy.start()

    def ready_weights(*use):
        for copy in weights(*use):
            copy.wait()

    def back_slot(k, layer):
        return lax.rem((1 - layer) * 3 + k + 1, 2)

    load("xb").start()
    perm_copy = pltpu.make_async_copy(perm_ref, perm, table_sem.at[0])
    spread_copy = pltpu.make_async_copy(spread_ref, weight.at[1, pl.ds(0, 1536)], table_sem.at[1])

    barrier = pltpu.get_barrier_semaphore()
    for far in CHIPS:
        pl.semaphore_signal(barrier, inc=1, device_id=chip_at(place, far), device_id_type=MESH)
    for flip, step in GROUP:
        pl.semaphore_signal(barrier, inc=1, device_id=in_group(place, flip, step), device_id_type=MESH)

    for src, dst in ((bo_ref, vo), (g1_ref, v1), (t1_ref, t1), (bu_ref, vu), (bd_ref, vd), (g2_ref, v2), (t2_ref, t2)):
        for layer in range(2):
            dst[layer] = src[layer : layer + 1, :].astype(f32)
    for layer in range(2):
        vq[layer, :, 0:768] = bq_ref[layer : layer + 1, 0:768].astype(f32)
        vq[layer, :, 768:1536] = jnp.zeros((1, 768), f32)
        vq[layer, :, 1536:2304] = bq_ref[layer : layer + 1, 768:1536].astype(f32)
    count = count_ref[0]
    keymask = jnp.where(lax.broadcasted_iota(jnp.int32, (1, 256), 1) < count, 0.0, -1e9)


    chip = (place["z"] * 4 + place["x"]) * 4 + place["y"]

    def gather_start(e):
        for r in range(6):
            every[e, core, chip, r : r + 1, :] = pool[e, :, 128 * r : 128 * r + 128]
        mine = every.at[e, core, chip]
        for far in CHIPS:
            pltpu.make_async_remote_copy(
                src_ref=mine, dst_ref=mine, send_sem=every_s.at[e], recv_sem=every_r.at[e],
                device_id=chip_at(place, far), device_id_type=MESH,
            ).start()

    def swap_copy(e):
        mine = every.at[e, core]
        return pltpu.make_async_remote_copy(
            src_ref=mine, dst_ref=mine, send_sem=swap_s.at[e], recv_sem=swap_r.at[e],
            device_id=neighbour(place, "c", 1), device_id_type=MESH,
        )

    def gather_swap(e):
        others = every.at[e, core, pl.ds(0, 63)]
        pltpu.make_async_copy(others, others, every_r.at[e]).wait()
        swap_copy(e).start()

    def gather_end(e):
        others = every.at[e, core, pl.ds(0, 63)]
        pltpu.make_async_copy(others, others, every_s.at[e]).wait()
        swap_copy(e).wait()


    def norm(z, layer, normed_ref, scaled_ref, gain, shift, rows):
        center = z - jnp.mean(z, axis=1, keepdims=True)
        scaled = lax.rsqrt(jnp.mean(center * center, axis=1, keepdims=True) + eps_norm)
        normed = center * scaled
        normed_ref[rows, :] = normed
        scaled_ref[rows, :] = scaled
        return normed * gain[layer] + shift[layer]

    def run_if(wanted):
        return (lambda job: job()) if wanted else (lambda job: None)

    def forward_layer(layer, extra):
        is_first, is_last = layer == 0, layer == 1
        use_q = (2, layer, 0, extra)
        use_u = (1, 0, 1, extra) if is_first else (1, 1, 0)
        use_d = (0, layer, layer)

        def free(*names):
            @run_if(is_last)
            def _():
                for name in names:
                    keep(name).wait()

        def store(*names):
            @run_if(is_first)
            def _():
                for name in names:
                    keep(name).start()

        @run_if(is_first)
        def _():
            load("xb").wait()
            grad[...] = xb[...].astype(f32)

        @run_if(is_last)
        def _():
            xb[...] = grad[...].astype(bf16)

        free("qkv")
        blocks = weights(*use_q)
        for m in range(3):
            cols = pl.ds(768 * m, 768)
            blocks[m].wait()
            mixed = jnp.dot(xb[...], extra[0, cols, :], preferred_element_type=f32) + vq[layer, :, cols]
            qkv[:, cols] = mixed.astype(bf16)
        store("qkv")

        @run_if(is_first)
        def _():
            fetch_weights(1, 0, 1, extra)
            fetch_weights(0, 0, 0)

        @run_if(is_last)
        def _():
            perm_copy.start()

        free("ctx")

        def attend(pair, _):
            q, k, v = (qkv[:, lanes_of(pair + 6 * third, 128)] for third in range(3))
            probs = pair_probs(q, k, keymask).astype(bf16)
            both = jnp.dot(probs, v, preferred_element_type=f32)
            first = lax.broadcasted_iota(jnp.int32, (256, 128), 1) < 64
            ctx[:, lanes_of(pair, 128)] = jnp.where(first, both[:256], both[256:]).astype(bf16)
            return 0

        lax.fori_loop(0, 6, attend, 0, unroll=6)
        store("ctx")

        @run_if(is_last)
        def _():
            gather_swap(0)

        blocks[3].wait()
        grad[...] += jnp.dot(ctx[...], extra[0, 2304:3072, :], preferred_element_type=f32) + vo[layer]

        @run_if(is_first)
        def _():
            fetch_weights(2, 1, 0, extra)
            fetch_weights(0, 1, 1)

        free("n1", "r1", "n2", "r2")

        def norm_one(i, _):
            rows = rows_of(i, 64)
            mid = norm(grad[rows, :], layer, n1, r1, v1, t1, rows)
            n2[rows, :] = mid
            d_att[rows, :] = mid.astype(bf16)
            return 0

        lax.fori_loop(0, 4, norm_one, 0, unroll=4)
        store("n1", "r1")
        free("inner")
        blocks = weights(*use_u)
        expand = extra.at[1] if is_first else weight.at[0]
        for m in range(4):
            cols = pl.ds(768 * m, 768)
            blocks[m].wait()
            value = jnp.dot(d_att[...], expand[cols, :], preferred_element_type=f32) + vu[layer, :, cols]
            inner[:, cols] = value
            d_inner[:, cols] = gelu_parts(value)[0].astype(bf16)
        store("inner")

        ready_weights(*use_d)
        n2[...] += jnp.dot(d_inner[...], weight[layer], preferred_element_type=f32) + vd[layer]

        @run_if(is_first)
        def _():
            fetch_weights(1, 1, 0)

        def norm_two(i, total):
            rows = rows_of(i, 64)
            result = norm(n2[rows, :], layer, n2, r2, v2, t2, rows)
            grad[rows, :] = result
            spot = lax.broadcasted_iota(jnp.int32, (64, 1), 0) + i * 64
            return total + jnp.sum(jnp.where(spot < count, result, 0.0), axis=0, keepdims=True)

        total = lax.fori_loop(0, 4, norm_two, jnp.zeros((1, 768), f32), unroll=4)
        pool[layer] = total / count.astype(f32)
        store("n2", "r2")

        @run_if(is_first)
        def _():
            pl.semaphore_wait(barrier, 70)
            gather_start(0)

        @run_if(is_last)
        def _():
            gather_end(0)
            gather_start(1)


    def pairing(e, loss):
        me = ((place["z"] * 4 + place["x"]) * 2 + core) * 4 + place["y"]
        row = lax.broadcasted_iota(jnp.int32, (128, 128), 0)
        col = lax.broadcasted_iota(jnp.int32, (128, 128), 1)
        rows = lax.broadcasted_iota(jnp.int32, (128, 1), 0)
        lane = lax.broadcasted_iota(jnp.int32, (1, 768), 1)
        companion = companion_ref[...]
        divisor = divisor_ref[0]
        partner = (row == companion).astype(f32)
        mine = jnp.sum(jnp.where(lax.broadcasted_iota(jnp.int32, (1, 128), 1) == me, companion, 0), axis=1, keepdims=True)
        chosen = (rows == mine).astype(f32)
        is_me = rows == me
        gathered = jnp.concatenate([every[e, c].reshape(16, 1, 4, 6, 128) for c in range(2)], axis=1).reshape(128, 6, 128)
        embed = jnp.concatenate(
            [gathered[:, r, :] for r in range(6)], axis=1
        )
        high = embed.astype(bf16)
        low = (embed - high.astype(f32)).astype(bf16)
        own = pool[e]
        total = jnp.zeros((1, 768), f32)
        for p in range(4):
            keep_p = (lane < widths_ref[p]).astype(f32)
            keep_low = keep_p.astype(bf16)
            high_p, low_p = high * keep_low, low * keep_low
            gram = (
                lax.dot_general(high_p, high, NT, preferred_element_type=f32)
                + lax.dot_general(high_p, low, NT, preferred_element_type=f32)
                + lax.dot_general(low_p, high, NT, preferred_element_type=f32)
            )
            diagonal = jnp.where(row == col, gram, 0.0)
            inverse = lax.rsqrt(jnp.sum(diagonal, axis=1, keepdims=True) + eps_norm)
            inverse_row = lax.rsqrt(jnp.sum(diagonal, axis=0, keepdims=True) + eps_norm)
            sims = gram * inverse * inverse_row / divisor
            sims = jnp.where(row == col, -1e30, sims)
            top = jnp.max(sims, axis=1, keepdims=True)
            lse = top + jnp.log(jnp.sum(jnp.exp(sims - top), axis=1, keepdims=True))
            loss = loss + (lse - jnp.sum(sims * partner, axis=1, keepdims=True))
            to_me = jnp.sum(jnp.where(col == me, sims, 0.0), axis=1, keepdims=True)
            lse_me = jnp.sum(jnp.where(is_me, lse, 0.0), axis=0, keepdims=True)
            weight_j = jnp.exp(to_me - lse_me) + jnp.exp(to_me - lse) - 2.0 * chosen
            dunit = jnp.sum(embed * (weight_j * inverse), axis=0, keepdims=True) * keep_p
            inverse_me = jnp.sum(jnp.where(is_me, inverse, 0.0), axis=0, keepdims=True)
            unit_me = own * keep_p * inverse_me
            inside = dunit - unit_me * jnp.sum(unit_me * dunit, axis=1, keepdims=True)
            total = total + inside * inverse_me
        d_emb[e] = total / (8.0 * divisor)
        return loss


    def norm_back(normed, scaled, gain, rounded, at_gain, at_shift, at_bias, layer):
        sums = [jnp.zeros((1, 768), f32) for _ in range(3)]
        for i in range(4):
            rows = pl.ds(64 * i, 64)
            dy, n = grad[rows, :], normed[rows, :]
            dn = dy * gain
            inside = dn - jnp.mean(dn, axis=1, keepdims=True) - n * jnp.mean(dn * n, axis=1, keepdims=True)
            dz = scaled[rows, :] * inside
            low = dz.astype(bf16)
            grad[rows, :] = dz
            rounded[rows, :] = low
            for k, term in enumerate((dy * n, dy, low.astype(f32))):
                sums[k] = sums[k] + jnp.sum(term, axis=0, keepdims=True)
        for at, total in zip((at_gain, at_shift, at_bias), sums):
            vectors[layer, :, at : at + 768] = total

    def turn_active():
        def turn(j, _):
            value = inner[:, lanes_of(j, 256)]
            act_t[lanes_of(j, 256), :] = gelu_parts(value)[0].T.astype(bf16)
            return 0

        lax.fori_loop(0, 12, turn, 0, unroll=2)

    def permute(operand, which):
        for o in range(3):
            apt[o, which] = lax.dot_general(perm[o], operand, NT, preferred_element_type=f32).astype(bf16)

    def begin_layer(layer):
        spots = lax.broadcasted_iota(jnp.int32, (256, 1), 0)
        pooled = jnp.where(spots < count, 1.0, 0.0) / count.astype(f32)

        @pl.when(layer == 1)
        def _():
            grad[...] = pooled * d_emb[1]

        @pl.when(layer == 0)
        def _():
            grad[...] += pooled * d_emb[0]
            load("n2").wait()
            load("r2").wait()
            load("inner").wait()
            turn_active()

        norm_back(n2, r2, v2[layer], d_outer, 3072, 3840, 2304, layer)

        @pl.when(layer == 1)
        def _():
            load("n2").start()
            load("r2").start()

    def through_expand(layer):
        slot = back_slot(0, layer)

        @pl.when(layer == 0)
        def _():
            ready_weights(0, 0, slot)

        def chunk(j, _):
            cols = lanes_of(j, 512)
            d_act = lax.dot_general(d_outer[...], weight[slot, cols, :], NT, preferred_element_type=f32)
            value = inner[:, cols]
            slope = gelu_parts(value)[1] + value * (jnp.exp(-0.5 * value * value) * 0.3989422804014327)
            low = (d_act * slope).astype(bf16)
            d_inner[:, cols] = low
            at = pl.ds(pl.multiple_of(6144 + j * 512, 512), 512)
            vectors[layer, :, at] = jnp.sum(low.astype(f32), axis=0, keepdims=True)
            return 0

        lax.fori_loop(0, 6, chunk, 0, unroll=2)
        fetch_weights(2, layer, slot)

        @pl.when(layer == 1)
        def _():
            load("inner").start()

        @pl.when(layer == 0)
        def _():
            load("n1").wait()
            load("r1").wait()
            permute((n1[...] * v1[0] + t1[0]).astype(bf16), 0)

    def through_mixer(layer):
        slot = back_slot(1, layer)

        @pl.when(layer == 0)
        def _():
            ready_weights(1, 0, slot)

        for m in range(4):
            cols = pl.ds(768 * m, 768)
            grad[...] += lax.dot_general(d_inner[:, cols], weight[slot, cols, :], NT, preferred_element_type=f32)
        norm_back(n1, r1, v1[layer], d_att, 768, 1536, 0, layer)

        @pl.when(layer == 1)
        def _():
            fetch_weights(0, 0, slot)
            load("n1").start()
            load("r1").start()

        slot = back_slot(2, layer)
        ready_weights(2, layer, slot)
        d_ctx[...] = lax.dot_general(d_att[...], weight[slot, 2304:3072, :], NT, preferred_element_type=f32).astype(bf16)

    def through_attention(layer, first_pair, pairs):
        def pair_back(i, _):
            pair = first_pair + i
            at = [lanes_of(pair + 6 * third, 128) for third in range(3)]
            q, k, v = (qkv[:, cols] for cols in at)
            probs = pair_probs(q, k, keymask)
            dc = head_halves(d_ctx[:, at[0]])
            dp = lax.dot_general(dc, v, NT, preferred_element_type=f32)
            ds = (probs * (dp - jnp.sum(dp * probs, axis=1, keepdims=True))).astype(bf16)
            dq = jnp.dot(
                jnp.concatenate([ds[:256], ds[256:]], axis=1), head_halves(k * 0.125), preferred_element_type=f32
            ).astype(bf16)
            dk = lax.dot_general(ds, head_halves(q * 0.125), TN, preferred_element_type=f32).astype(bf16)
            dv = lax.dot_general(probs.astype(bf16), dc, TN, preferred_element_type=f32).astype(bf16)
            for cols, value in zip(at, (dq, dk, dv)):
                d_qkv[:, cols] = value
            for start, value in ((4608, dq), (5376, dv)):
                where = pl.ds(pl.multiple_of(start + pair * 128, 128), 128)
                vectors[layer, :, where] = jnp.sum(value.astype(f32), axis=0, keepdims=True)
            return 0

        lax.fori_loop(0, pairs, pair_back, 0, unroll=2)

    def through_projection(layer):
        slot = back_slot(2, layer)
        for m in range(3):
            cols = pl.ds(768 * m, 768)
            grad[...] += lax.dot_general(d_qkv[:, cols], weight[slot, cols, :], NT, preferred_element_type=f32)

        @pl.when(layer == 1)
        def _():
            fetch_weights(1, 0, slot)
            load("qkv").start()

        @pl.when(layer == 0)
        def _():
            dx_copy.start()

    dx_copy = pltpu.make_async_copy(grad, dx_ref.at[0], table_sem.at[2])
    emb_copy = pltpu.make_async_copy(pool, emb_hbm, table_sem.at[3])
    loss_copy = pltpu.make_async_copy(loss_row, loss_hbm, table_sem.at[4])
    out_copy = pltpu.make_async_copy(out_ref, out_hbm, table_sem.at[5])
    vec_copy = pltpu.make_async_copy(vec_out_ref, vec_hbm, table_sem.at[6])

    def store_rows(o, slot, mine, tile0, value):
        for j in range(value.shape[1] // 128):
            part = value[:, 128 * j : 128 * (j + 1)].reshape(16, 3, 8, 128)
            if mine:
                half[o, slot, :, tile0 + 3 * j : tile0 + 3 * j + 3] = part
            else:
                send[o, :, tile0 + 3 * j : tile0 + 3 * j + 3] = part

    def product(o, slot, which, ref, at, width, tile0):
        for mine in (False, True):
            c = core if mine else 1 - core
            lhs = apt[o, which, pl.ds(pl.multiple_of(c * 384, 128), 384), :]
            for w in range(0, width, 256):
                value = jnp.dot(lhs, ref[:, at + w : at + w + 256], preferred_element_type=f32)
                store_rows(o, slot, mine, tile0 + 3 * (w // 128), value)

    def product_shrink(slot, k):
        def block(z, _):
            for mine in (False, True):
                c = core if mine else 1 - core
                lhs = jnp.concatenate(
                    [act_t[pl.ds(pl.multiple_of(z * 768 + x * 192 + c * 96, 32), 96), :] for x in range(4)], axis=0
                )
                value = jnp.dot(lhs, d_outer[:, 384 * k : 384 * (k + 1)], preferred_element_type=f32)
                for x in range(4):
                    for y in range(4):
                        for j in range(3):
                            p = {"x": x, "y": y, "z": z}
                            d1, d2, d3 = (p[axis] for axis in ORDERS[j])
                            row = x * 96 + (y * 3 + j) * 8
                            for ct in range(3):
                                tile = value[row : row + 8, 128 * ct : 128 * ct + 128]
                                if mine:
                                    half[j, slot, d1 * 4 + d2, d3 * 3 + ct] = tile
                                else:
                                    send[j, d1 * 4 + d2, d3 * 3 + ct] = tile
            return 0

        lax.fori_loop(0, 4, block, 0)

    def make(u):
        slot = lax.rem(u, 4)
        layer = 1 - u // 6
        kind = lax.rem(u, 6)

        def to_other_core(o):
            copy0(o, u).start()

        @pl.when(kind == 0)
        def _():
            begin_layer(layer)
            product_shrink(slot, 0)
            for o in range(3):
                to_other_core(o)

        @pl.when(kind == 1)
        def _():
            product_shrink(slot, 1)
            for o in range(3):
                to_other_core(o)

        for k in range(2):
            @pl.when(kind == 2 + k)
            def _():
                for o in range(3):
                    product(o, slot, 0, d_inner, (k * 3 + o) * 512, 512, 0)
                    to_other_core(o)

        @pl.when(kind == 4)
        def _():
            for o in range(3):
                product(o, slot, 0, d_qkv, o * 768, 512, 0)
                to_other_core(o)

        @pl.when(kind == 5)
        def _():
            for o in range(3):
                product(o, slot, 0, d_qkv, o * 768 + 512, 256, 0)
                product(o, slot, 1, d_att, o * 256, 256, 6)
                to_other_core(o)

    def follow(u):
        layer = 1 - u // 6
        kind = lax.rem(u, 6)

        @pl.when(kind == 1)
        def _():
            through_expand(layer)

        @pl.when(kind == 2)
        def _():
            through_mixer(layer)

        @pl.when(kind == 3)
        def _():
            @pl.when(layer == 0)
            def _():
                load("xb").wait()
                load("ctx").wait()

            permute(xb[...], 0)
            permute(ctx[...], 1)

            @pl.when(layer == 1)
            def _():
                load("xb").start()
                load("ctx").start()

            @pl.when(layer == 0)
            def _():
                load("qkv").wait()

            through_attention(layer, 0, 4)

        @pl.when(kind == 4)
        def _():
            through_attention(layer, 4, 2)
            through_projection(layer)


    def exchange(o, k, slot, src_up, src_down, got):
        axis = ORDERS[o][k // 2]
        copies = [
            pltpu.make_async_remote_copy(
                src_ref=src, dst_ref=got.at[o, slot, way], send_sem=sems_s.at[o, k, slot], recv_sem=sems_r.at[o, k, slot],
                device_id=neighbour(place, axis, step), device_id_type=MESH,
            )
            for way, (src, step) in enumerate(((src_up, 1), (src_down, -1)))
        ]
        return copies, got.at[o, slot], sems_s.at[o, k, slot], sems_r.at[o, k, slot]

    def begin(exchanged):
        for copy in exchanged[0]:
            copy.start()

    def end(exchanged):
        _, landed, sent_sem, landed_sem = exchanged
        pltpu.make_async_copy(landed, landed, sent_sem).wait()
        pltpu.make_async_copy(landed, landed, landed_sem).wait()

    def spots(o, phase):
        a = place[ORDERS[o][phase]]
        return a, lax.rem(a + 1, 4), lax.rem(a + 2, 4), lax.rem(a + 3, 4)

    def copy0(o, u):
        slot = lax.rem(u, 2)
        return pltpu.make_async_remote_copy(
            src_ref=send.at[o], dst_ref=got0.at[o, slot], send_sem=sem0_s.at[o], recv_sem=sem0_r.at[o, slot],
            device_id=neighbour(place, "c", 1), device_id_type=MESH,
        )

    def step_a(o, phase, u):
        slot = lax.rem(u, SLOTS)
        a, up, far, down = spots(o, phase)
        if phase == 0:
            src, got = (half.at[o, lax.rem(u, 4), pl.ds(far * 4, 2)], half.at[o, lax.rem(u, 4), pl.ds(far * 4 + 2, 2)]), got1a
        elif phase == 1:
            src, got = (half2.at[o, slot, far, pl.ds(0, 6)], half2.at[o, slot, far, pl.ds(6, 6)]), got2a
        else:
            src, got = (half3.at[o, slot, far, pl.ds(0, 2)], half3.at[o, slot, far, pl.ds(2, 2)]), got3a
        return exchange(o, 2 * phase, slot, src[0], src[1], got)

    def step_b(o, phase, u):
        slot = lax.rem(u, SLOTS)
        a, up, far, down = spots(o, phase)
        if phase == 0:
            src, got = (half.at[o, lax.rem(u, 4), pl.ds(up * 4, 4)], half.at[o, lax.rem(u, 4), pl.ds(down * 4, 4)]), got1b
        elif phase == 1:
            src, got = (half2.at[o, slot, up], half2.at[o, slot, down]), got2b
        else:
            src, got = (half3.at[o, slot, up], half3.at[o, slot, down]), got3b
        return exchange(o, 2 * phase + 1, slot, src[0], src[1], got)

    def add_a(o, phase, u):
        slot = lax.rem(u, SLOTS)
        a, up, far, down = spots(o, phase)
        if phase == 0:
            for i in range(2):
                half[o, lax.rem(u, 4), up * 4 + i] += got1a[o, slot, 0, i]
                half[o, lax.rem(u, 4), down * 4 + 2 + i] += got1a[o, slot, 1, i]
        elif phase == 1:
            half2[o, slot, up, 0:6] += got2a[o, slot, 0]
            half2[o, slot, down, 6:12] += got2a[o, slot, 1]
        else:
            half3[o, slot, up, 0:2] += got3a[o, slot, 0]
            half3[o, slot, down, 2:4] += got3a[o, slot, 1]

    def add_b(o, phase, u):
        slot = lax.rem(u, SLOTS)
        a, up, far, down = spots(o, phase)
        if phase == 0:
            for i in range(4):
                half2[o, slot, i] = half[o, lax.rem(u, 4), a * 4 + i] + got1b[o, slot, 0, i] + got1b[o, slot, 1, i]
        elif phase == 1:
            to_third(o, slot, u, half2[o, slot, a] + got2b[o, slot, 0] + got2b[o, slot, 1])
        else:
            out_ref[u, o] = half3[o, slot, a] + got3b[o, slot, 0] + got3b[o, slot, 1]

    def to_third(o, slot, u, total):
        @pl.when(lax.rem(u, 6) < 2)
        def _():
            for k in range(4):
                half3[o, slot, k, 0:3] = total[3 * k : 3 * k + 3]

        @pl.when(lax.rem(u, 6) >= 2)
        def _():
            for ct in range(4):
                rows24[o, ct] = total[3 * ct : 3 * ct + 3].reshape(24, 128)
            for k in range(4):
                for ct in range(4):
                    half3[o, slot, k, ct, 0:6, :] = rows24[o, ct, 6 * k : 6 * k + 6, :]

    def direct(o, phase, u):
        slot, way = lax.rem(u, SLOTS), lax.rem(u, 2)
        a = place[ORDERS[o][phase]]
        src, got = ((half2, got2d), (half3, got3d))[phase - 1]
        copies = [
            pltpu.make_async_remote_copy(
                src_ref=src.at[o, slot, lax.rem(a + step, 4)], dst_ref=got.at[o, way, step - 1],
                send_sem=direct_s.at[o, phase - 1, way], recv_sem=direct_r.at[o, phase - 1, way],
                device_id=neighbour(place, ORDERS[o][phase], step), device_id_type=MESH,
            )
            for step in (1, 2, 3)
        ]
        return copies, got.at[o, way], direct_s.at[o, phase - 1, way], direct_r.at[o, phase - 1, way]

    def direct_second(u):
        slot, way = lax.rem(u, SLOTS), lax.rem(u, 2)
        for o in range(3):
            end(direct(o, 1, u))
            total = half2[o, slot, place[ORDERS[o][1]]]
            for i in range(3):
                total += got2d[o, way, i]
            to_third(o, slot, u, total)
            begin(direct(o, 2, u))

    def direct_third(u):
        slot, way = lax.rem(u, SLOTS), lax.rem(u, 2)
        for o in range(3):
            end(direct(o, 2, u))
            total = half3[o, slot, place[ORDERS[o][2]]]
            for i in range(3):
                total += got3d[o, way, i]
            out_ref[u, o] = total

    def spread_vectors():
        for layer in range(2):
            total = jnp.zeros((128, 128), f32)
            for start, width, keep in VECTORS:
                d = lax.broadcasted_iota(jnp.int32, (128, width), 0) * keep
                q = lax.broadcasted_iota(jnp.int32, (128, width), 1)
                own = jnp.where((q >= d) & (q < d + keep), vectors[layer, :, start : start + width], 0.0)
                high = own.astype(bf16)
                low = (own - high.astype(f32)).astype(bf16)
                for part in range(width // 768):
                    k = start // 768 + part
                    lanes = weight[1, 768 * (k // 6) : 768 * (k // 6 + 1), 128 * (k % 6) : 128 * (k % 6 + 1)]
                    at = slice(768 * part, 768 * (part + 1))
                    total += jnp.dot(high[:, at], lanes, preferred_element_type=f32)
                    total += jnp.dot(low[:, at], lanes, preferred_element_type=f32)
            total = total.reshape(4, 4, 8, 128)
            for z in range(4):
                for x in range(4):
                    vec_src[z, x, layer] = total[z, x]

    def vector_copies(k, landed, pieces):
        copies = [
            pltpu.make_async_remote_copy(
                src_ref=src, dst_ref=landed.at[i], send_sem=vec_s.at[k], recv_sem=vec_r.at[k], device_id=device, device_id_type=MESH
            )
            for i, (src, device) in enumerate(pieces)
        ]
        return copies, landed, vec_s.at[k], vec_r.at[k]

    def copies_z():
        return vector_copies(0, vec_z, [(vec_src.at[lax.rem(place["z"] + i, 4)], neighbour(place, "z", i)) for i in (1, 2, 3)])

    def copies_x():
        mine = place["z"]
        return vector_copies(1, vec_x, [(vec_src.at[mine, lax.rem(place["x"] + i, 4)], neighbour(place, "x", i)) for i in (1, 2, 3)])

    def copies_group():
        return vector_copies(2, vec_cy, [(vec_mid, in_group(place, flip, step)) for flip, step in GROUP])

    def vectors_start():
        spread_copy.wait()
        spread_vectors()
        begin(copies_z())

    def vectors_second():
        end(copies_z())
        for x in range(4):
            vec_src[place["z"], x] += vec_z[0, x] + vec_z[1, x] + vec_z[2, x]
        begin(copies_x())

    def vectors_third():
        end(copies_x())
        vec_mid[...] = vec_src[place["z"], place["x"]] + vec_x[0] + vec_x[1] + vec_x[2]
        begin(copies_group())

    def vectors_last():
        end(copies_group())
        total = vec_mid[...]
        for i in range(7):
            total += vec_cy[i]
        mine = lax.broadcasted_iota(jnp.int32, (2, 8, 128), 1) == core * 4 + place["y"]
        vec_out_ref[...] = jnp.sum(jnp.where(mine, total, 0.0), axis=1)

    def when(u, first, last, job):
        @pl.when((u >= first) & (u < last))
        def _():
            job(u)

    def enter(u):
        slot = lax.rem(u, SLOTS)
        for o in range(3):
            copy0(o, u).wait()

            def add(i, _):
                half[o, lax.rem(u, 4), i] += got0[o, lax.rem(u, 2), i]
                return 0

            lax.fori_loop(0, 16, add, 0)
            begin(step_a(o, 0, u))

    def second(phase):
        def job(u):
            for o in range(3):
                end(step_a(o, phase, u))
                add_a(o, phase, u)
                begin(step_b(o, phase, u))
        return job

    def third(phase):
        def job(u):
            for o in range(3):
                end(step_b(o, phase, u))
                add_b(o, phase, u)
                if phase == 0:
                    @pl.when(u < DIRECT)
                    def _():
                        begin(step_a(o, 1, u))

                    @pl.when(u >= DIRECT)
                    def _():
                        begin(direct(o, 1, u))
                elif phase == 1:
                    begin(step_a(o, 2, u))
        return job

    def tick(u, _):
        when(u, 0, TRIPLES, make)
        when(u - 3, 0, TRIPLES, third(0))
        when(u - 4, 0, DIRECT, second(1))
        when(u - 5, 0, DIRECT, third(1))
        when(u - 6, 0, DIRECT, second(2))
        when(u - 7, 0, DIRECT, third(2))
        when(u - 4, DIRECT, TRIPLES, direct_second)
        when(u - 5, DIRECT, TRIPLES, direct_third)
        when(u, 0, TRIPLES, enter)
        when(u - 1, 0, TRIPLES, second(0))
        when(u, 0, TRIPLES, follow)

        @pl.when(u == TRIPLES - 1)
        def _():
            spread_copy.start()

        for k, job in enumerate((vectors_start, vectors_second, vectors_third, vectors_last)):
            pl.when(u == TRIPLES + k)(job)
        return 0


    def forward_both(extra):
        fetch_weights(2, 0, 0, extra)
        forward_layer(0, extra)
        forward_layer(1, extra)

    pl.run_scoped(forward_both, pltpu.VMEM((2, 3072, 768), bf16))
    emb_copy.start()
    half3[...] = jnp.zeros_like(half3)
    loss = pairing(0, jnp.zeros((128, 1), f32))
    turn_active()
    gather_swap(1)
    perm_copy.wait()
    permute(d_att[...], 0)
    gather_end(1)
    loss_row[...] = pairing(1, loss) / 8.0
    loss_copy.start()

    def reduce_all(half_ref, send_ref):
        nonlocal half, send
        half, send = half_ref, send_ref
        lax.fori_loop(0, DIRECT + 7, tick, 0)

    pl.run_scoped(reduce_all, pltpu.VMEM((3, 4, 16, 12, 8, 128), f32), pltpu.VMEM((3, 16, 12, 8, 128), f32))
    out_copy.start()
    vec_copy.start()
    for copy in (dx_copy, emb_copy, loss_copy, out_copy, vec_copy):
        copy.wait()


def permutations():
    rows = np.arange(768).reshape(4, 4, 2, 4, 6)
    names = {"z": 0, "x": 1, "c": 2, "y": 3}
    out = np.zeros((3, 768, 768), np.float32)
    for o, (d1, d2, d3) in enumerate(ORDERS):
        taken = rows.transpose(2, names[d1], names[d2], names[d3], 4).reshape(-1)
        out[o, np.arange(768), taken] = 1
    return out.astype(ml_dtypes.bfloat16)


def lane_places():
    out = np.zeros((9216, 128), np.float32)
    lane = 0
    for start, width, keep in VECTORS:
        q = np.arange(width)
        out[start + q, lane + q % keep] = 1
        lane += keep
    out = out.reshape(2, 6, 768, 128).transpose(0, 2, 1, 3).reshape(1536, 768)
    return out.astype(ml_dtypes.bfloat16)


def finish_kernel(out_hbm, vec_hbm, loss_hbm, emb_hbm, dx_hbm, *refs):
    loss_out, emb_out, dx_out, qkv_out, qv_out, mixer_out, bias_out, gain_out, shift_out, up_out, ffn_out, down_out, downbias_out, fingain_out, finshift_out = refs[:15]
    out_ref, vec_ref, loss_ref, emb_ref, dx_ref, sem = refs[15:]
    copies = [
        pltpu.make_async_copy(src, dst, sem.at[k])
        for k, (src, dst) in enumerate(((out_hbm, out_ref), (vec_hbm, vec_ref), (loss_hbm, loss_ref), (emb_hbm, emb_ref), (dx_hbm, dx_ref)))
    ]
    for copy in copies:
        copy.start()
    for copy in copies[:4]:
        copy.wait()
    for layer in range(2):
        emb_out[0, layer : layer + 1, :] = emb_ref[layer]
    copies[4].wait()
    last = pltpu.make_async_copy(dx_ref, dx_out, sem.at[4])
    last.start()
    for layer in range(2):
        first = 6 * (1 - layer)
        for k in range(2):
            for o in range(3):
                for ct in range(3):
                    down_out[layer, 8 * o : 8 * o + 8, 384 * k + 128 * ct : 384 * k + 128 * ct + 128] = out_ref[first + k, o, ct]
                for ct in range(4):
                    at = (k * 3 + o) * 512 + 128 * ct
                    up_out[:, layer, at : at + 128] = out_ref[first + 2 + k, o, ct, 0:6, :]
        for o in range(3):
            for ct in range(4):
                at = o * 768 + 128 * ct
                qkv_out[:, layer, at : at + 128] = out_ref[first + 4, o, ct, 0:6, :]
            for ct in range(2):
                at = o * 768 + 512 + 128 * ct
                qkv_out[:, layer, at : at + 128] = out_ref[first + 5, o, ct, 0:6, :]
                at = o * 256 + 128 * ct
                mixer_out[:, layer, at : at + 128] = out_ref[first + 5, o, 2 + ct, 0:6, :]
    lane = 0
    for (_, _, keep), dst in zip(
        VECTORS, (bias_out, gain_out, shift_out, downbias_out, fingain_out, finshift_out, qv_out, ffn_out)
    ):
        dst[...] = vec_ref[:, lane : lane + keep]
        lane += keep
    rows = lax.broadcasted_iota(jnp.int32, (128, 1), 0)
    for k in range(4):
        loss_out[k] = jnp.sum(jnp.where(rows == lax.axis_index("batch") * 4 + k, loss_ref[...], 0.0))
    last.wait()


def body(slots, counts, companion, widths, divisor, triple, bias_qv, mixer, bias_mixer, gain_one, shift_one, expand, bias_expand, shrink, bias_shrink, gain_two, shift_two):
    tile = (8, 128)
    vmem = pl.BlockSpec(memory_space=pltpu.VMEM)
    smem = pl.BlockSpec(memory_space=pltpu.SMEM)
    hbm = pl.BlockSpec(memory_space=pl.ANY)

    def vm(*shape, dtype=f32):
        return pltpu.VMEM(shape, dtype)

    dma = pltpu.SemaphoreType.DMA
    saved = [((256, 2304), bf16), ((256, 768), bf16), ((256, 768), f32), ((256, 1), f32), ((256, 3072), f32), ((256, 768), f32), ((256, 1), f32)]
    shapes = [((TRIPLES, 3, 4) + tile, f32), ((2, 128), f32), ((128, 1), f32), ((2, 1, 768), f32), ((1, 256, 768), f32)] + saved
    results = pl.pallas_call(
        whole_kernel,
        out_shape=[jax.ShapeDtypeStruct(s, t) for s, t in shapes],
        in_specs=[smem, vmem, smem, smem] + [vmem] * 8 + [hbm] * 7,
        out_specs=[hbm] * 12,
        scratch_shapes=[
            vm(2, 3072, 768, dtype=bf16), vm(3, 768, 768, dtype=bf16), vm(256, 768, dtype=bf16), vm(256, 2304, dtype=bf16),
            vm(256, 768, dtype=bf16), vm(256, 768), vm(256, 1), vm(256, 3072), vm(256, 768), vm(256, 1), vm(256, 768),
            vm(256, 768, dtype=bf16), vm(256, 768, dtype=bf16), vm(256, 768, dtype=bf16), vm(3072, 256, dtype=bf16),
            vm(256, 3072, dtype=bf16), vm(256, 2304, dtype=bf16), vm(2, 1, 9216), vm(3, 2, 768, 256, dtype=bf16),
            vm(2, 1, 2304), vm(2, 1, 768), vm(2, 1, 768), vm(2, 1, 768), vm(2, 1, 3072), vm(2, 1, 768), vm(2, 1, 768), vm(2, 1, 768),
            vm(2, 1, 768), vm(2, 1, 768), vm(2, 2, 64, 6, 128), vm(TRIPLES, 3, 4, *tile), vm(2, 128), vm(128, 1),
            vm(3, 2, 16, 12, *tile),
            vm(3, SLOTS, 2, 2, 12, *tile), vm(3, SLOTS, 2, 4, 12, *tile),
            vm(3, SLOTS, 4, 12, *tile), vm(3, SLOTS, 2, 6, *tile), vm(3, SLOTS, 2, 12, *tile),
            vm(3, SLOTS, 4, 4, *tile), vm(3, SLOTS, 2, 2, *tile), vm(3, SLOTS, 2, 4, *tile), vm(3, 4, 24, 128),
            vm(3, 2, 3, 12, *tile), vm(3, 2, 3, 4, *tile),
            vm(4, 4, 2, *tile), vm(3, 4, 2, *tile), vm(3, 2, *tile), vm(2, *tile), vm(7, 2, *tile),
            dma((4, 4)), dma((7,)), dma((8,)), dma((7,)), dma((2,)), dma((2,)), dma((2,)), dma((2,)),
            dma((3, 6, SLOTS)), dma((3, 6, SLOTS)), dma((3,)), dma((3, 2)), dma((3, 2, 2)), dma((3, 2, 2)),
            dma((3,)), dma((3,)),
        ],
        compiler_params=pltpu.CompilerParams(
            collective_id=1, has_side_effects=True, vmem_limit_bytes=63 * 1024 * 1024
        ),
    )(
        counts, companion[None], widths, divisor,
        bias_qv, bias_mixer, gain_one, shift_one, bias_expand, bias_shrink, gain_two, shift_two,
        slots, triple, mixer, expand, shrink, jnp.asarray(permutations()), jnp.asarray(lane_places()),
    )
    out, vec_out, loss, embeddings, dx = results[:5]
    shapes = [(4,), (1, 2, 768), (1, 256, 768), (6, 2, 2304), (2, 12), (6, 2, 768), (2, 6), (2, 6), (2, 6), (6, 2, 3072), (2, 24), (2, 24, 768), (2, 6), (2, 6), (2, 6)]
    loss, embeddings, *rest = pl.pallas_call(
        finish_kernel,
        out_shape=[jax.ShapeDtypeStruct(s, f32) for s in shapes],
        in_specs=[hbm] * 5,
        out_specs=[smem, vmem, hbm] + [vmem] * 12,
        scratch_shapes=[vm(TRIPLES, 3, 4, *tile), vm(2, 128), vm(128, 1), vm(2, 1, 768), vm(1, 256, 768), dma((5,))],
        compiler_params=pltpu.CompilerParams(vmem_limit_bytes=63 * 1024 * 1024),
    )(out, vec_out, loss, embeddings, dx)
    rest = [r.transpose(1, 0, 2) if r.shape[:2] == (6, 2) else r for r in rest]
    return (loss, embeddings, *rest)


def solution(mesh):
    return jax.shard_map(
        body,
        mesh=mesh,
        in_specs=(
            P(("batch", "tile"), None, None),
            P(("batch", "tile")),
            P(),
            P(),
            P(),
            P(),
            P(),
            P(),
            P(),
            P(),
            P(),
            P(),
            P(),
            P(),
            P(),
            P(),
            P(),
        ),
        out_specs=(
            P("batch"),
            P(("batch", "tile"), None, None),
            P(("batch", "tile"), None, None),
            P(None, ("batch", "tile"), None),
            P(None, ("batch", "tile")),
            P(None, ("batch", "tile"), None),
            P(None, ("batch", "tile")),
            P(None, ("batch", "tile")),
            P(None, ("batch", "tile")),
            P(None, ("batch", "tile"), None),
            P(None, ("batch", "tile")),
            P(None, ("batch", "tile"), None),
            P(None, ("batch", "tile")),
            P(None, ("batch", "tile")),
            P(None, ("batch", "tile")),
        ),
        check_vma=False,
    )
```

```python
import jax
import jax.numpy as jnp
import ml_dtypes
import numpy as np
from jax import lax
from jax.experimental import pallas as pl
from jax.experimental.pallas import tpu as pltpu
from jax.sharding import PartitionSpec as P

eps_norm = 1e-06

f32, bf16 = jnp.float32, jnp.bfloat16
MESH = pl.DeviceIdType.MESH
TRIPLES = 12
SLOTS = 3
DIRECT = 10
ORDERS = (("x", "y", "z"), ("y", "z", "x"), ("z", "x", "y"))


def my_place():
    b = lax.axis_index("batch")
    return {"z": b // 8, "x": lax.rem(b // 2, 4), "c": lax.rem(b, 2), "y": lax.axis_index("tile")}


def device_at(place):
    return {"batch": (place["z"] * 4 + place["x"]) * 2 + place["c"], "tile": place["y"]}


def neighbour(place, axis, step):
    there = dict(place)
    if axis == "c":
        there["c"] = 1 - place["c"]
    else:
        there[axis] = lax.rem(place[axis] + step + 4, 4)
    return device_at(there)


GROUP = tuple((flip, step) for flip in (0, 1) for step in range(4) if flip or step)
VECTORS = tuple((768 * k, 768, 6) for k in range(6)) + ((4608, 1536, 12), (6144, 3072, 24))


CHIPS = sorted(
    ((z, x, y) for z in range(4) for x in range(4) for y in range(4) if z or x or y),
    key=lambda steps: -sum(min(step, 4 - step) for step in steps),
)


def for_other_chips(place, job):
    for steps in CHIPS:
        there = dict(place)
        for axis, step in zip("zxy", steps):
            there[axis] = lax.rem(place[axis] + step, 4)
        job(device_at(there))


def in_group(place, flip, step):
    there = dict(place)
    there["c"] = lax.rem(place["c"] + flip, 2)
    there["y"] = lax.rem(place["y"] + step, 4)
    return device_at(there)


def gelu_parts(inner):
    half = 0.5 * (1.0 + lax.erf(inner * 0.7071067811865476))
    return inner * half, half


def lanes_of(j, width):
    return pl.ds(pl.multiple_of(j * width, width), width)


def rows_of(i, height):
    return pl.ds(pl.multiple_of(i * height, height), height)


NT = (((1,), (1,)), ((), ()))
TN = (((0,), (0,)), ((), ()))


def head_halves(pair):
    first = lax.broadcasted_iota(jnp.int32, pair.shape, 1) < 64
    nothing = jnp.zeros_like(pair)
    return jnp.concatenate([jnp.where(first, pair, nothing), jnp.where(first, nothing, pair)], axis=0)


def pair_probs(q, k, keymask):
    scores = lax.dot_general(head_halves(q * 0.125), k, NT, preferred_element_type=f32) + keymask
    expo = jnp.exp(scores - jnp.max(scores, axis=1, keepdims=True))
    return expo * (1.0 / jnp.sum(expo, axis=1, keepdims=True))


def whole_kernel(
    count_ref, companion_ref, widths_ref, divisor_ref,
    bq_ref, bo_ref, g1_ref, t1_ref, bu_ref, bd_ref, g2_ref, t2_ref,
    x_ref, wq_ref, wo_ref, wu_ref, wd_ref, perm_ref, spread_ref,
    out_hbm, vec_hbm, loss_hbm, emb_hbm, dx_ref,
    qkv_keep, ctx_keep, n1_keep, r1_keep, inner_keep, n2_keep, r2_keep,
    weight, perm, xb, qkv, ctx, n1, r1, inner, n2, r2, grad, d_outer, d_att, d_ctx, act_t, d_inner, d_qkv, vectors, apt,
    vq, vo, v1, t1, vu, vd, v2, t2, pool, d_emb, every, out_ref, vec_out_ref, loss_row,
    got0, got1a, got1b, half2, got2a, got2b, half3, got3a, got3b, rows24, got2d, got3d,
    vec_src, vec_z, vec_x, vec_mid, vec_cy,
    weight_sem, keep_sem, load_sem, table_sem, every_s, every_r, swap_s, swap_r,
    sems_s, sems_r, sem0_s, sem0_r, direct_s, direct_r, vec_s, vec_r,
):
    place = my_place()
    core = place["c"]
    half = send = None


    kept = {
        "qkv": (qkv, qkv_keep, 0), "ctx": (ctx, ctx_keep, 1), "n1": (n1, n1_keep, 2), "r1": (r1, r1_keep, 3),
        "inner": (inner, inner_keep, 4), "n2": (n2, n2_keep, 5), "r2": (r2, r2_keep, 6),
    }

    def keep(name):
        here, there, k = kept[name]
        return pltpu.make_async_copy(here, there, keep_sem.at[k])

    def load(name):
        if name == "xb":
            return pltpu.make_async_copy(x_ref.at[0], xb, load_sem.at[7])
        here, there, k = kept[name]
        return pltpu.make_async_copy(there, here, load_sem.at[k])

    def weights(k, layer, slot, extra=None):
        blocks = []
        for m in range(4):
            cols = pl.ds(768 * m, 768)
            if k == 0:
                src = wd_ref.at[layer, cols]
            elif k == 1:
                src = wu_ref.at[layer, :, cols]
            else:
                src = wq_ref.at[layer, :, cols] if m < 3 else wo_ref.at[layer]
            dst, sem = (weight.at[slot, cols], weight_sem.at[slot, m]) if extra is None else (extra.at[slot, cols], weight_sem.at[2 + slot, m])
            blocks.append(pltpu.make_async_copy(src, dst, sem))
        return blocks

    def fetch_weights(*use):
        for copy in weights(*use):
            copy.start()

    def ready_weights(*use):
        for copy in weights(*use):
            copy.wait()

    def back_slot(k, layer):
        return lax.rem((1 - layer) * 3 + k + 1, 2)

    load("xb").start()
    perm_copy = pltpu.make_async_copy(perm_ref, perm, table_sem.at[0])
    spread_copy = pltpu.make_async_copy(spread_ref, weight.at[1, pl.ds(0, 1536)], table_sem.at[1])

    barrier = pltpu.get_barrier_semaphore()
    for_other_chips(place, lambda there: pl.semaphore_signal(barrier, inc=1, device_id=there, device_id_type=MESH))
    for flip, step in GROUP:
        pl.semaphore_signal(barrier, inc=1, device_id=in_group(place, flip, step), device_id_type=MESH)

    for src, dst in ((bo_ref, vo), (g1_ref, v1), (t1_ref, t1), (bu_ref, vu), (bd_ref, vd), (g2_ref, v2), (t2_ref, t2)):
        for layer in range(2):
            dst[layer] = src[layer : layer + 1, :].astype(f32)
    for layer in range(2):
        vq[layer, :, 0:768] = bq_ref[layer : layer + 1, 0:768].astype(f32)
        vq[layer, :, 768:1536] = jnp.zeros((1, 768), f32)
        vq[layer, :, 1536:2304] = bq_ref[layer : layer + 1, 768:1536].astype(f32)
    count = count_ref[0]
    keymask = jnp.where(lax.broadcasted_iota(jnp.int32, (1, 256), 1) < count, 0.0, -1e9)


    chip = (place["z"] * 4 + place["x"]) * 4 + place["y"]

    def gather_start(e):
        for r in range(6):
            every[e, core, chip, r : r + 1, :] = pool[e, :, 128 * r : 128 * r + 128]
        mine = every.at[e, core, chip]
        for_other_chips(place, lambda there: pltpu.make_async_remote_copy(
            src_ref=mine, dst_ref=mine, send_sem=every_s.at[e], recv_sem=every_r.at[e], device_id=there, device_id_type=MESH
        ).start())

    def swap_copy(e):
        mine = every.at[e, core]
        return pltpu.make_async_remote_copy(
            src_ref=mine, dst_ref=mine, send_sem=swap_s.at[e], recv_sem=swap_r.at[e],
            device_id=neighbour(place, "c", 1), device_id_type=MESH,
        )

    def gather_swap(e):
        others = every.at[e, core, pl.ds(0, 63)]
        pltpu.make_async_copy(others, others, every_r.at[e]).wait()
        swap_copy(e).start()

    def gather_end(e):
        others = every.at[e, core, pl.ds(0, 63)]
        pltpu.make_async_copy(others, others, every_s.at[e]).wait()
        swap_copy(e).wait()


    def norm(z, layer, normed_ref, scaled_ref, gain, shift, rows):
        center = z - jnp.mean(z, axis=1, keepdims=True)
        scaled = lax.rsqrt(jnp.mean(center * center, axis=1, keepdims=True) + eps_norm)
        normed = center * scaled
        normed_ref[rows, :] = normed
        scaled_ref[rows, :] = scaled
        return normed * gain[layer] + shift[layer]

    def forward_layer(layer, extra):
        is_first, is_last = layer == 0, layer == 1
        use_q, use_u, use_d = (2, layer, 0, extra), (1, layer, 1, extra), (0, layer, layer)

        @pl.when(is_last)
        def _():
            pl.semaphore_wait(barrier, 70)
            gather_start(0)

        def free(*names):
            @pl.when(is_last)
            def _():
                for name in names:
                    keep(name).wait()

        def store(*names):
            @pl.when(is_first)
            def _():
                for name in names:
                    keep(name).start()

        @pl.when(is_first)
        def _():
            load("xb").wait()
            grad[...] = xb[...].astype(f32)

        @pl.when(is_last)
        def _():
            xb[...] = grad[...].astype(bf16)

        free("qkv")
        blocks = weights(*use_q)
        for m in range(3):
            cols = pl.ds(768 * m, 768)
            blocks[m].wait()
            mixed = jnp.dot(xb[...], extra[0, cols, :], preferred_element_type=f32) + vq[layer, :, cols]
            qkv[:, cols] = mixed.astype(bf16)
        store("qkv")

        @pl.when(is_first)
        def _():
            fetch_weights(1, 0, 1, extra)
            fetch_weights(0, 0, 0)

        @pl.when(is_last)
        def _():
            perm_copy.start()

        free("ctx")

        def attend(pair, _):
            q, k, v = (qkv[:, lanes_of(pair + 6 * third, 128)] for third in range(3))
            probs = pair_probs(q, k, keymask).astype(bf16)
            both = jnp.dot(probs, v, preferred_element_type=f32)
            first = lax.broadcasted_iota(jnp.int32, (256, 128), 1) < 64
            ctx[:, lanes_of(pair, 128)] = jnp.where(first, both[:256], both[256:]).astype(bf16)
            return 0

        lax.fori_loop(0, 6, attend, 0, unroll=6)
        store("ctx")

        @pl.when(is_last)
        def _():
            gather_swap(0)

        blocks[3].wait()
        grad[...] += jnp.dot(ctx[...], extra[0, 2304:3072, :], preferred_element_type=f32) + vo[layer]

        @pl.when(is_first)
        def _():
            fetch_weights(2, 1, 0, extra)
            fetch_weights(0, 1, 1)

        free("n1", "r1", "n2", "r2")

        def norm_one(i, _):
            rows = rows_of(i, 64)
            mid = norm(grad[rows, :], layer, n1, r1, v1, t1, rows)
            n2[rows, :] = mid
            d_att[rows, :] = mid.astype(bf16)
            return 0

        lax.fori_loop(0, 4, norm_one, 0, unroll=4)
        store("n1", "r1")
        free("inner")
        blocks = weights(*use_u)
        for m in range(4):
            cols = pl.ds(768 * m, 768)
            blocks[m].wait()
            value = jnp.dot(d_att[...], extra[1, cols, :], preferred_element_type=f32) + vu[layer, :, cols]
            inner[:, cols] = value
            d_inner[:, cols] = gelu_parts(value)[0].astype(bf16)
        store("inner")

        @pl.when(is_first)
        def _():
            fetch_weights(1, 1, 1, extra)

        ready_weights(*use_d)
        n2[...] += jnp.dot(d_inner[...], weight[layer], preferred_element_type=f32) + vd[layer]

        @pl.when(is_first)
        def _():
            fetch_weights(1, 1, 0)

        def norm_two(i, total):
            rows = rows_of(i, 64)
            result = norm(n2[rows, :], layer, n2, r2, v2, t2, rows)
            grad[rows, :] = result
            spot = lax.broadcasted_iota(jnp.int32, (64, 1), 0) + i * 64
            return total + jnp.sum(jnp.where(spot < count, result, 0.0), axis=0, keepdims=True)

        total = lax.fori_loop(0, 4, norm_two, jnp.zeros((1, 768), f32), unroll=4)
        pool[layer] = total / count.astype(f32)
        store("n2", "r2")

        @pl.when(is_last)
        def _():
            gather_end(0)


    def pairing(e, loss):
        me = ((place["z"] * 4 + place["x"]) * 2 + core) * 4 + place["y"]
        row = lax.broadcasted_iota(jnp.int32, (128, 128), 0)
        col = lax.broadcasted_iota(jnp.int32, (128, 128), 1)
        rows = lax.broadcasted_iota(jnp.int32, (128, 1), 0)
        lane = lax.broadcasted_iota(jnp.int32, (1, 768), 1)
        companion = companion_ref[...]
        divisor = divisor_ref[0]
        partner = (row == companion).astype(f32)
        mine = jnp.sum(jnp.where(lax.broadcasted_iota(jnp.int32, (1, 128), 1) == me, companion, 0), axis=1, keepdims=True)
        chosen = (rows == mine).astype(f32)
        is_me = rows == me
        gathered = jnp.concatenate([every[e, c].reshape(16, 1, 4, 6, 128) for c in range(2)], axis=1).reshape(128, 6, 128)
        embed = jnp.concatenate(
            [gathered[:, r, :] for r in range(6)], axis=1
        )
        high = embed.astype(bf16)
        low = (embed - high.astype(f32)).astype(bf16)
        own = pool[e]
        total = jnp.zeros((1, 768), f32)
        for p in range(4):
            keep_p = (lane < widths_ref[p]).astype(f32)
            keep_low = keep_p.astype(bf16)
            high_p, low_p = high * keep_low, low * keep_low
            gram = (
                lax.dot_general(high_p, high, NT, preferred_element_type=f32)
                + lax.dot_general(high_p, low, NT, preferred_element_type=f32)
                + lax.dot_general(low_p, high, NT, preferred_element_type=f32)
            )
            diagonal = jnp.where(row == col, gram, 0.0)
            inverse = lax.rsqrt(jnp.sum(diagonal, axis=1, keepdims=True) + eps_norm)
            inverse_row = lax.rsqrt(jnp.sum(diagonal, axis=0, keepdims=True) + eps_norm)
            sims = gram * inverse * inverse_row / divisor
            sims = jnp.where(row == col, -1e30, sims)
            top = jnp.max(sims, axis=1, keepdims=True)
            lse = top + jnp.log(jnp.sum(jnp.exp(sims - top), axis=1, keepdims=True))
            loss = loss + (lse - jnp.sum(sims * partner, axis=1, keepdims=True))
            to_me = jnp.sum(jnp.where(col == me, sims, 0.0), axis=1, keepdims=True)
            lse_me = jnp.sum(jnp.where(is_me, lse, 0.0), axis=0, keepdims=True)
            weight_j = jnp.exp(to_me - lse_me) + jnp.exp(to_me - lse) - 2.0 * chosen
            dunit = jnp.sum(embed * (weight_j * inverse), axis=0, keepdims=True) * keep_p
            inverse_me = jnp.sum(jnp.where(is_me, inverse, 0.0), axis=0, keepdims=True)
            unit_me = own * keep_p * inverse_me
            inside = dunit - unit_me * jnp.sum(unit_me * dunit, axis=1, keepdims=True)
            total = total + inside * inverse_me
        d_emb[e] = total / (8.0 * divisor)
        return loss


    def norm_back(normed, scaled, gain, rounded, at_gain, at_shift, at_bias, layer):
        sums = [jnp.zeros((1, 768), f32) for _ in range(3)]
        for i in range(4):
            rows = pl.ds(64 * i, 64)
            dy, n = grad[rows, :], normed[rows, :]
            dn = dy * gain
            inside = dn - jnp.mean(dn, axis=1, keepdims=True) - n * jnp.mean(dn * n, axis=1, keepdims=True)
            dz = scaled[rows, :] * inside
            low = dz.astype(bf16)
            grad[rows, :] = dz
            rounded[rows, :] = low
            for k, term in enumerate((dy * n, dy, low.astype(f32))):
                sums[k] = sums[k] + jnp.sum(term, axis=0, keepdims=True)
        for at, total in zip((at_gain, at_shift, at_bias), sums):
            vectors[layer, :, at : at + 768] = total

    def turn_active():
        def turn(j, _):
            value = inner[:, lanes_of(j, 256)]
            act_t[lanes_of(j, 256), :] = gelu_parts(value)[0].T.astype(bf16)
            return 0

        lax.fori_loop(0, 12, turn, 0, unroll=2)

    def permute(operand, which):
        def one(o, _):
            apt[o, which] = lax.dot_general(perm[o], operand, NT, preferred_element_type=f32).astype(bf16)
            return 0

        lax.fori_loop(0, 3, one, 0, unroll=3)

    def begin_layer(layer):
        spots = lax.broadcasted_iota(jnp.int32, (256, 1), 0)
        pooled = jnp.where(spots < count, 1.0, 0.0) / count.astype(f32)

        @pl.when(layer == 1)
        def _():
            grad[...] = pooled * d_emb[1]

        @pl.when(layer == 0)
        def _():
            grad[...] += pooled * d_emb[0]
            load("n2").wait()
            load("r2").wait()
            load("inner").wait()
            turn_active()

        norm_back(n2, r2, v2[layer], d_outer, 3072, 3840, 2304, layer)

        @pl.when(layer == 1)
        def _():
            load("n2").start()
            load("r2").start()

    def through_expand(layer):
        slot = back_slot(0, layer)

        @pl.when(layer == 0)
        def _():
            ready_weights(0, 0, slot)

        def chunk(j, _):
            cols = lanes_of(j, 512)
            d_act = lax.dot_general(d_outer[...], weight[slot, cols, :], NT, preferred_element_type=f32)
            value = inner[:, cols]
            slope = gelu_parts(value)[1] + value * (jnp.exp(-0.5 * value * value) * 0.3989422804014327)
            low = (d_act * slope).astype(bf16)
            d_inner[:, cols] = low
            at = pl.ds(pl.multiple_of(6144 + j * 512, 512), 512)
            vectors[layer, :, at] = jnp.sum(low.astype(f32), axis=0, keepdims=True)
            return 0

        lax.fori_loop(0, 6, chunk, 0, unroll=2)
        fetch_weights(2, layer, slot)

        @pl.when(layer == 1)
        def _():
            load("inner").start()

        @pl.when(layer == 0)
        def _():
            load("n1").wait()
            load("r1").wait()
            permute((n1[...] * v1[0] + t1[0]).astype(bf16), 0)

    def through_mixer(layer):
        slot = back_slot(1, layer)

        @pl.when(layer == 0)
        def _():
            ready_weights(1, 0, slot)

        @pl.when(layer == 1)
        def _():
            ready_weights(1, 1, slot)

        for m in range(4):
            cols = pl.ds(768 * m, 768)
            grad[...] += lax.dot_general(d_inner[:, cols], weight[slot, cols, :], NT, preferred_element_type=f32)
        norm_back(n1, r1, v1[layer], d_att, 768, 1536, 0, layer)

        @pl.when(layer == 1)
        def _():
            fetch_weights(0, 0, slot)
            load("n1").start()
            load("r1").start()

        slot = back_slot(2, layer)
        ready_weights(2, layer, slot)
        d_ctx[...] = lax.dot_general(d_att[...], weight[slot, 2304:3072, :], NT, preferred_element_type=f32).astype(bf16)

    def through_attention(layer, first_pair, pairs):
        def pair_back(i, _):
            pair = first_pair + i
            at = [lanes_of(pair + 6 * third, 128) for third in range(3)]
            q, k, v = (qkv[:, cols] for cols in at)
            probs = pair_probs(q, k, keymask)
            dc = head_halves(d_ctx[:, at[0]])
            dp = lax.dot_general(dc, v, NT, preferred_element_type=f32)
            ds = (probs * (dp - jnp.sum(dp * probs, axis=1, keepdims=True))).astype(bf16)
            dq = jnp.dot(
                jnp.concatenate([ds[:256], ds[256:]], axis=1), head_halves(k * 0.125), preferred_element_type=f32
            ).astype(bf16)
            dk = lax.dot_general(ds, head_halves(q * 0.125), TN, preferred_element_type=f32).astype(bf16)
            dv = lax.dot_general(probs.astype(bf16), dc, TN, preferred_element_type=f32).astype(bf16)
            for cols, value in zip(at, (dq, dk, dv)):
                d_qkv[:, cols] = value
            for start, value in ((4608, dq), (5376, dv)):
                where = pl.ds(pl.multiple_of(start + pair * 128, 128), 128)
                vectors[layer, :, where] = jnp.sum(value.astype(f32), axis=0, keepdims=True)
            return 0

        lax.fori_loop(0, pairs, pair_back, 0, unroll=2)

    def through_projection(layer):
        slot = back_slot(2, layer)
        for m in range(3):
            cols = pl.ds(768 * m, 768)
            grad[...] += lax.dot_general(d_qkv[:, cols], weight[slot, cols, :], NT, preferred_element_type=f32)

        @pl.when(layer == 1)
        def _():
            fetch_weights(1, 0, slot)
            load("qkv").start()

        @pl.when(layer == 0)
        def _():
            dx_copy.start()

    dx_copy = pltpu.make_async_copy(grad, dx_ref.at[0], table_sem.at[2])
    emb_copy = pltpu.make_async_copy(pool, emb_hbm, table_sem.at[3])
    loss_copy = pltpu.make_async_copy(loss_row, loss_hbm, table_sem.at[4])
    out_copy = pltpu.make_async_copy(out_ref, out_hbm, table_sem.at[5])
    vec_copy = pltpu.make_async_copy(vec_out_ref, vec_hbm, table_sem.at[6])

    def store_rows(o, slot, mine, tile0, value):
        for j in range(value.shape[1] // 128):
            part = value[:, 128 * j : 128 * (j + 1)].reshape(16, 3, 8, 128)
            if mine:
                half[o, slot, :, tile0 + 3 * j : tile0 + 3 * j + 3] = part
            else:
                send[o, :, tile0 + 3 * j : tile0 + 3 * j + 3] = part

    def product(mine, slot, uses):
        c = core if mine else 1 - core

        def one(o, _):
            for which, ref, start, width, tile0 in uses:
                lhs = apt[o, which, pl.ds(pl.multiple_of(c * 384, 128), 384), :]
                for w in range(0, width, 256):
                    cols = pl.ds(pl.multiple_of(start(o) + w, 256), 256)
                    value = jnp.dot(lhs, ref[:, cols], preferred_element_type=f32)
                    store_rows(o, slot, mine, tile0 + 3 * (w // 128), value)
            return 0

        lax.fori_loop(0, 3, one, 0, unroll=3)

    def product_shrink(mine, slot, k):
        def block(z, _):
            c = core if mine else 1 - core
            lhs = jnp.concatenate(
                [act_t[pl.ds(pl.multiple_of(z * 768 + x * 192 + c * 96, 32), 96), :] for x in range(4)], axis=0
            )
            value = jnp.dot(lhs, d_outer[:, pl.ds(pl.multiple_of(384 * k, 128), 384)], preferred_element_type=f32)
            for x in range(4):
                for y in range(4):
                    for j in range(3):
                        p = {"x": x, "y": y, "z": z}
                        d1, d2, d3 = (p[axis] for axis in ORDERS[j])
                        row = x * 96 + (y * 3 + j) * 8
                        for ct in range(3):
                            tile = value[row : row + 8, 128 * ct : 128 * ct + 128]
                            if mine:
                                half[j, slot, d1 * 4 + d2, d3 * 3 + ct] = tile
                            else:
                                send[j, d1 * 4 + d2, d3 * 3 + ct] = tile
            return 0

        lax.fori_loop(0, 4, block, 0)

    def make(u):
        slot = lax.rem(u, 4)
        layer = 1 - u // 6
        kind = lax.rem(u, 6)

        def both_halves(job):
            job(False)
            for o in range(3):
                copy0(o, u).start()
            job(True)

        @pl.when(kind == 0)
        def _():
            begin_layer(layer)

        @pl.when(kind < 2)
        def _():
            both_halves(lambda mine: product_shrink(mine, slot, kind))

        @pl.when((kind == 2) | (kind == 3))
        def _():
            both_halves(lambda mine: product(mine, slot, [(0, d_inner, lambda o: (kind - 2) * 1536 + o * 512, 512, 0)]))

        @pl.when(kind == 4)
        def _():
            both_halves(lambda mine: product(mine, slot, [(0, d_qkv, lambda o: o * 768, 512, 0)]))

        @pl.when(kind == 5)
        def _():
            both_halves(lambda mine: product(
                mine, slot, [(0, d_qkv, lambda o: o * 768 + 512, 256, 0), (1, d_att, lambda o: o * 256, 256, 6)]
            ))

    def follow(u):
        layer = 1 - u // 6
        kind = lax.rem(u, 6)

        @pl.when(kind == 1)
        def _():
            through_expand(layer)

        @pl.when(kind == 2)
        def _():
            through_mixer(layer)

        @pl.when(kind == 3)
        def _():
            @pl.when(layer == 0)
            def _():
                load("xb").wait()
                load("ctx").wait()

            permute(xb[...], 0)
            permute(ctx[...], 1)

            @pl.when(layer == 1)
            def _():
                load("xb").start()
                load("ctx").start()

            @pl.when(layer == 0)
            def _():
                load("qkv").wait()

            through_attention(layer, 0, 4)

        @pl.when(kind == 4)
        def _():
            through_attention(layer, 4, 2)
            through_projection(layer)


    def exchange(o, k, slot, src_up, src_down, got):
        axis = ORDERS[o][k // 2]
        copies = [
            pltpu.make_async_remote_copy(
                src_ref=src, dst_ref=got.at[o, slot, way], send_sem=sems_s.at[o, k, slot], recv_sem=sems_r.at[o, k, slot],
                device_id=neighbour(place, axis, step), device_id_type=MESH,
            )
            for way, (src, step) in enumerate(((src_up, 1), (src_down, -1)))
        ]
        return copies, got.at[o, slot], sems_s.at[o, k, slot], sems_r.at[o, k, slot]

    def begin(exchanged):
        for copy in exchanged[0]:
            copy.start()

    def end(exchanged):
        _, landed, sent_sem, landed_sem = exchanged
        pltpu.make_async_copy(landed, landed, sent_sem).wait()
        pltpu.make_async_copy(landed, landed, landed_sem).wait()

    def spots(o, phase):
        a = place[ORDERS[o][phase]]
        return a, lax.rem(a + 1, 4), lax.rem(a + 2, 4), lax.rem(a + 3, 4)

    def copy0(o, u):
        slot = lax.rem(u, 2)
        return pltpu.make_async_remote_copy(
            src_ref=send.at[o], dst_ref=got0.at[o, slot], send_sem=sem0_s.at[o], recv_sem=sem0_r.at[o, slot],
            device_id=neighbour(place, "c", 1), device_id_type=MESH,
        )

    def step_a(o, phase, u):
        slot = lax.rem(u, SLOTS)
        a, up, far, down = spots(o, phase)
        if phase == 0:
            src, got = (half.at[o, lax.rem(u, 4), pl.ds(far * 4, 2)], half.at[o, lax.rem(u, 4), pl.ds(far * 4 + 2, 2)]), got1a
        elif phase == 1:
            src, got = (half2.at[o, slot, far, pl.ds(0, 6)], half2.at[o, slot, far, pl.ds(6, 6)]), got2a
        else:
            src, got = (half3.at[o, slot, far, pl.ds(0, 2)], half3.at[o, slot, far, pl.ds(2, 2)]), got3a
        return exchange(o, 2 * phase, slot, src[0], src[1], got)

    def step_b(o, phase, u):
        slot = lax.rem(u, SLOTS)
        a, up, far, down = spots(o, phase)
        if phase == 0:
            src, got = (half.at[o, lax.rem(u, 4), pl.ds(up * 4, 4)], half.at[o, lax.rem(u, 4), pl.ds(down * 4, 4)]), got1b
        elif phase == 1:
            src, got = (half2.at[o, slot, up], half2.at[o, slot, down]), got2b
        else:
            src, got = (half3.at[o, slot, up], half3.at[o, slot, down]), got3b
        return exchange(o, 2 * phase + 1, slot, src[0], src[1], got)

    def add_a(o, phase, u):
        slot = lax.rem(u, SLOTS)
        a, up, far, down = spots(o, phase)
        if phase == 0:
            for i in range(2):
                half[o, lax.rem(u, 4), up * 4 + i] += got1a[o, slot, 0, i]
                half[o, lax.rem(u, 4), down * 4 + 2 + i] += got1a[o, slot, 1, i]
        elif phase == 1:
            half2[o, slot, up, 0:6] += got2a[o, slot, 0]
            half2[o, slot, down, 6:12] += got2a[o, slot, 1]
        else:
            half3[o, slot, up, 0:2] += got3a[o, slot, 0]
            half3[o, slot, down, 2:4] += got3a[o, slot, 1]

    def add_b(o, phase, u):
        slot = lax.rem(u, SLOTS)
        a, up, far, down = spots(o, phase)
        if phase == 0:
            for i in range(4):
                half2[o, slot, i] = half[o, lax.rem(u, 4), a * 4 + i] + got1b[o, slot, 0, i] + got1b[o, slot, 1, i]
        elif phase == 1:
            to_third(o, slot, u, half2[o, slot, a] + got2b[o, slot, 0] + got2b[o, slot, 1])
        else:
            out_ref[u, o] = half3[o, slot, a] + got3b[o, slot, 0] + got3b[o, slot, 1]

    def to_third(o, slot, u, total):
        @pl.when(lax.rem(u, 6) < 2)
        def _():
            for k in range(4):
                half3[o, slot, k, 0:3] = total[3 * k : 3 * k + 3]

        @pl.when(lax.rem(u, 6) >= 2)
        def _():
            for ct in range(4):
                rows24[o, ct] = total[3 * ct : 3 * ct + 3].reshape(24, 128)
            for k in range(4):
                for ct in range(4):
                    half3[o, slot, k, ct, 0:6, :] = rows24[o, ct, 6 * k : 6 * k + 6, :]

    def direct(o, phase, u):
        slot, way = lax.rem(u, SLOTS), lax.rem(u, 2)
        a = place[ORDERS[o][phase]]
        src, got = ((half2, got2d), (half3, got3d))[phase - 1]
        copies = [
            pltpu.make_async_remote_copy(
                src_ref=src.at[o, slot, lax.rem(a + step, 4)], dst_ref=got.at[o, way, step - 1],
                send_sem=direct_s.at[o, phase - 1, way], recv_sem=direct_r.at[o, phase - 1, way],
                device_id=neighbour(place, ORDERS[o][phase], step), device_id_type=MESH,
            )
            for step in (1, 2, 3)
        ]
        return copies, got.at[o, way], direct_s.at[o, phase - 1, way], direct_r.at[o, phase - 1, way]

    def direct_second(u):
        slot, way = lax.rem(u, SLOTS), lax.rem(u, 2)
        for o in range(3):
            end(direct(o, 1, u))
            total = half2[o, slot, place[ORDERS[o][1]]]
            for i in range(3):
                total += got2d[o, way, i]
            to_third(o, slot, u, total)
            begin(direct(o, 2, u))

    def direct_third(u):
        slot, way = lax.rem(u, SLOTS), lax.rem(u, 2)
        for o in range(3):
            end(direct(o, 2, u))
            total = half3[o, slot, place[ORDERS[o][2]]]
            for i in range(3):
                total += got3d[o, way, i]
            out_ref[u, o] = total

    def spread_vectors(layer):
        total = jnp.zeros((128, 128), f32)
        for start, width, keep in VECTORS:
            d = lax.broadcasted_iota(jnp.int32, (128, width), 0) * keep
            q = lax.broadcasted_iota(jnp.int32, (128, width), 1)
            own = jnp.where((q >= d) & (q < d + keep), vectors[layer, :, start : start + width], 0.0)
            high = own.astype(bf16)
            low = (own - high.astype(f32)).astype(bf16)
            for part in range(width // 768):
                k = start // 768 + part
                lanes = weight[1, 768 * (k // 6) : 768 * (k // 6 + 1), 128 * (k % 6) : 128 * (k % 6 + 1)]
                at = slice(768 * part, 768 * (part + 1))
                total += jnp.dot(high[:, at], lanes, preferred_element_type=f32)
                total += jnp.dot(low[:, at], lanes, preferred_element_type=f32)
        total = total.reshape(4, 4, 8, 128)
        for z in range(4):
            for x in range(4):
                vec_src[z, x, layer] = total[z, x]

    def vector_copies(k, landed, pieces):
        copies = [
            pltpu.make_async_remote_copy(
                src_ref=src, dst_ref=landed.at[i], send_sem=vec_s.at[k], recv_sem=vec_r.at[k], device_id=device, device_id_type=MESH
            )
            for i, (src, device) in enumerate(pieces)
        ]
        return copies, landed, vec_s.at[k], vec_r.at[k]

    def copies_z():
        return vector_copies(0, vec_z, [(vec_src.at[lax.rem(place["z"] + i, 4)], neighbour(place, "z", i)) for i in (1, 2, 3)])

    def copies_x():
        mine = place["z"]
        return vector_copies(1, vec_x, [(vec_src.at[mine, lax.rem(place["x"] + i, 4)], neighbour(place, "x", i)) for i in (1, 2, 3)])

    def copies_group():
        return vector_copies(2, vec_cy, [(vec_mid, in_group(place, flip, step)) for flip, step in GROUP])

    def vectors_first():
        spread_copy.wait()
        spread_vectors(1)

    def vectors_start():
        spread_vectors(0)
        begin(copies_z())

    def vectors_second():
        end(copies_z())
        for x in range(4):
            vec_src[place["z"], x] += vec_z[0, x] + vec_z[1, x] + vec_z[2, x]
        begin(copies_x())

    def vectors_third():
        end(copies_x())
        vec_mid[...] = vec_src[place["z"], place["x"]] + vec_x[0] + vec_x[1] + vec_x[2]
        begin(copies_group())

    def vectors_last():
        end(copies_group())
        total = vec_mid[...]
        for i in range(7):
            total += vec_cy[i]
        mine = lax.broadcasted_iota(jnp.int32, (2, 8, 128), 1) == core * 4 + place["y"]
        vec_out_ref[...] = jnp.sum(jnp.where(mine, total, 0.0), axis=1)

    def when(u, first, last, job):
        @pl.when((u >= first) & (u < last))
        def _():
            job(u)

    def enter(u):
        slot = lax.rem(u, SLOTS)
        for o in range(3):
            copy0(o, u).wait()

            def add(i, _):
                half[o, lax.rem(u, 4), i] += got0[o, lax.rem(u, 2), i]
                return 0

            lax.fori_loop(0, 16, add, 0)
            begin(step_a(o, 0, u))

    def second(phase):
        def job(u):
            for o in range(3):
                end(step_a(o, phase, u))
                add_a(o, phase, u)
                begin(step_b(o, phase, u))
        return job

    def third(phase):
        def job(u):
            for o in range(3):
                end(step_b(o, phase, u))
                add_b(o, phase, u)
                if phase == 0:
                    @pl.when(u < DIRECT)
                    def _():
                        begin(step_a(o, 1, u))

                    @pl.when(u >= DIRECT)
                    def _():
                        begin(direct(o, 1, u))
                elif phase == 1:
                    begin(step_a(o, 2, u))
        return job

    def tick(u, _):
        when(u, 0, TRIPLES, make)
        when(u - 3, 0, TRIPLES, third(0))
        when(u - 4, 0, DIRECT, second(1))
        when(u - 5, 0, DIRECT, third(1))
        when(u - 6, 0, DIRECT, second(2))
        when(u - 7, 0, DIRECT, third(2))
        when(u - 4, DIRECT, TRIPLES, direct_second)
        when(u - 5, DIRECT, TRIPLES, direct_third)
        when(u, 0, TRIPLES, enter)
        when(u - 1, 0, TRIPLES, second(0))
        when(u, 0, TRIPLES, follow)

        for k, job in ((8, spread_copy.start), (9, vectors_first), (11, vectors_start), (12, vectors_second), (13, vectors_third), (14, vectors_last)):
            pl.when(u == k)(job)
        return 0


    def forward_both(extra):
        fetch_weights(2, 0, 0, extra)

        def layer_step(layer, _):
            forward_layer(layer, extra)
            return 0

        lax.fori_loop(0, 2, layer_step, 0)
        gather_start(1)

    pl.run_scoped(forward_both, pltpu.VMEM((2, 3072, 768), bf16))
    emb_copy.start()
    half3[...] = jnp.zeros_like(half3)

    def layer_loss(e, loss):
        @pl.when(e == 1)
        def _():
            turn_active()
            gather_swap(1)
            perm_copy.wait()
            permute(d_att[...], 0)
            gather_end(1)

        return pairing(e, loss)

    loss_row[...] = lax.fori_loop(0, 2, layer_loss, jnp.zeros((128, 1), f32)) / 8.0
    loss_copy.start()

    def reduce_all(half_ref, send_ref):
        nonlocal half, send
        half, send = half_ref, send_ref
        lax.fori_loop(0, DIRECT + 7, tick, 0)

    pl.run_scoped(reduce_all, pltpu.VMEM((3, 4, 16, 12, 8, 128), f32), pltpu.VMEM((3, 16, 12, 8, 128), f32))
    out_copy.start()
    vec_copy.start()
    for copy in (dx_copy, emb_copy, loss_copy, out_copy, vec_copy):
        copy.wait()


def permutations():
    rows = np.arange(768).reshape(4, 4, 2, 4, 6)
    names = {"z": 0, "x": 1, "c": 2, "y": 3}
    out = np.zeros((3, 768, 768), np.float32)
    for o, (d1, d2, d3) in enumerate(ORDERS):
        taken = rows.transpose(2, names[d1], names[d2], names[d3], 4).reshape(-1)
        out[o, np.arange(768), taken] = 1
    return out.astype(ml_dtypes.bfloat16)


def lane_places():
    out = np.zeros((9216, 128), np.float32)
    lane = 0
    for start, width, keep in VECTORS:
        q = np.arange(width)
        out[start + q, lane + q % keep] = 1
        lane += keep
    out = out.reshape(2, 6, 768, 128).transpose(0, 2, 1, 3).reshape(1536, 768)
    return out.astype(ml_dtypes.bfloat16)


def finish_kernel(out_hbm, vec_hbm, loss_hbm, emb_hbm, dx_hbm, *refs):
    loss_out, emb_out, dx_out, qkv_out, qv_out, mixer_out, bias_out, gain_out, shift_out, up_out, ffn_out, down_out, downbias_out, fingain_out, finshift_out = refs[:15]
    out_ref, vec_ref, loss_ref, emb_ref, dx_ref, sem = refs[15:]
    copies = [
        pltpu.make_async_copy(src, dst, sem.at[k])
        for k, (src, dst) in enumerate(((out_hbm, out_ref), (vec_hbm, vec_ref), (loss_hbm, loss_ref), (emb_hbm, emb_ref), (dx_hbm, dx_ref)))
    ]
    for copy in copies:
        copy.start()
    for copy in copies[:4]:
        copy.wait()
    for layer in range(2):
        emb_out[0, layer : layer + 1, :] = emb_ref[layer]
    copies[4].wait()
    last = pltpu.make_async_copy(dx_ref, dx_out, sem.at[4])
    last.start()
    for layer in range(2):
        first = 6 * (1 - layer)
        for k in range(2):
            for o in range(3):
                for ct in range(3):
                    down_out[layer, 8 * o : 8 * o + 8, 384 * k + 128 * ct : 384 * k + 128 * ct + 128] = out_ref[first + k, o, ct]
                for ct in range(4):
                    at = (k * 3 + o) * 512 + 128 * ct
                    up_out[:, layer, at : at + 128] = out_ref[first + 2 + k, o, ct, 0:6, :]
        for o in range(3):
            for ct in range(4):
                at = o * 768 + 128 * ct
                qkv_out[:, layer, at : at + 128] = out_ref[first + 4, o, ct, 0:6, :]
            for ct in range(2):
                at = o * 768 + 512 + 128 * ct
                qkv_out[:, layer, at : at + 128] = out_ref[first + 5, o, ct, 0:6, :]
                at = o * 256 + 128 * ct
                mixer_out[:, layer, at : at + 128] = out_ref[first + 5, o, 2 + ct, 0:6, :]
    lane = 0
    for (_, _, keep), dst in zip(
        VECTORS, (bias_out, gain_out, shift_out, downbias_out, fingain_out, finshift_out, qv_out, ffn_out)
    ):
        dst[...] = vec_ref[:, lane : lane + keep]
        lane += keep
    rows = lax.broadcasted_iota(jnp.int32, (128, 1), 0)
    for k in range(4):
        loss_out[k] = jnp.sum(jnp.where(rows == lax.axis_index("batch") * 4 + k, loss_ref[...], 0.0))
    last.wait()


def body(slots, counts, companion, widths, divisor, triple, bias_qv, mixer, bias_mixer, gain_one, shift_one, expand, bias_expand, shrink, bias_shrink, gain_two, shift_two):
    tile = (8, 128)
    vmem = pl.BlockSpec(memory_space=pltpu.VMEM)
    smem = pl.BlockSpec(memory_space=pltpu.SMEM)
    hbm = pl.BlockSpec(memory_space=pl.ANY)

    def vm(*shape, dtype=f32):
        return pltpu.VMEM(shape, dtype)

    dma = pltpu.SemaphoreType.DMA
    saved = [((256, 2304), bf16), ((256, 768), bf16), ((256, 768), f32), ((256, 1), f32), ((256, 3072), f32), ((256, 768), f32), ((256, 1), f32)]
    shapes = [((TRIPLES, 3, 4) + tile, f32), ((2, 128), f32), ((128, 1), f32), ((2, 1, 768), f32), ((1, 256, 768), f32)] + saved
    results = pl.pallas_call(
        whole_kernel,
        out_shape=[jax.ShapeDtypeStruct(s, t) for s, t in shapes],
        in_specs=[smem, vmem, smem, smem] + [vmem] * 8 + [hbm] * 7,
        out_specs=[hbm] * 12,
        scratch_shapes=[
            vm(2, 3072, 768, dtype=bf16), vm(3, 768, 768, dtype=bf16), vm(256, 768, dtype=bf16), vm(256, 2304, dtype=bf16),
            vm(256, 768, dtype=bf16), vm(256, 768), vm(256, 1), vm(256, 3072), vm(256, 768), vm(256, 1), vm(256, 768),
            vm(256, 768, dtype=bf16), vm(256, 768, dtype=bf16), vm(256, 768, dtype=bf16), vm(3072, 256, dtype=bf16),
            vm(256, 3072, dtype=bf16), vm(256, 2304, dtype=bf16), vm(2, 1, 9216), vm(3, 2, 768, 256, dtype=bf16),
            vm(2, 1, 2304), vm(2, 1, 768), vm(2, 1, 768), vm(2, 1, 768), vm(2, 1, 3072), vm(2, 1, 768), vm(2, 1, 768), vm(2, 1, 768),
            vm(2, 1, 768), vm(2, 1, 768), vm(2, 2, 64, 6, 128), vm(TRIPLES, 3, 4, *tile), vm(2, 128), vm(128, 1),
            vm(3, 2, 16, 12, *tile),
            vm(3, SLOTS, 2, 2, 12, *tile), vm(3, SLOTS, 2, 4, 12, *tile),
            vm(3, SLOTS, 4, 12, *tile), vm(3, SLOTS, 2, 6, *tile), vm(3, SLOTS, 2, 12, *tile),
            vm(3, SLOTS, 4, 4, *tile), vm(3, SLOTS, 2, 2, *tile), vm(3, SLOTS, 2, 4, *tile), vm(3, 4, 24, 128),
            vm(3, 2, 3, 12, *tile), vm(3, 2, 3, 4, *tile),
            vm(4, 4, 2, *tile), vm(3, 4, 2, *tile), vm(3, 2, *tile), vm(2, *tile), vm(7, 2, *tile),
            dma((4, 4)), dma((7,)), dma((8,)), dma((7,)), dma((2,)), dma((2,)), dma((2,)), dma((2,)),
            dma((3, 6, SLOTS)), dma((3, 6, SLOTS)), dma((3,)), dma((3, 2)), dma((3, 2, 2)), dma((3, 2, 2)),
            dma((3,)), dma((3,)),
        ],
        compiler_params=pltpu.CompilerParams(
            collective_id=1, has_side_effects=True, vmem_limit_bytes=63 * 1024 * 1024
        ),
    )(
        counts, companion[None], widths, divisor,
        bias_qv, bias_mixer, gain_one, shift_one, bias_expand, bias_shrink, gain_two, shift_two,
        slots, triple, mixer, expand, shrink, jnp.asarray(permutations()), jnp.asarray(lane_places()),
    )
    out, vec_out, loss, embeddings, dx = results[:5]
    shapes = [(4,), (1, 2, 768), (1, 256, 768), (6, 2, 2304), (2, 12), (6, 2, 768), (2, 6), (2, 6), (2, 6), (6, 2, 3072), (2, 24), (2, 24, 768), (2, 6), (2, 6), (2, 6)]
    loss, embeddings, *rest = pl.pallas_call(
        finish_kernel,
        out_shape=[jax.ShapeDtypeStruct(s, f32) for s in shapes],
        in_specs=[hbm] * 5,
        out_specs=[smem, vmem, hbm] + [vmem] * 12,
        scratch_shapes=[vm(TRIPLES, 3, 4, *tile), vm(2, 128), vm(128, 1), vm(2, 1, 768), vm(1, 256, 768), dma((5,))],
        compiler_params=pltpu.CompilerParams(vmem_limit_bytes=63 * 1024 * 1024),
    )(out, vec_out, loss, embeddings, dx)
    rest = [r.transpose(1, 0, 2) if r.shape[:2] == (6, 2) else r for r in rest]
    return (loss, embeddings, *rest)


def solution(mesh):
    return jax.shard_map(
        body,
        mesh=mesh,
        in_specs=(
            P(("batch", "tile"), None, None),
            P(("batch", "tile")),
            P(),
            P(),
            P(),
            P(),
            P(),
            P(),
            P(),
            P(),
            P(),
            P(),
            P(),
            P(),
            P(),
            P(),
            P(),
        ),
        out_specs=(
            P("batch"),
            P(("batch", "tile"), None, None),
            P(("batch", "tile"), None, None),
            P(None, ("batch", "tile"), None),
            P(None, ("batch", "tile")),
            P(None, ("batch", "tile"), None),
            P(None, ("batch", "tile")),
            P(None, ("batch", "tile")),
            P(None, ("batch", "tile")),
            P(None, ("batch", "tile"), None),
            P(None, ("batch", "tile")),
            P(None, ("batch", "tile"), None),
            P(None, ("batch", "tile")),
            P(None, ("batch", "tile")),
            P(None, ("batch", "tile")),
        ),
        check_vma=False,
    )
```

```python
import jax
import jax.numpy as jnp
import ml_dtypes
import numpy as np
from jax import lax
from jax.experimental import pallas as pl
from jax.experimental.pallas import tpu as pltpu
from jax.sharding import PartitionSpec as P

eps_norm = 1e-06

f32, bf16 = jnp.float32, jnp.bfloat16
MESH = pl.DeviceIdType.MESH
TRIPLES = 12
SLOTS = 3
DIRECT = 10
ORDERS = (("x", "y", "z"), ("y", "z", "x"), ("z", "x", "y"))


def my_place():
    b = lax.axis_index("batch")
    return {"z": b // 8, "x": lax.rem(b // 2, 4), "c": lax.rem(b, 2), "y": lax.axis_index("tile")}


def device_at(place):
    return {"batch": (place["z"] * 4 + place["x"]) * 2 + place["c"], "tile": place["y"]}


def neighbour(place, axis, step):
    there = dict(place)
    if axis == "c":
        there["c"] = 1 - place["c"]
    else:
        there[axis] = lax.rem(place[axis] + step + 4, 4)
    return device_at(there)


GROUP = tuple((flip, step) for flip in (0, 1) for step in range(4) if flip or step)
VECTORS = tuple((768 * k, 768, 6) for k in range(6)) + ((4608, 1536, 12), (6144, 3072, 24))


CHIPS = sorted(
    ((z, x, y) for z in range(4) for x in range(4) for y in range(4) if z or x or y),
    key=lambda steps: -sum(min(step, 4 - step) for step in steps),
)


def for_other_chips(place, job):
    for steps in CHIPS:
        there = dict(place)
        for axis, step in zip("zxy", steps):
            there[axis] = lax.rem(place[axis] + step, 4)
        job(device_at(there))


def in_group(place, flip, step):
    there = dict(place)
    there["c"] = lax.rem(place["c"] + flip, 2)
    there["y"] = lax.rem(place["y"] + step, 4)
    return device_at(there)


def gelu_parts(inner):
    half = 0.5 * (1.0 + lax.erf(inner * 0.7071067811865476))
    return inner * half, half


def lanes_of(j, width):
    return pl.ds(pl.multiple_of(j * width, width), width)


def rows_of(i, height):
    return pl.ds(pl.multiple_of(i * height, height), height)


NT = (((1,), (1,)), ((), ()))
TN = (((0,), (0,)), ((), ()))


def head_halves(pair):
    first = lax.broadcasted_iota(jnp.int32, pair.shape, 1) < 64
    nothing = jnp.zeros_like(pair)
    return jnp.concatenate([jnp.where(first, pair, nothing), jnp.where(first, nothing, pair)], axis=0)


def pair_probs(q, k, keymask):
    scores = lax.dot_general(head_halves(q * 0.125), k, NT, preferred_element_type=f32) + keymask
    expo = jnp.exp(scores - jnp.max(scores, axis=1, keepdims=True))
    return expo * (1.0 / jnp.sum(expo, axis=1, keepdims=True))


def whole_kernel(
    count_ref, companion_ref, widths_ref, divisor_ref,
    bq_ref, bo_ref, g1_ref, t1_ref, bu_ref, bd_ref, g2_ref, t2_ref,
    x_ref, wq_ref, wo_ref, wu_ref, wd_ref, perm_ref, spread_ref,
    out_hbm, vec_hbm, loss_hbm, emb_hbm, dx_ref,
    qkv_keep, ctx_keep, n1_keep, r1_keep, inner_keep, n2_keep, r2_keep,
    weight, perm, xb, qkv, ctx, n1, r1, inner, n2, r2, grad, d_outer, d_att, d_ctx, act_t, d_inner, d_qkv, vectors, apt,
    vq, vo, v1, t1, vu, vd, v2, t2, pool, d_emb, every, out_ref, vec_out_ref, loss_row,
    got0, got1a, got1b, half2, got2a, got2b, half3, got3a, got3b, rows24, got2d, got3d,
    vec_src, vec_z, vec_x, vec_mid, vec_cy,
    weight_sem, keep_sem, load_sem, table_sem, every_s, every_r, swap_s, swap_r,
    sems_s, sems_r, sem0_s, sem0_r, direct_s, direct_r, vec_s, vec_r,
):
    place = my_place()
    core = place["c"]
    half = send = None


    kept = {
        "qkv": (qkv, qkv_keep, 0), "ctx": (ctx, ctx_keep, 1), "n1": (n1, n1_keep, 2), "r1": (r1, r1_keep, 3),
        "inner": (inner, inner_keep, 4), "n2": (n2, n2_keep, 5), "r2": (r2, r2_keep, 6),
    }

    def keep(name):
        here, there, k = kept[name]
        return pltpu.make_async_copy(here, there, keep_sem.at[k])

    def load(name):
        if name == "xb":
            return pltpu.make_async_copy(x_ref.at[0], xb, load_sem.at[7])
        here, there, k = kept[name]
        return pltpu.make_async_copy(there, here, load_sem.at[k])

    def weights(k, layer, slot, extra=None):
        blocks = []
        for m in range(4):
            cols = pl.ds(768 * m, 768)
            if k == 0:
                src = wd_ref.at[layer, cols]
            elif k == 1:
                src = wu_ref.at[layer, :, cols]
            else:
                src = wq_ref.at[layer, :, cols] if m < 3 else wo_ref.at[layer]
            dst, sem = (weight.at[slot, cols], weight_sem.at[slot, m]) if extra is None else (extra.at[slot, cols], weight_sem.at[2 + slot, m])
            blocks.append(pltpu.make_async_copy(src, dst, sem))
        return blocks

    def fetch_weights(*use):
        for copy in weights(*use):
            copy.start()

    def ready_weights(*use):
        for copy in weights(*use):
            copy.wait()

    def back_slot(k, layer):
        return lax.rem((1 - layer) * 3 + k + 1, 2)

    load("xb").start()
    perm_copy = pltpu.make_async_copy(perm_ref, perm, table_sem.at[0])
    spread_copy = pltpu.make_async_copy(spread_ref, weight.at[1, pl.ds(0, 1536)], table_sem.at[1])

    barrier = pltpu.get_barrier_semaphore()
    for_other_chips(place, lambda there: pl.semaphore_signal(barrier, inc=1, device_id=there, device_id_type=MESH))
    for flip, step in GROUP:
        pl.semaphore_signal(barrier, inc=1, device_id=in_group(place, flip, step), device_id_type=MESH)

    for src, dst in ((bo_ref, vo), (g1_ref, v1), (t1_ref, t1), (bu_ref, vu), (bd_ref, vd), (g2_ref, v2), (t2_ref, t2)):
        for layer in range(2):
            dst[layer] = src[layer : layer + 1, :].astype(f32)
    for layer in range(2):
        vq[layer, :, 0:768] = bq_ref[layer : layer + 1, 0:768].astype(f32)
        vq[layer, :, 768:1536] = jnp.zeros((1, 768), f32)
        vq[layer, :, 1536:2304] = bq_ref[layer : layer + 1, 768:1536].astype(f32)
    count = count_ref[0]
    keymask = jnp.where(lax.broadcasted_iota(jnp.int32, (1, 256), 1) < count, 0.0, -1e9)


    chip = (place["z"] * 4 + place["x"]) * 4 + place["y"]

    def gather_start(e):
        for r in range(6):
            every[e, core, chip, r : r + 1, :] = pool[e, :, 128 * r : 128 * r + 128]
        mine = every.at[e, core, chip]
        for_other_chips(place, lambda there: pltpu.make_async_remote_copy(
            src_ref=mine, dst_ref=mine, send_sem=every_s.at[e], recv_sem=every_r.at[e], device_id=there, device_id_type=MESH
        ).start())

    def swap_copy(e):
        mine = every.at[e, core]
        return pltpu.make_async_remote_copy(
            src_ref=mine, dst_ref=mine, send_sem=swap_s.at[e], recv_sem=swap_r.at[e],
            device_id=neighbour(place, "c", 1), device_id_type=MESH,
        )

    def gather_swap(e):
        others = every.at[e, core, pl.ds(0, 63)]
        pltpu.make_async_copy(others, others, every_r.at[e]).wait()
        swap_copy(e).start()

    def gather_end(e):
        others = every.at[e, core, pl.ds(0, 63)]
        pltpu.make_async_copy(others, others, every_s.at[e]).wait()
        swap_copy(e).wait()


    def norm(z, layer, normed_ref, scaled_ref, gain, shift, rows):
        center = z - jnp.mean(z, axis=1, keepdims=True)
        scaled = lax.rsqrt(jnp.mean(center * center, axis=1, keepdims=True) + eps_norm)
        normed = center * scaled
        normed_ref[rows, :] = normed
        scaled_ref[rows, :] = scaled
        return normed * gain[layer] + shift[layer]

    def forward_layer(layer, extra):
        is_first, is_last = layer == 0, layer == 1
        use_q, use_u, use_d = (2, layer, 0, extra), (1, layer, 1, extra), (0, layer, layer)

        @pl.when(is_last)
        def _():
            pl.semaphore_wait(barrier, 70)
            gather_start(0)

        def free(*names):
            @pl.when(is_last)
            def _():
                for name in names:
                    keep(name).wait()

        def store(*names):
            @pl.when(is_first)
            def _():
                for name in names:
                    keep(name).start()

        @pl.when(is_first)
        def _():
            load("xb").wait()
            grad[...] = xb[...].astype(f32)

        @pl.when(is_last)
        def _():
            xb[...] = grad[...].astype(bf16)

        free("qkv")
        blocks = weights(*use_q)
        for m in range(3):
            cols = pl.ds(768 * m, 768)
            blocks[m].wait()
            mixed = jnp.dot(xb[...], extra[0, cols, :], preferred_element_type=f32) + vq[layer, :, cols]
            qkv[:, cols] = mixed.astype(bf16)
        store("qkv")

        @pl.when(is_first)
        def _():
            fetch_weights(1, 0, 1, extra)
            fetch_weights(0, 0, 0)

        @pl.when(is_last)
        def _():
            perm_copy.start()

        free("ctx")

        def attend(pair, _):
            q, k, v = (qkv[:, lanes_of(pair + 6 * third, 128)] for third in range(3))
            probs = pair_probs(q, k, keymask).astype(bf16)
            both = jnp.dot(probs, v, preferred_element_type=f32)
            first = lax.broadcasted_iota(jnp.int32, (256, 128), 1) < 64
            ctx[:, lanes_of(pair, 128)] = jnp.where(first, both[:256], both[256:]).astype(bf16)
            return 0

        lax.fori_loop(0, 6, attend, 0, unroll=6)
        store("ctx")

        @pl.when(is_last)
        def _():
            gather_swap(0)

        blocks[3].wait()
        grad[...] += jnp.dot(ctx[...], extra[0, 2304:3072, :], preferred_element_type=f32) + vo[layer]

        @pl.when(is_first)
        def _():
            fetch_weights(2, 1, 0, extra)
            fetch_weights(0, 1, 1)

        free("n1", "r1", "n2", "r2")

        def norm_one(i, _):
            rows = rows_of(i, 64)
            mid = norm(grad[rows, :], layer, n1, r1, v1, t1, rows)
            n2[rows, :] = mid
            d_att[rows, :] = mid.astype(bf16)
            return 0

        lax.fori_loop(0, 4, norm_one, 0, unroll=4)
        store("n1", "r1")
        free("inner")
        blocks = weights(*use_u)
        for m in range(4):
            cols = pl.ds(768 * m, 768)
            blocks[m].wait()
            value = jnp.dot(d_att[...], extra[1, cols, :], preferred_element_type=f32) + vu[layer, :, cols]
            inner[:, cols] = value
            d_inner[:, cols] = gelu_parts(value)[0].astype(bf16)
        store("inner")

        @pl.when(is_first)
        def _():
            fetch_weights(1, 1, 1, extra)

        ready_weights(*use_d)
        n2[...] += jnp.dot(d_inner[...], weight[layer], preferred_element_type=f32) + vd[layer]

        @pl.when(is_first)
        def _():
            fetch_weights(1, 1, 0)

        def norm_two(i, total):
            rows = rows_of(i, 64)
            result = norm(n2[rows, :], layer, n2, r2, v2, t2, rows)
            grad[rows, :] = result
            spot = lax.broadcasted_iota(jnp.int32, (64, 1), 0) + i * 64
            return total + jnp.sum(jnp.where(spot < count, result, 0.0), axis=0, keepdims=True)

        total = lax.fori_loop(0, 4, norm_two, jnp.zeros((1, 768), f32), unroll=4)
        pool[layer] = total / count.astype(f32)
        store("n2", "r2")

        @pl.when(is_last)
        def _():
            gather_end(0)


    def pairing(e, loss):
        me = ((place["z"] * 4 + place["x"]) * 2 + core) * 4 + place["y"]
        row = lax.broadcasted_iota(jnp.int32, (128, 128), 0)
        col = lax.broadcasted_iota(jnp.int32, (128, 128), 1)
        rows = lax.broadcasted_iota(jnp.int32, (128, 1), 0)
        lane = lax.broadcasted_iota(jnp.int32, (1, 768), 1)
        companion = companion_ref[...]
        divisor = divisor_ref[0]
        partner = (row == companion).astype(f32)
        mine = jnp.sum(jnp.where(lax.broadcasted_iota(jnp.int32, (1, 128), 1) == me, companion, 0), axis=1, keepdims=True)
        chosen = (rows == mine).astype(f32)
        is_me = rows == me
        gathered = jnp.concatenate([every[e, c].reshape(16, 1, 4, 6, 128) for c in range(2)], axis=1).reshape(128, 6, 128)
        embed = jnp.concatenate(
            [gathered[:, r, :] for r in range(6)], axis=1
        )
        high = embed.astype(bf16)
        low = (embed - high.astype(f32)).astype(bf16)
        own = pool[e]
        total = jnp.zeros((1, 768), f32)
        keeps = [(lane < widths_ref[p]).astype(f32) for p in range(4)]
        high_all = jnp.concatenate([high * keep_p.astype(bf16) for keep_p in keeps], axis=0)
        low_all = jnp.concatenate([low * keep_p.astype(bf16) for keep_p in keeps], axis=0)
        grams = (
            lax.dot_general(high_all, high, NT, preferred_element_type=f32)
            + lax.dot_general(high_all, low, NT, preferred_element_type=f32)
            + lax.dot_general(low_all, high, NT, preferred_element_type=f32)
        )
        for p, keep_p in enumerate(keeps):
            gram = grams[128 * p : 128 * (p + 1)]
            diagonal = jnp.where(row == col, gram, 0.0)
            inverse = lax.rsqrt(jnp.sum(diagonal, axis=1, keepdims=True) + eps_norm)
            inverse_row = lax.rsqrt(jnp.sum(diagonal, axis=0, keepdims=True) + eps_norm)
            sims = gram * inverse * inverse_row / divisor
            sims = jnp.where(row == col, -1e30, sims)
            top = jnp.max(sims, axis=1, keepdims=True)
            lse = top + jnp.log(jnp.sum(jnp.exp(sims - top), axis=1, keepdims=True))
            loss = loss + (lse - jnp.sum(sims * partner, axis=1, keepdims=True))
            to_me = jnp.sum(jnp.where(col == me, sims, 0.0), axis=1, keepdims=True)
            lse_me = jnp.sum(jnp.where(is_me, lse, 0.0), axis=0, keepdims=True)
            weight_j = jnp.exp(to_me - lse_me) + jnp.exp(to_me - lse) - 2.0 * chosen
            dunit = jnp.sum(embed * (weight_j * inverse), axis=0, keepdims=True) * keep_p
            inverse_me = jnp.sum(jnp.where(is_me, inverse, 0.0), axis=0, keepdims=True)
            unit_me = own * keep_p * inverse_me
            inside = dunit - unit_me * jnp.sum(unit_me * dunit, axis=1, keepdims=True)
            total = total + inside * inverse_me
        d_emb[e] = total / (8.0 * divisor)
        return loss


    def norm_back(normed, scaled, gain, rounded, at_gain, at_shift, at_bias, layer):
        sums = [jnp.zeros((1, 768), f32) for _ in range(3)]
        for i in range(4):
            rows = pl.ds(64 * i, 64)
            dy, n = grad[rows, :], normed[rows, :]
            dn = dy * gain
            inside = dn - jnp.mean(dn, axis=1, keepdims=True) - n * jnp.mean(dn * n, axis=1, keepdims=True)
            dz = scaled[rows, :] * inside
            low = dz.astype(bf16)
            grad[rows, :] = dz
            rounded[rows, :] = low
            for k, term in enumerate((dy * n, dy, low.astype(f32))):
                sums[k] = sums[k] + jnp.sum(term, axis=0, keepdims=True)
        for at, total in zip((at_gain, at_shift, at_bias), sums):
            vectors[layer, :, at : at + 768] = total

    def turn_active():
        def turn(j, _):
            value = inner[:, lanes_of(j, 256)]
            act_t[lanes_of(j, 256), :] = gelu_parts(value)[0].T.astype(bf16)
            return 0

        lax.fori_loop(0, 12, turn, 0, unroll=2)

    def permute(operand, which):
        def one(o, _):
            apt[o, which] = lax.dot_general(perm[o], operand, NT, preferred_element_type=f32).astype(bf16)
            return 0

        lax.fori_loop(0, 3, one, 0, unroll=3)

    def begin_layer(layer):
        spots = lax.broadcasted_iota(jnp.int32, (256, 1), 0)
        pooled = jnp.where(spots < count, 1.0, 0.0) / count.astype(f32)

        @pl.when(layer == 1)
        def _():
            grad[...] = pooled * d_emb[1]

        @pl.when(layer == 0)
        def _():
            grad[...] += pooled * d_emb[0]
            load("n2").wait()
            load("r2").wait()
            load("inner").wait()
            turn_active()

        norm_back(n2, r2, v2[layer], d_outer, 3072, 3840, 2304, layer)

        @pl.when(layer == 1)
        def _():
            load("n2").start()
            load("r2").start()

    def through_expand(layer):
        slot = back_slot(0, layer)

        @pl.when(layer == 0)
        def _():
            ready_weights(0, 0, slot)

        def chunk(j, _):
            cols = lanes_of(j, 512)
            d_act = lax.dot_general(d_outer[...], weight[slot, cols, :], NT, preferred_element_type=f32)
            value = inner[:, cols]
            slope = gelu_parts(value)[1] + value * (jnp.exp(-0.5 * value * value) * 0.3989422804014327)
            low = (d_act * slope).astype(bf16)
            d_inner[:, cols] = low
            at = pl.ds(pl.multiple_of(6144 + j * 512, 512), 512)
            vectors[layer, :, at] = jnp.sum(low.astype(f32), axis=0, keepdims=True)
            return 0

        lax.fori_loop(0, 6, chunk, 0, unroll=2)
        fetch_weights(2, layer, slot)

        @pl.when(layer == 1)
        def _():
            load("inner").start()

        @pl.when(layer == 0)
        def _():
            load("n1").wait()
            load("r1").wait()
            permute((n1[...] * v1[0] + t1[0]).astype(bf16), 0)

    def through_mixer(layer):
        slot = back_slot(1, layer)

        @pl.when(layer == 0)
        def _():
            ready_weights(1, 0, slot)

        @pl.when(layer == 1)
        def _():
            ready_weights(1, 1, slot)

        for m in range(4):
            cols = pl.ds(768 * m, 768)
            grad[...] += lax.dot_general(d_inner[:, cols], weight[slot, cols, :], NT, preferred_element_type=f32)
        norm_back(n1, r1, v1[layer], d_att, 768, 1536, 0, layer)

        @pl.when(layer == 1)
        def _():
            fetch_weights(0, 0, slot)
            load("n1").start()
            load("r1").start()

        slot = back_slot(2, layer)
        ready_weights(2, layer, slot)
        d_ctx[...] = lax.dot_general(d_att[...], weight[slot, 2304:3072, :], NT, preferred_element_type=f32).astype(bf16)

    def through_attention(layer, first_pair, pairs):
        def pair_back(i, _):
            pair = first_pair + i
            at = [lanes_of(pair + 6 * third, 128) for third in range(3)]
            q, k, v = (qkv[:, cols] for cols in at)
            probs = pair_probs(q, k, keymask)
            dc = head_halves(d_ctx[:, at[0]])
            dp = lax.dot_general(dc, v, NT, preferred_element_type=f32)
            ds = (probs * (dp - jnp.sum(dp * probs, axis=1, keepdims=True))).astype(bf16)
            dq = jnp.dot(
                jnp.concatenate([ds[:256], ds[256:]], axis=1), head_halves(k * 0.125), preferred_element_type=f32
            ).astype(bf16)
            dk = lax.dot_general(ds, head_halves(q * 0.125), TN, preferred_element_type=f32).astype(bf16)
            dv = lax.dot_general(probs.astype(bf16), dc, TN, preferred_element_type=f32).astype(bf16)
            for cols, value in zip(at, (dq, dk, dv)):
                d_qkv[:, cols] = value
            for start, value in ((4608, dq), (5376, dv)):
                where = pl.ds(pl.multiple_of(start + pair * 128, 128), 128)
                vectors[layer, :, where] = jnp.sum(value.astype(f32), axis=0, keepdims=True)
            return 0

        lax.fori_loop(0, pairs, pair_back, 0, unroll=2)

    def through_projection(layer):
        slot = back_slot(2, layer)
        for m in range(3):
            cols = pl.ds(768 * m, 768)
            grad[...] += lax.dot_general(d_qkv[:, cols], weight[slot, cols, :], NT, preferred_element_type=f32)

        @pl.when(layer == 1)
        def _():
            fetch_weights(1, 0, slot)
            load("qkv").start()

        @pl.when(layer == 0)
        def _():
            dx_copy.start()

    dx_copy = pltpu.make_async_copy(grad, dx_ref.at[0], table_sem.at[2])
    emb_copy = pltpu.make_async_copy(pool, emb_hbm, table_sem.at[3])
    loss_copy = pltpu.make_async_copy(loss_row, loss_hbm, table_sem.at[4])
    out_copy = pltpu.make_async_copy(out_ref, out_hbm, table_sem.at[5])
    vec_copy = pltpu.make_async_copy(vec_out_ref, vec_hbm, table_sem.at[6])

    def store_rows(o, slot, mine, tile0, value):
        for j in range(value.shape[1] // 128):
            part = value[:, 128 * j : 128 * (j + 1)].reshape(16, 3, 8, 128)
            if mine:
                half[o, slot, :, tile0 + 3 * j : tile0 + 3 * j + 3] = part
            else:
                send[o, lax.rem(slot, 2), :, tile0 + 3 * j : tile0 + 3 * j + 3] = part

    def product(mine, slot, uses):
        c = core if mine else 1 - core

        def one(o, _):
            for which, ref, start, width, tile0 in uses:
                lhs = apt[o, which, pl.ds(pl.multiple_of(c * 384, 128), 384), :]
                for w in range(0, width, 256):
                    cols = pl.ds(pl.multiple_of(start(o) + w, 256), 256)
                    value = jnp.dot(lhs, ref[:, cols], preferred_element_type=f32)
                    store_rows(o, slot, mine, tile0 + 3 * (w // 128), value)
            return 0

        lax.fori_loop(0, 3, one, 0, unroll=3)

    def product_shrink(mine, slot, k):
        def block(z, _):
            c = core if mine else 1 - core
            lhs = jnp.concatenate(
                [act_t[pl.ds(pl.multiple_of(z * 768 + x * 192 + c * 96, 32), 96), :] for x in range(4)], axis=0
            )
            value = jnp.dot(lhs, d_outer[:, pl.ds(pl.multiple_of(384 * k, 128), 384)], preferred_element_type=f32)
            for x in range(4):
                for y in range(4):
                    for j in range(3):
                        p = {"x": x, "y": y, "z": z}
                        d1, d2, d3 = (p[axis] for axis in ORDERS[j])
                        row = x * 96 + (y * 3 + j) * 8
                        for ct in range(3):
                            tile = value[row : row + 8, 128 * ct : 128 * ct + 128]
                            if mine:
                                half[j, slot, d1 * 4 + d2, d3 * 3 + ct] = tile
                            else:
                                send[j, lax.rem(slot, 2), d1 * 4 + d2, d3 * 3 + ct] = tile
            return 0

        lax.fori_loop(0, 4, block, 0)

    def make(u):
        slot = lax.rem(u, 4)
        layer = 1 - u // 6
        kind = lax.rem(u, 6)

        def both_halves(job):
            job(False)
            for o in range(3):
                copy0(o, u).start()
            job(True)

        @pl.when(kind == 0)
        def _():
            begin_layer(layer)

        @pl.when(kind < 2)
        def _():
            both_halves(lambda mine: product_shrink(mine, slot, kind))

        @pl.when((kind == 2) | (kind == 3))
        def _():
            both_halves(lambda mine: product(mine, slot, [(0, d_inner, lambda o: (kind - 2) * 1536 + o * 512, 512, 0)]))

        @pl.when(kind == 4)
        def _():
            both_halves(lambda mine: product(mine, slot, [(0, d_qkv, lambda o: o * 768, 512, 0)]))

        @pl.when(kind == 5)
        def _():
            both_halves(lambda mine: product(
                mine, slot, [(0, d_qkv, lambda o: o * 768 + 512, 256, 0), (1, d_att, lambda o: o * 256, 256, 6)]
            ))

    def follow(u):
        layer = 1 - u // 6
        kind = lax.rem(u, 6)

        @pl.when(kind == 1)
        def _():
            through_expand(layer)

        @pl.when(kind == 2)
        def _():
            through_mixer(layer)

        @pl.when(kind == 3)
        def _():
            @pl.when(layer == 0)
            def _():
                load("xb").wait()
                load("ctx").wait()

            permute(xb[...], 0)
            permute(ctx[...], 1)

            @pl.when(layer == 1)
            def _():
                load("xb").start()
                load("ctx").start()

            @pl.when(layer == 0)
            def _():
                load("qkv").wait()

            through_attention(layer, 0, 4)

        @pl.when(kind == 4)
        def _():
            through_attention(layer, 4, 2)
            through_projection(layer)


    def exchange(o, k, slot, src_up, src_down, got):
        axis = ORDERS[o][k // 2]
        copies = [
            pltpu.make_async_remote_copy(
                src_ref=src, dst_ref=got.at[o, slot, way], send_sem=sems_s.at[o, k, slot], recv_sem=sems_r.at[o, k, slot],
                device_id=neighbour(place, axis, step), device_id_type=MESH,
            )
            for way, (src, step) in enumerate(((src_up, 1), (src_down, -1)))
        ]
        return copies, got.at[o, slot], sems_s.at[o, k, slot], sems_r.at[o, k, slot]

    def begin(exchanged):
        for copy in exchanged[0]:
            copy.start()

    def end(exchanged):
        _, landed, sent_sem, landed_sem = exchanged
        pltpu.make_async_copy(landed, landed, sent_sem).wait()
        pltpu.make_async_copy(landed, landed, landed_sem).wait()

    def spots(o, phase):
        a = place[ORDERS[o][phase]]
        return a, lax.rem(a + 1, 4), lax.rem(a + 2, 4), lax.rem(a + 3, 4)

    def copy0(o, u):
        slot, way = lax.rem(u, SLOTS), lax.rem(u, 2)
        return pltpu.make_async_remote_copy(
            src_ref=send.at[o, way], dst_ref=got0.at[o, slot], send_sem=sem0_s.at[o, way], recv_sem=sem0_r.at[o, slot],
            device_id=neighbour(place, "c", 1), device_id_type=MESH,
        )

    def step_a(o, phase, u):
        slot = lax.rem(u, SLOTS)
        a, up, far, down = spots(o, phase)
        if phase == 0:
            src, got = (half.at[o, lax.rem(u, 4), pl.ds(far * 4, 2)], half.at[o, lax.rem(u, 4), pl.ds(far * 4 + 2, 2)]), got1a
        elif phase == 1:
            src, got = (half2.at[o, slot, far, pl.ds(0, 6)], half2.at[o, slot, far, pl.ds(6, 6)]), got2a
        else:
            src, got = (half3.at[o, slot, far, pl.ds(0, 2)], half3.at[o, slot, far, pl.ds(2, 2)]), got3a
        return exchange(o, 2 * phase, slot, src[0], src[1], got)

    def step_b(o, phase, u):
        slot = lax.rem(u, SLOTS)
        a, up, far, down = spots(o, phase)
        if phase == 0:
            src, got = (half.at[o, lax.rem(u, 4), pl.ds(up * 4, 4)], half.at[o, lax.rem(u, 4), pl.ds(down * 4, 4)]), got1b
        elif phase == 1:
            src, got = (half2.at[o, slot, up], half2.at[o, slot, down]), got2b
        else:
            src, got = (half3.at[o, slot, up], half3.at[o, slot, down]), got3b
        return exchange(o, 2 * phase + 1, slot, src[0], src[1], got)

    def add_a(o, phase, u):
        slot = lax.rem(u, SLOTS)
        a, up, far, down = spots(o, phase)
        if phase == 0:
            for i in range(2):
                half[o, lax.rem(u, 4), up * 4 + i] += got1a[o, slot, 0, i]
                half[o, lax.rem(u, 4), down * 4 + 2 + i] += got1a[o, slot, 1, i]
        elif phase == 1:
            half2[o, slot, up, 0:6] += got2a[o, slot, 0]
            half2[o, slot, down, 6:12] += got2a[o, slot, 1]
        else:
            half3[o, slot, up, 0:2] += got3a[o, slot, 0]
            half3[o, slot, down, 2:4] += got3a[o, slot, 1]

    def add_b(o, phase, u):
        slot = lax.rem(u, SLOTS)
        a, up, far, down = spots(o, phase)
        if phase == 0:
            for i in range(4):
                half2[o, slot, i] = half[o, lax.rem(u, 4), a * 4 + i] + got1b[o, slot, 0, i] + got1b[o, slot, 1, i]
        elif phase == 1:
            to_third(o, slot, u, half2[o, slot, a] + got2b[o, slot, 0] + got2b[o, slot, 1])
        else:
            out_ref[u, o] = half3[o, slot, a] + got3b[o, slot, 0] + got3b[o, slot, 1]

    def to_third(o, slot, u, total):
        @pl.when(lax.rem(u, 6) < 2)
        def _():
            for k in range(4):
                half3[o, slot, k, 0:3] = total[3 * k : 3 * k + 3]

        @pl.when(lax.rem(u, 6) >= 2)
        def _():
            for ct in range(4):
                rows24[o, ct] = total[3 * ct : 3 * ct + 3].reshape(24, 128)
            for k in range(4):
                for ct in range(4):
                    half3[o, slot, k, ct, 0:6, :] = rows24[o, ct, 6 * k : 6 * k + 6, :]

    def direct(o, phase, u):
        slot, way = lax.rem(u, SLOTS), lax.rem(u, 2)
        a = place[ORDERS[o][phase]]
        src, got = ((half2, got2d), (half3, got3d))[phase - 1]
        copies = [
            pltpu.make_async_remote_copy(
                src_ref=src.at[o, slot, lax.rem(a + step, 4)], dst_ref=got.at[o, way, step - 1],
                send_sem=direct_s.at[o, phase - 1, way], recv_sem=direct_r.at[o, phase - 1, way],
                device_id=neighbour(place, ORDERS[o][phase], step), device_id_type=MESH,
            )
            for step in (1, 2, 3)
        ]
        return copies, got.at[o, way], direct_s.at[o, phase - 1, way], direct_r.at[o, phase - 1, way]

    def direct_second(u):
        slot, way = lax.rem(u, SLOTS), lax.rem(u, 2)
        for o in range(3):
            end(direct(o, 1, u))
            total = half2[o, slot, place[ORDERS[o][1]]]
            for i in range(3):
                total += got2d[o, way, i]
            to_third(o, slot, u, total)
            begin(direct(o, 2, u))

    def direct_third(u):
        slot, way = lax.rem(u, SLOTS), lax.rem(u, 2)
        for o in range(3):
            end(direct(o, 2, u))
            total = half3[o, slot, place[ORDERS[o][2]]]
            for i in range(3):
                total += got3d[o, way, i]
            out_ref[u, o] = total

    def spread_vectors(layer):
        total = jnp.zeros((128, 128), f32)
        for start, width, keep in VECTORS:
            d = lax.broadcasted_iota(jnp.int32, (128, width), 0) * keep
            q = lax.broadcasted_iota(jnp.int32, (128, width), 1)
            own = jnp.where((q >= d) & (q < d + keep), vectors[layer, :, start : start + width], 0.0)
            high = own.astype(bf16)
            low = (own - high.astype(f32)).astype(bf16)
            for part in range(width // 768):
                k = start // 768 + part
                lanes = weight[1, 768 * (k // 6) : 768 * (k // 6 + 1), 128 * (k % 6) : 128 * (k % 6 + 1)]
                at = slice(768 * part, 768 * (part + 1))
                total += jnp.dot(high[:, at], lanes, preferred_element_type=f32)
                total += jnp.dot(low[:, at], lanes, preferred_element_type=f32)
        total = total.reshape(4, 4, 8, 128)
        for z in range(4):
            for x in range(4):
                vec_src[z, x, layer] = total[z, x]

    def vector_copies(k, landed, pieces):
        copies = [
            pltpu.make_async_remote_copy(
                src_ref=src, dst_ref=landed.at[i], send_sem=vec_s.at[k], recv_sem=vec_r.at[k], device_id=device, device_id_type=MESH
            )
            for i, (src, device) in enumerate(pieces)
        ]
        return copies, landed, vec_s.at[k], vec_r.at[k]

    def copies_z():
        return vector_copies(0, vec_z, [(vec_src.at[lax.rem(place["z"] + i, 4)], neighbour(place, "z", i)) for i in (1, 2, 3)])

    def copies_x():
        mine = place["z"]
        return vector_copies(1, vec_x, [(vec_src.at[mine, lax.rem(place["x"] + i, 4)], neighbour(place, "x", i)) for i in (1, 2, 3)])

    def copies_group():
        return vector_copies(2, vec_cy, [(vec_mid, in_group(place, flip, step)) for flip, step in GROUP])

    def vectors_first():
        spread_copy.wait()
        spread_vectors(1)

    def vectors_start():
        spread_vectors(0)
        begin(copies_z())

    def vectors_second():
        end(copies_z())
        for x in range(4):
            vec_src[place["z"], x] += vec_z[0, x] + vec_z[1, x] + vec_z[2, x]
        begin(copies_x())

    def vectors_third():
        end(copies_x())
        vec_mid[...] = vec_src[place["z"], place["x"]] + vec_x[0] + vec_x[1] + vec_x[2]
        begin(copies_group())

    def vectors_last():
        end(copies_group())
        total = vec_mid[...]
        for i in range(7):
            total += vec_cy[i]
        mine = lax.broadcasted_iota(jnp.int32, (2, 8, 128), 1) == core * 4 + place["y"]
        vec_out_ref[...] = jnp.sum(jnp.where(mine, total, 0.0), axis=1)

    def when(u, first, last, job):
        @pl.when((u >= first) & (u < last))
        def _():
            job(u)

    def enter(u):
        slot = lax.rem(u, SLOTS)
        for o in range(3):
            copy0(o, u).wait()

            def add(i, _):
                half[o, lax.rem(u, 4), i] += got0[o, slot, i]
                return 0

            lax.fori_loop(0, 16, add, 0)
            begin(step_a(o, 0, u))

    def second(phase):
        def job(u):
            for o in range(3):
                end(step_a(o, phase, u))
                add_a(o, phase, u)
                begin(step_b(o, phase, u))
        return job

    def third(phase):
        def job(u):
            for o in range(3):
                end(step_b(o, phase, u))
                add_b(o, phase, u)
                if phase == 0:
                    @pl.when(u < DIRECT)
                    def _():
                        begin(step_a(o, 1, u))

                    @pl.when(u >= DIRECT)
                    def _():
                        begin(direct(o, 1, u))
                elif phase == 1:
                    begin(step_a(o, 2, u))
        return job

    def tick(u, _):
        def make_one(v, _):
            make(v)
            return 0

        lax.fori_loop(jnp.where(u == 0, 0, jnp.maximum(u, 2)), jnp.where(u == 0, 2, jnp.minimum(u + 1, TRIPLES)), make_one, 0)
        when(u - 3, 0, TRIPLES, third(0))
        when(u - 4, 0, DIRECT, second(1))
        when(u - 5, 0, DIRECT, third(1))
        when(u - 6, 0, DIRECT, second(2))
        when(u - 7, 0, DIRECT, third(2))
        when(u - 4, DIRECT, TRIPLES, direct_second)
        when(u - 5, DIRECT, TRIPLES, direct_third)
        when(u, 0, TRIPLES, enter)
        when(u - 1, 0, TRIPLES, second(0))
        when(u, 0, TRIPLES, follow)

        for k, job in ((8, spread_copy.start), (9, vectors_first), (11, vectors_start), (12, vectors_second), (13, vectors_third), (14, vectors_last)):
            pl.when(u == k)(job)
        return 0


    def forward_both(extra):
        fetch_weights(2, 0, 0, extra)

        def layer_step(layer, _):
            forward_layer(layer, extra)
            return 0

        lax.fori_loop(0, 2, layer_step, 0)
        gather_start(1)

    pl.run_scoped(forward_both, pltpu.VMEM((2, 3072, 768), bf16))
    emb_copy.start()
    half3[...] = jnp.zeros_like(half3)

    def layer_loss(e, loss):
        @pl.when(e == 1)
        def _():
            turn_active()
            gather_swap(1)
            perm_copy.wait()
            permute(d_att[...], 0)
            gather_end(1)

        return pairing(e, loss)

    loss_row[...] = lax.fori_loop(0, 2, layer_loss, jnp.zeros((128, 1), f32)) / 8.0
    loss_copy.start()

    def reduce_all(half_ref, send_ref):
        nonlocal half, send
        half, send = half_ref, send_ref
        lax.fori_loop(0, DIRECT + 7, tick, 0)

    pl.run_scoped(reduce_all, pltpu.VMEM((3, 4, 16, 12, 8, 128), f32), pltpu.VMEM((3, 2, 16, 12, 8, 128), f32))
    out_copy.start()
    vec_copy.start()
    for copy in (dx_copy, emb_copy, loss_copy, out_copy, vec_copy):
        copy.wait()


def permutations():
    rows = np.arange(768).reshape(4, 4, 2, 4, 6)
    names = {"z": 0, "x": 1, "c": 2, "y": 3}
    out = np.zeros((3, 768, 768), np.float32)
    for o, (d1, d2, d3) in enumerate(ORDERS):
        taken = rows.transpose(2, names[d1], names[d2], names[d3], 4).reshape(-1)
        out[o, np.arange(768), taken] = 1
    return out.astype(ml_dtypes.bfloat16)


def lane_places():
    out = np.zeros((9216, 128), np.float32)
    lane = 0
    for start, width, keep in VECTORS:
        q = np.arange(width)
        out[start + q, lane + q % keep] = 1
        lane += keep
    out = out.reshape(2, 6, 768, 128).transpose(0, 2, 1, 3).reshape(1536, 768)
    return out.astype(ml_dtypes.bfloat16)


def finish_kernel(out_hbm, vec_hbm, loss_hbm, emb_hbm, dx_hbm, *refs):
    loss_out, emb_out, dx_out, qkv_out, qv_out, mixer_out, bias_out, gain_out, shift_out, up_out, ffn_out, down_out, downbias_out, fingain_out, finshift_out = refs[:15]
    out_ref, vec_ref, loss_ref, emb_ref, dx_ref, sem = refs[15:]
    copies = [
        pltpu.make_async_copy(src, dst, sem.at[k])
        for k, (src, dst) in enumerate(((out_hbm, out_ref), (vec_hbm, vec_ref), (loss_hbm, loss_ref), (emb_hbm, emb_ref), (dx_hbm, dx_ref)))
    ]
    for copy in copies:
        copy.start()
    for copy in copies[:4]:
        copy.wait()
    for layer in range(2):
        emb_out[0, layer : layer + 1, :] = emb_ref[layer]
    copies[4].wait()
    last = pltpu.make_async_copy(dx_ref, dx_out, sem.at[4])
    last.start()
    for layer in range(2):
        first = 6 * (1 - layer)
        for k in range(2):
            for o in range(3):
                for ct in range(3):
                    down_out[layer, 8 * o : 8 * o + 8, 384 * k + 128 * ct : 384 * k + 128 * ct + 128] = out_ref[first + k, o, ct]
                for ct in range(4):
                    at = (k * 3 + o) * 512 + 128 * ct
                    up_out[:, layer, at : at + 128] = out_ref[first + 2 + k, o, ct, 0:6, :]
        for o in range(3):
            for ct in range(4):
                at = o * 768 + 128 * ct
                qkv_out[:, layer, at : at + 128] = out_ref[first + 4, o, ct, 0:6, :]
            for ct in range(2):
                at = o * 768 + 512 + 128 * ct
                qkv_out[:, layer, at : at + 128] = out_ref[first + 5, o, ct, 0:6, :]
                at = o * 256 + 128 * ct
                mixer_out[:, layer, at : at + 128] = out_ref[first + 5, o, 2 + ct, 0:6, :]
    lane = 0
    for (_, _, keep), dst in zip(
        VECTORS, (bias_out, gain_out, shift_out, downbias_out, fingain_out, finshift_out, qv_out, ffn_out)
    ):
        dst[...] = vec_ref[:, lane : lane + keep]
        lane += keep
    rows = lax.broadcasted_iota(jnp.int32, (128, 1), 0)
    for k in range(4):
        loss_out[k] = jnp.sum(jnp.where(rows == lax.axis_index("batch") * 4 + k, loss_ref[...], 0.0))
    last.wait()


def body(slots, counts, companion, widths, divisor, triple, bias_qv, mixer, bias_mixer, gain_one, shift_one, expand, bias_expand, shrink, bias_shrink, gain_two, shift_two):
    tile = (8, 128)
    vmem = pl.BlockSpec(memory_space=pltpu.VMEM)
    smem = pl.BlockSpec(memory_space=pltpu.SMEM)
    hbm = pl.BlockSpec(memory_space=pl.ANY)

    def vm(*shape, dtype=f32):
        return pltpu.VMEM(shape, dtype)

    dma = pltpu.SemaphoreType.DMA
    saved = [((256, 2304), bf16), ((256, 768), bf16), ((256, 768), f32), ((256, 1), f32), ((256, 3072), f32), ((256, 768), f32), ((256, 1), f32)]
    shapes = [((TRIPLES, 3, 4) + tile, f32), ((2, 128), f32), ((128, 1), f32), ((2, 1, 768), f32), ((1, 256, 768), f32)] + saved
    results = pl.pallas_call(
        whole_kernel,
        out_shape=[jax.ShapeDtypeStruct(s, t) for s, t in shapes],
        in_specs=[smem, vmem, smem, smem] + [vmem] * 8 + [hbm] * 7,
        out_specs=[hbm] * 12,
        scratch_shapes=[
            vm(2, 3072, 768, dtype=bf16), vm(3, 768, 768, dtype=bf16), vm(256, 768, dtype=bf16), vm(256, 2304, dtype=bf16),
            vm(256, 768, dtype=bf16), vm(256, 768), vm(256, 1), vm(256, 3072), vm(256, 768), vm(256, 1), vm(256, 768),
            vm(256, 768, dtype=bf16), vm(256, 768, dtype=bf16), vm(256, 768, dtype=bf16), vm(3072, 256, dtype=bf16),
            vm(256, 3072, dtype=bf16), vm(256, 2304, dtype=bf16), vm(2, 1, 9216), vm(3, 2, 768, 256, dtype=bf16),
            vm(2, 1, 2304), vm(2, 1, 768), vm(2, 1, 768), vm(2, 1, 768), vm(2, 1, 3072), vm(2, 1, 768), vm(2, 1, 768), vm(2, 1, 768),
            vm(2, 1, 768), vm(2, 1, 768), vm(2, 2, 64, 6, 128), vm(TRIPLES, 3, 4, *tile), vm(2, 128), vm(128, 1),
            vm(3, SLOTS, 16, 12, *tile),
            vm(3, SLOTS, 2, 2, 12, *tile), vm(3, SLOTS, 2, 4, 12, *tile),
            vm(3, SLOTS, 4, 12, *tile), vm(3, SLOTS, 2, 6, *tile), vm(3, SLOTS, 2, 12, *tile),
            vm(3, SLOTS, 4, 4, *tile), vm(3, SLOTS, 2, 2, *tile), vm(3, SLOTS, 2, 4, *tile), vm(3, 4, 24, 128),
            vm(3, 2, 3, 12, *tile), vm(3, 2, 3, 4, *tile),
            vm(4, 4, 2, *tile), vm(3, 4, 2, *tile), vm(3, 2, *tile), vm(2, *tile), vm(7, 2, *tile),
            dma((4, 4)), dma((7,)), dma((8,)), dma((7,)), dma((2,)), dma((2,)), dma((2,)), dma((2,)),
            dma((3, 6, SLOTS)), dma((3, 6, SLOTS)), dma((3, 2)), dma((3, SLOTS)), dma((3, 2, 2)), dma((3, 2, 2)),
            dma((3,)), dma((3,)),
        ],
        compiler_params=pltpu.CompilerParams(
            collective_id=1, has_side_effects=True, vmem_limit_bytes=63 * 1024 * 1024
        ),
    )(
        counts, companion[None], widths, divisor,
        bias_qv, bias_mixer, gain_one, shift_one, bias_expand, bias_shrink, gain_two, shift_two,
        slots, triple, mixer, expand, shrink, jnp.asarray(permutations()), jnp.asarray(lane_places()),
    )
    out, vec_out, loss, embeddings, dx = results[:5]
    shapes = [(4,), (1, 2, 768), (1, 256, 768), (6, 2, 2304), (2, 12), (6, 2, 768), (2, 6), (2, 6), (2, 6), (6, 2, 3072), (2, 24), (2, 24, 768), (2, 6), (2, 6), (2, 6)]
    loss, embeddings, *rest = pl.pallas_call(
        finish_kernel,
        out_shape=[jax.ShapeDtypeStruct(s, f32) for s in shapes],
        in_specs=[hbm] * 5,
        out_specs=[smem, vmem, hbm] + [vmem] * 12,
        scratch_shapes=[vm(TRIPLES, 3, 4, *tile), vm(2, 128), vm(128, 1), vm(2, 1, 768), vm(1, 256, 768), dma((5,))],
        compiler_params=pltpu.CompilerParams(vmem_limit_bytes=63 * 1024 * 1024),
    )(out, vec_out, loss, embeddings, dx)
    rest = [r.transpose(1, 0, 2) if r.shape[:2] == (6, 2) else r for r in rest]
    return (loss, embeddings, *rest)


def solution(mesh):
    return jax.shard_map(
        body,
        mesh=mesh,
        in_specs=(
            P(("batch", "tile"), None, None),
            P(("batch", "tile")),
            P(),
            P(),
            P(),
            P(),
            P(),
            P(),
            P(),
            P(),
            P(),
            P(),
            P(),
            P(),
            P(),
            P(),
            P(),
        ),
        out_specs=(
            P("batch"),
            P(("batch", "tile"), None, None),
            P(("batch", "tile"), None, None),
            P(None, ("batch", "tile"), None),
            P(None, ("batch", "tile")),
            P(None, ("batch", "tile"), None),
            P(None, ("batch", "tile")),
            P(None, ("batch", "tile")),
            P(None, ("batch", "tile")),
            P(None, ("batch", "tile"), None),
            P(None, ("batch", "tile")),
            P(None, ("batch", "tile"), None),
            P(None, ("batch", "tile")),
            P(None, ("batch", "tile")),
            P(None, ("batch", "tile")),
        ),
        check_vma=False,
    )
```
